32 devices in a mesh: gx: 8 (over y, x, core), gy: 4 (over z).
Axes of the slice: x: 2, y: 2, z: 4, core: 2. Of those that a mesh axis runs over, the one named last changes fastest.
Arguments:
- spectrum: bfloat16 [32, 512, 1152], P('gx', 'gy'), may hold values from 0.099609375 to 2
- ocean_state: float32 [3, 16, 32, 512], P(None, None, 'gx', 'gy'), may hold values from -3 to 3
- sea_mask: int32 [32, 512], P('gx', 'gy'), may hold values from 0 to 1, as said below
Outputs:
- new_spectrum: bfloat16 [32, 512, 1152], P('gx', 'gy')
- new_ocean: float32 [3, 16, 32, 512], P(None, None, 'gx', 'gy')
The draws below stay inside these ranges and needn't reach their ends.
Inputs may be any that keep to these rules, and one draw needn't show every extreme that they name: `sea_mask`: 1 marks a sea cell, 0 a land cell.
All inputs are finite; a program needn't handle non-finite values.
Results may differ from the reference program's by a relative error of at most 0.0043.
Values may be sent and summed in bfloat16 or wider, within the bound.
No kernel may reach another device: no remote copies, remote signals or barrier semaphores. Data moves between devices by JAX's collectives and lax.ppermute only.
A program may use at most 64 MiB of HBM per device.

```python
import math
import jax
import jax.numpy as jnp
from jax import lax

NF = 32
NDIR = 36
NZ = 16
STEPS = 2
NX = 32
NY = 512


def draw_sea_mask(key, part):
    key_start, key_walk, key_isle = jax.random.split(key, 3)
    coast_start = jax.random.randint(key_start, (), NX // 8, NX // 3 + 1)
    stride = jax.random.randint(key_walk, (NY,), -2, 3)
    coastline = jnp.clip(coast_start + jnp.cumsum(stride), 0, NX // 2)
    land_cells = jnp.arange(NX)[:, None] < coastline[None, :]
    island = jax.random.randint(key_isle, (NX, NY), 0, 16) == 0
    return jnp.where(land_cells | island, 0, 1).astype(jnp.int32)


def steps_of(own_key, shape, shards, smallest, top_value):
    gain = 1.0
    for dim, shards_of in shards:
        draws = jax.random.uniform(jax.random.fold_in(jax.random.fold_in(own_key, 6), dim), (shards_of,), jnp.float32, smallest / len(shards), top_value / len(shards))
        gain = gain * jnp.repeat(jnp.exp(draws), shape[dim] // shards_of).reshape((-1,) + (1,) * (len(shape) - 1 - dim))
    return gain


def noise(rng, dims, spread, most, pieces=(), kind=jnp.bfloat16):
    gain = steps_of(rng, dims, pieces, -0.22, 0.18) if pieces else 1.0
    values = jax.random.normal(rng, dims, jnp.float32) * spread * gain
    return jnp.minimum(jnp.maximum(values, -most), most).astype(kind)


def setup_inputs(seed: int = 0) -> dict:
    splits = jax.random.split(jax.random.key(seed), 4)
    return {
        "spectrum": jnp.clip(jnp.exp(math.log(2.0) - 2.9996462 * jax.random.uniform(splits[0], (NX, NY, NF * NDIR), jnp.float32) ** steps_of(splits[0], (NX, NY, NF * NDIR), ((0, 8), (1, 4)), -0.2, 0.2)), 0.099609375, 2.0).astype(jnp.bfloat16),
        "ocean_state": noise(splits[1], (3, NZ, NX, NY), 0.5, 3.0, ((2, 8), (3, 4)), jnp.float32),
        "sea_mask": draw_sea_mask(jax.random.fold_in(splits[3], 71), 0),
    }


COURANT = 0.4
RATIO = 0.93
TURN = 0.1
STRESS = 0.1
CORIOLIS = 0.2
PRESS = 0.1
VISC = 0.15
ADVECT = 0.5
DIFFUSE = 0.15


def spectral_tables(n_freq, n_dir):
    speeds = COURANT * RATIO ** jnp.arange(n_freq, dtype=jnp.float32)
    angles = -0.5 * math.pi + (jnp.arange(n_dir, dtype=jnp.float32) + 0.5) * (2.0 * math.pi / n_dir)
    return speeds, jnp.cos(angles), jnp.sin(angles)


def beam_warming(courant, center, near_cell, far_cell):
    return -0.5 * courant * (3.0 * center - 4.0 * near_cell + far_cell) + 0.5 * courant * courant * (center - 2.0 * near_cell + far_cell)


def turning_rate(cosines, sines, zonal_xgrad, zonal_ygrad, north_xgrad, north_ygrad):
    return TURN * (cosines * sines * (zonal_xgrad - north_ygrad) + sines * sines * north_xgrad - cosines * cosines * zonal_ygrad)


def refraction(center, turn_rate):
    previous = jnp.roll(center, 1, axis=-3)
    following = jnp.roll(center, -1, axis=-3)
    return -(jnp.maximum(turn_rate, 0.0) * (center - previous) + jnp.minimum(turn_rate, 0.0) * (following - center))


def stencil_terms(padded):
    middle = padded[..., 1:-1, 1:-1]
    grad_x = (padded[..., 2:, 1:-1] - padded[..., :-2, 1:-1]) * 0.5
    grad_y = (padded[..., 1:-1, 2:] - padded[..., 1:-1, :-2]) * 0.5
    laplace = padded[..., 2:, 1:-1] + padded[..., :-2, 1:-1] + padded[..., 1:-1, 2:] + padded[..., 1:-1, :-2] - 4.0 * middle
    return middle, grad_x, grad_y, laplace


def ocean_step(padded, stress, wet_cells):
    zonal, zonal_xgrad, zonal_ygrad, zonal_spread = stencil_terms(padded[0])
    north, north_xgrad, north_ygrad, north_spread = stencil_terms(padded[1])
    heat, heat_xgrad, heat_ygrad, heat_spread = stencil_terms(padded[2])
    push_x = PRESS * jnp.cumsum(heat_xgrad, axis=0)
    push_y = PRESS * jnp.cumsum(heat_ygrad, axis=0)
    surface = (jnp.arange(zonal.shape[0]) == 0).astype(jnp.float32)[:, None, None]
    zonal_next = wet_cells * (zonal + CORIOLIS * north - push_x + VISC * zonal_spread + surface * stress[0])
    north_next = wet_cells * (north - CORIOLIS * zonal - push_y + VISC * north_spread + surface * stress[1])
    heat_next = heat + wet_cells * (-ADVECT * (zonal * heat_xgrad + north * heat_ygrad) + DIFFUSE * heat_spread)
    return jnp.stack([zonal_next, north_next, heat_next])


def wave_slab(slab, celerity, cosines, sines, shear, wet_cells):
    n_dir = slab.shape[0]
    half_dirs = n_dir // 2
    quarter = n_dir // 4
    padded = jnp.pad(slab.astype(jnp.float32), ((0, 0), (2, 2), (2, 2)))
    center = padded[:, 2:-2, 2:-2]
    direction = jnp.arange(n_dir)[:, None, None]
    east_side = direction >= half_dirs
    north_side = (direction < quarter) | (direction >= 3 * quarter)
    near_x = jnp.where(east_side, padded[:, 3:-1, 2:-2], padded[:, 1:-3, 2:-2])
    far_x = jnp.where(east_side, padded[:, 4:, 2:-2], padded[:, :-4, 2:-2])
    near_y = jnp.where(north_side, padded[:, 2:-2, 3:-1], padded[:, 2:-2, 1:-3])
    far_y = jnp.where(north_side, padded[:, 2:-2, 4:], padded[:, 2:-2, :-4])
    courant_x = celerity * jnp.abs(cosines)[:, None, None]
    courant_y = celerity * jnp.abs(sines)[:, None, None]
    turn_rate = turning_rate(cosines[:, None, None], sines[:, None, None], shear[0], shear[1], shear[2], shear[3])
    updated = wet_cells * (center + beam_warming(courant_x, center, near_x, far_x) + beam_warming(courant_y, center, near_y, far_y) + refraction(center, turn_rate))
    return updated.astype(jnp.bfloat16)


def reference(spectrum, ocean_state, sea_mask):
    wet_cells = sea_mask.astype(jnp.float32)
    masked = spectrum * sea_mask.astype(jnp.bfloat16)[:, :, None]
    spectrum_now = masked.reshape(NX, NY, NF, NDIR).transpose(2, 3, 0, 1)
    ocean_now = ocean_state
    speeds, cosines, sines = spectral_tables(NF, NDIR)
    weights = (STRESS * speeds[:, None, None] * jnp.stack([cosines, sines])[None, :, :]).astype(jnp.bfloat16)
    for step_index in range(STEPS):
        padded = jnp.pad(ocean_now, ((0, 0), (0, 0), (1, 1), (1, 1)))
        _, zonal_xgrad, zonal_ygrad, _ = stencil_terms(padded[0, 0])
        _, north_xgrad, north_ygrad, _ = stencil_terms(padded[1, 0])
        shear = (zonal_xgrad, zonal_ygrad, north_xgrad, north_ygrad)

        def one_freq(stress, slice_data):
            slab, celerity, weight_row = slice_data
            stress = stress + jnp.dot(weight_row, slab.reshape(NDIR, -1), preferred_element_type=jnp.float32).reshape(stress.shape)
            return stress, wave_slab(slab, celerity, cosines, sines, shear, wet_cells)

        stress, spectrum_now = lax.scan(one_freq, jnp.zeros((2, NX, NY), jnp.float32), (spectrum_now, speeds, weights))
        ocean_now = ocean_step(padded, stress, wet_cells)
    final = spectrum_now.transpose(2, 3, 0, 1).reshape(NX, NY, NF * NDIR)
    return final, ocean_now
```

```python
import math

import jax
import jax.numpy as jnp
import numpy as np
from jax import lax
from jax.experimental import pallas as pl
from jax.experimental.pallas import tpu as pltpu
from jax.sharding import PartitionSpec as P

NF = 32
NDIR = 36
NZ = 16
HALF = NDIR // 2
QUARTER = NDIR // 4
ROWS = 4
LANES = 128
BINS = NF * NDIR

COURANT = 0.4
RATIO = 0.93
TURN = 0.1
STRESS = 0.1
CORIOLIS = 0.2
PRESS = 0.1
VISC = 0.15
ADVECT = 0.5
DIFFUSE = 0.15

F32 = jnp.float32
BF16 = jnp.bfloat16
VM = pl.BlockSpec(memory_space=pltpu.VMEM)
PARAMS = pltpu.CompilerParams(vmem_limit_bytes=48 * 1024 * 1024)

SPECTRA = 2 * HALF * NF
OCEAN = 3 * NZ
XROWS = SPECTRA + 2 * OCEAN
YROWS = HALF * 8 + 16

ANGLES = -0.5 * math.pi + (np.arange(NDIR, dtype=np.float32) + np.float32(0.5)) * np.float32(
    2.0 * math.pi / NDIR
)
COS = np.cos(ANGLES).astype(np.float32)
SIN = np.sin(ANGLES).astype(np.float32)
SPEEDS = (COURANT * RATIO ** np.arange(NF, dtype=np.float64)).astype(np.float32)


def stress_table():
    table = np.zeros((ROWS, 16, NDIR, NF), np.float32)
    for c, part in enumerate((COS, SIN)):
        weights = np.float32(STRESS) * SPEEDS[None, :] * part[:, None]
        for x in range(ROWS):
            table[x, c * 8 + 1 + x] = weights
    return table.reshape(ROWS, 16, BINS)


def is_even(axis):
    return lax.rem(lax.axis_index(axis), 2) == 0


def split(v):
    high = v.astype(BF16).astype(F32)
    return high, v - high


def roll(v, shift, axis):
    return pltpu.roll(v, shift % v.shape[axis], axis)


def lane_of(shape):
    return lax.broadcasted_iota(jnp.int32, shape, len(shape) - 1)


def pack_y_edges(cells, k, south, out_ref, lanes):
    start = LANES - 2 if south else 0
    packed = jnp.zeros((8, LANES), F32)
    for x in range(ROWS):
        for g in range(4):
            at = 8 * g + 2 * x
            moved = roll(cells[x][8 * g : 8 * g + 8], at - start, 1)
            packed = jnp.where((lanes >= at) & (lanes < at + 2), moved, packed)
    out_ref[k] = packed


def pack_ocean_columns(blocks, lanes):
    first = jnp.zeros((8, LANES), F32)
    last = jnp.zeros((8, LANES), F32)
    for c in range(3):
        for z in range(NZ):
            block = blocks[c][8 * z : 8 * z + 8]
            at = c * NZ + z
            first = jnp.where(lanes == at, roll(block, at, 1), first)
            last = jnp.where(lanes == at, roll(block, at - (LANES - 1), 1), last)
    return first, last


def send_x(n_ref, ocean_rows, mine_ref, low_side):
    row = jnp.where(low_side, 0, 2)
    first = jnp.where(low_side, HALF, 0)
    edge = n_ref[pl.ds(row, 2), pl.ds(first, HALF)]
    mine_ref[0:SPECTRA, :] = edge.reshape(SPECTRA, LANES).astype(BF16)
    low, high = ocean_rows
    whole, rest = split(jnp.where(low_side, low, high))
    mine_ref[SPECTRA : SPECTRA + OCEAN, :] = whole.astype(BF16)
    mine_ref[SPECTRA + OCEAN : XROWS, :] = rest.astype(BF16)


def send_y(edges_ref, first, last, even, outs):
    for slot, out_ref in enumerate(outs):
        takes_last = even if slot == 0 else jnp.logical_not(even)
        which = takes_last.astype(jnp.int32)
        out_ref[0 : HALF * 8, :] = edges_ref[which].reshape(HALF * 8, LANES).astype(BF16)
        whole, rest = split(jnp.where(takes_last, last, first))
        out_ref[HALF * 8 : YROWS, :] = jnp.concatenate([whole, rest], 0).astype(BF16)


def start_kernel(s_ref, o_ref, mask_ref, n_ref, xe_ref, xo_ref, ye_ref, yo_ref, t_ref, e_ref):
    lanes = lane_of((8, LANES))
    wet = mask_ref[...].astype(F32)
    for x in range(ROWS):
        t_ref[x] = jnp.transpose(s_ref[x].astype(F32))

    def pack(south, shift):
        def body(k, carry):
            cells = []
            for x in range(ROWS):
                cell = t_ref[x, pl.ds(k, NF, stride=NDIR), :] * wet[x : x + 1]
                n_ref[x, k] = cell
                cells.append(cell)
            pack_y_edges(cells, k - shift, south, e_ref.at[1 if south else 0], lanes)
            return carry

        return body

    lax.fori_loop(0, QUARTER, pack(False, 0), 0)
    lax.fori_loop(QUARTER, 3 * QUARTER, pack(True, QUARTER), 0)
    lax.fori_loop(3 * QUARTER, NDIR, pack(False, HALF), 0)
    even_x, even_y = is_even("gx"), is_even("gy")
    rows = tuple(o_ref[:, :, r, :].reshape(OCEAN, LANES) for r in (0, ROWS - 1))
    send_x(n_ref, rows, xe_ref, jnp.logical_not(even_x))
    send_x(n_ref, rows, xo_ref, even_x)
    pad = jnp.zeros((1, LANES), F32)
    blocks = [
        jnp.concatenate(
            [part for z in range(NZ) for part in (pad, o_ref[c, z], pad, pad, pad)], 0
        )
        for c in range(3)
    ]
    first, last = pack_ocean_columns(blocks, lanes)
    send_y(e_ref, first, last, even_y, (ye_ref, yo_ref))


def tables_kernel(speed_ref, tab_ref):
    speed = speed_ref[...]
    for k in range(NDIR):
        cx, cy = speed * abs(float(COS[k])), speed * abs(float(SIN[k]))
        near_x, far_x = cx * (2.0 - cx), (0.5 * cx) * (cx - 1.0)
        near_y, far_y = cy * (2.0 - cy), (0.5 * cy) * (cy - 1.0)
        tab_ref[0, k] = 1.0 - ((near_x + far_x) + (near_y + far_y))
        tab_ref[1, k] = near_x
        tab_ref[2, k] = far_x
        tab_ref[3, k] = near_y
        tab_ref[4, k] = far_y


def land_halos(even_x, even_y, xe_ref, xo_ref, ye_ref, yo_ref, xh_ref, yh_ref):
    side = even_x.astype(jnp.int32)
    shape = (2, HALF, NF, LANES)
    xh_ref[side] = xe_ref[0:SPECTRA, :].astype(F32).reshape(shape)
    xh_ref[1 - side] = xo_ref[0:SPECTRA, :].astype(F32).reshape(shape)

    def rows(ref):
        return ref[SPECTRA : SPECTRA + OCEAN, :].astype(F32) + ref[SPECTRA + OCEAN : XROWS, :].astype(F32)

    a, b = rows(xe_ref), rows(xo_ref)
    left, right = jnp.where(even_x, b, a), jnp.where(even_x, a, b)
    side = 1 - even_y.astype(jnp.int32)
    shape = (HALF, 8, LANES)
    yh_ref[side] = ye_ref[0 : HALF * 8, :].astype(F32).reshape(shape)
    yh_ref[1 - side] = yo_ref[0 : HALF * 8, :].astype(F32).reshape(shape)

    def columns(ref):
        both = ref[HALF * 8 : YROWS, :].astype(F32)
        return both[0:8] + both[8:16]

    a, b = columns(ye_ref), columns(yo_ref)
    above, below = jnp.where(even_y, a, b), jnp.where(even_y, b, a)
    return left, right, below, above


def extend_ocean(o_ref, left, right, ext_ref):
    for c in range(3):
        for z in range(NZ):
            at = c * NZ + z
            ext_ref[c, 8 * z : 8 * z + 1, :] = left[at : at + 1]
            ext_ref[c, 8 * z + 1 : 8 * z + 5, :] = o_ref[c, z]
            ext_ref[c, 8 * z + 5 : 8 * z + 6, :] = right[at : at + 1]
            ext_ref[c, 8 * z + 6 : 8 * z + 8, :] = jnp.zeros((2, LANES), F32)


def neighbours(c, q, below, above, levels):
    lanes = lane_of(q.shape)
    low = jnp.concatenate([roll(below, -(c * NZ + z), 1) for z in range(levels)], 0)
    high = jnp.concatenate([roll(above, LANES - 1 - (c * NZ + z), 1) for z in range(levels)], 0)
    return (
        roll(q, 1, 0),
        roll(q, -1, 0),
        jnp.where(lanes == 0, low, roll(q, 1, 1)),
        jnp.where(lanes == LANES - 1, high, roll(q, -1, 1)),
    )


def refraction_rates(ext_ref, below, above, rate_ref):
    grads = []
    for c in range(2):
        xm, xp, ym, yp = neighbours(c, ext_ref[c, 0:8, :], below, above, 1)
        grads.append(((xp - xm) * 0.5, (yp - ym) * 0.5))
    (ux, uy), (vx, vy) = grads
    stretch = ux - vy
    for k in range(NDIR):
        c, s = float(COS[k]), float(SIN[k])
        rate_ref[k] = (TURN * c * s) * stretch + (TURN * s * s) * vx - (TURN * c * c) * uy


def advance_ocean(ext_ref, below, above, stress, wet8, out_ref):
    zonal, north, heat = (ext_ref[c] for c in range(3))
    wet = jnp.concatenate([wet8] * NZ, 0)

    def stencil(c, q):
        xm, xp, ym, yp = neighbours(c, q, below, above, NZ)
        return (xp - xm) * 0.5, (yp - ym) * 0.5, xp + xm + yp + ym - 4.0 * q

    _, _, zonal_lap = stencil(0, zonal)
    _, _, north_lap = stencil(1, north)
    heat_x, heat_y, heat_lap = stencil(2, heat)

    def running(v):
        total = v[0:8]
        sums = [total]
        for z in range(1, NZ):
            total = total + v[8 * z : 8 * z + 8]
            sums.append(total)
        return jnp.concatenate(sums, 0)

    rest = jnp.zeros((8 * (NZ - 1), LANES), F32)
    push_u = jnp.concatenate([stress[0:8], rest], 0)
    push_v = jnp.concatenate([stress[8:16], rest], 0)
    new = (
        wet * (zonal + CORIOLIS * north - PRESS * running(heat_x) + VISC * zonal_lap + push_u),
        wet * (north - CORIOLIS * zonal - PRESS * running(heat_y) + VISC * north_lap + push_v),
        heat + wet * (DIFFUSE * heat_lap - ADVECT * (zonal * heat_x + north * heat_y)),
    )
    for c in range(3):
        for z in range(NZ):
            out_ref[c, z] = new[c][8 * z + 1 : 8 * z + 5]
    return new


def stress_of(n_ref, weights_ref):
    total = jnp.zeros((16, LANES), F32)
    for x in range(ROWS):
        cells = n_ref[x].reshape(BINS, LANES).astype(BF16)
        total = total + jnp.dot(weights_ref[x], cells, preferred_element_type=F32)
    return total


def advance_waves(n_ref, xh_ref, yh_ref, rate_ref, wet, tab_ref, quarter, rows, emit):
    half = quarter // 2
    south = quarter in (1, 2)
    lanes = lane_of((NF, LANES))

    def body(j, carry):
        k = quarter * QUARTER + j
        below = jnp.where(k == 0, NDIR - 1, k - 1) if quarter == 0 else k - 1
        above = jnp.where(k == NDIR - 1, 0, k + 1) if quarter == 3 else k + 1
        kk = k - half * HALF
        edge = yh_ref[1, k - QUARTER] if south else yh_ref[0, k if quarter == 0 else k - HALF]
        weights = [tab_ref[t, k] for t in range(5)]

        def row(r):
            if r < 0:
                return xh_ref[0, r + 2, kk]
            return n_ref[r, k] if r < ROWS else xh_ref[1, r - ROWS, kk]

        results = []
        for x in rows:
            cell = n_ref[x, k]
            step = 1 if half else -1
            start = LANES - 2 if south else 0
            halo = jnp.concatenate(
                [roll(edge, start - (8 * g + 2 * x), 1) for g in range(4)], 0
            )
            if south:
                near_y = roll(jnp.where(lanes == LANES - 1, halo, cell), 1, 1)
                far_y = roll(jnp.where(lanes >= LANES - 2, halo, cell), 2, 1)
            else:
                near_y = roll(jnp.where(lanes == 0, halo, cell), -1, 1)
                far_y = roll(jnp.where(lanes < 2, halo, cell), -2, 1)
            rate = jnp.broadcast_to(rate_ref[k, x + 1 : x + 2, :], (NF, LANES))
            upwind = jnp.where(rate > 0.0, n_ref[x, below], n_ref[x, above])
            total = cell * weights[0] + row(x + step) * weights[1] + row(x + 2 * step) * weights[2]
            total = total + (near_y * weights[3] + far_y * weights[4])
            total = total + jnp.abs(rate) * (upwind - cell)
            results.append((x, total * wet[x]))
        emit(k, results)
        return carry

    lax.fori_loop(0, QUARTER, body, 0)


def wet_rows(mask_ref):
    wet = mask_ref[...].astype(F32)
    pad = jnp.zeros((1, LANES), F32)
    wet8 = jnp.concatenate([pad, wet, pad, pad, pad], 0)
    return [jnp.broadcast_to(wet[x : x + 1], (NF, LANES)) for x in range(ROWS)], wet8


def middle_kernel(n_ref, o_ref, mask_ref, tab_ref, w_ref, xe_in, xo_in, ye_in, yo_in,
                  new_ref, ocean_ref, xe_ref, xo_ref, ye_ref, yo_ref,
                  xh_ref, yh_ref, ext_ref, rate_ref, e_ref):
    lanes = lane_of((8, LANES))
    even_x, even_y = is_even("gx"), is_even("gy")
    wet, wet8 = wet_rows(mask_ref)
    left, right, below, above = land_halos(even_x, even_y, xe_in, xo_in, ye_in, yo_in, xh_ref, yh_ref)
    extend_ocean(o_ref, left, right, ext_ref)
    refraction_rates(ext_ref, below, above, rate_ref)
    for quarter in range(4):
        south = quarter in (1, 2)
        shift = QUARTER if south else (0 if quarter == 0 else HALF)

        def emit(k, results, south=south, shift=shift):
            cells = [v.astype(BF16).astype(F32) for _, v in results]
            for x, cell in enumerate(cells):
                new_ref[x, k] = cell
            pack_y_edges(cells, k - shift, south, e_ref.at[1 if south else 0], lanes)

        advance_waves(n_ref, xh_ref, yh_ref, rate_ref, wet, tab_ref, quarter, range(ROWS), emit)
    new = advance_ocean(ext_ref, below, above, stress_of(n_ref, w_ref), wet8, ocean_ref)
    rows = tuple(
        jnp.concatenate([new[c][8 * z + r : 8 * z + r + 1] for c in range(3) for z in range(NZ)], 0)
        for r in (1, ROWS)
    )
    send_x(new_ref, rows, xe_ref, jnp.logical_not(even_x))
    send_x(new_ref, rows, xo_ref, even_x)
    first, last = pack_ocean_columns(new, lanes)
    send_y(e_ref, first, last, even_y, (ye_ref, yo_ref))


def last_kernel(n_ref, o_ref, mask_ref, tab_ref, w_ref, xe_in, xo_in, ye_in, yo_in,
                out_ref, ocean_ref, xh_ref, yh_ref, ext_ref, rate_ref, t_ref):
    even_x, even_y = is_even("gx"), is_even("gy")
    wet, wet8 = wet_rows(mask_ref)
    left, right, below, above = land_halos(even_x, even_y, xe_in, xo_in, ye_in, yo_in, xh_ref, yh_ref)
    extend_ocean(o_ref, left, right, ext_ref)
    refraction_rates(ext_ref, below, above, rate_ref)

    def emit(k, results):
        for x, cell in results:
            t_ref[x, pl.ds(k, NF, stride=NDIR), :] = cell

    for quarter in range(4):
        advance_waves(n_ref, xh_ref, yh_ref, rate_ref, wet, tab_ref, quarter, range(ROWS), emit)
    advance_ocean(ext_ref, below, above, stress_of(n_ref, w_ref), wet8, ocean_ref)
    for x in range(ROWS):
        out_ref[x] = jnp.transpose(t_ref[x]).astype(BF16)


def swap_pairs(axis, odd):
    size = lax.axis_size(axis)
    pairs = []
    for i in range(odd, size - 1, 2):
        pairs += [(i, i + 1), (i + 1, i)]
    return pairs


def exchange(xe, xo, ye, yo):
    xo = lax.ppermute(xo, "gx", swap_pairs("gx", 1))
    xe = lax.ppermute(xe, "gx", swap_pairs("gx", 0))
    ye = lax.ppermute(ye, "gy", swap_pairs("gy", 0))
    yo = lax.ppermute(yo, "gy", swap_pairs("gy", 1))
    return xe, xo, ye, yo


def shapes(*wanted):
    return [jax.ShapeDtypeStruct(shape, dtype) for shape, dtype in wanted]


EDGES = (((XROWS, LANES), BF16), ((XROWS, LANES), BF16), ((YROWS, LANES), BF16), ((YROWS, LANES), BF16))
GRID = ((ROWS, NDIR, NF, LANES), F32)
SCRATCH = [
    pltpu.VMEM((2, 2, HALF, NF, LANES), F32),
    pltpu.VMEM((2, HALF, 8, LANES), F32),
    pltpu.VMEM((3, 8 * NZ, LANES), F32),
    pltpu.VMEM((NDIR, 8, LANES), F32),
]


def local(spectrum, ocean_state, sea_mask):
    ocean_shape = (ocean_state.shape, F32)
    n, *edges = pl.pallas_call(
        start_kernel,
        out_shape=shapes(GRID, *EDGES),
        in_specs=[VM] * 3,
        out_specs=[VM] * 5,
        scratch_shapes=[pltpu.VMEM((ROWS, BINS, LANES), F32), pltpu.VMEM((2, HALF, 8, LANES), F32)],
        compiler_params=PARAMS,
        name="start",
    )(spectrum, ocean_state, sea_mask)
    speed = jnp.asarray(np.broadcast_to(SPEEDS[:, None], (NF, LANES)))
    weights = jnp.asarray(stress_table(), dtype=BF16)
    tab = pl.pallas_call(
        tables_kernel,
        out_shape=shapes(((5, NDIR, NF, LANES), F32))[0],
        in_specs=[VM],
        out_specs=VM,
        compiler_params=PARAMS,
        name="tables",
    )(speed)
    edges = exchange(*edges)
    n, ocean, *edges = pl.pallas_call(
        middle_kernel,
        out_shape=shapes(GRID, ocean_shape, *EDGES),
        in_specs=[VM] * 9,
        out_specs=[VM] * 6,
        scratch_shapes=SCRATCH + [pltpu.VMEM((2, HALF, 8, LANES), F32)],
        compiler_params=PARAMS,
        name="middle",
    )(n, ocean_state, sea_mask, tab, weights, *edges)
    edges = exchange(*edges)
    return pl.pallas_call(
        last_kernel,
        out_shape=shapes((spectrum.shape, BF16), ocean_shape),
        in_specs=[VM] * 9,
        out_specs=[VM] * 2,
        scratch_shapes=SCRATCH + [pltpu.VMEM((ROWS, BINS, LANES), F32)],
        compiler_params=PARAMS,
        name="last",
    )(n, ocean, sea_mask, tab, weights, *edges)


def solution(mesh):
    placed = (P("gx", "gy", None), P(None, None, "gx", "gy"), P("gx", "gy"))
    return jax.shard_map(
        local,
        mesh=mesh,
        in_specs=placed,
        out_specs=(P("gx", "gy", None), P(None, None, "gx", "gy")),
        check_vma=False,
    )
```

```python
import math

import jax
import jax.numpy as jnp
import numpy as np
from jax import lax
from jax.experimental import pallas as pl
from jax.experimental.pallas import tpu as pltpu
from jax.sharding import PartitionSpec as P

NF = 32
NDIR = 36
NZ = 16
HALF = NDIR // 2
QUARTER = NDIR // 4
ROWS = 4
LANES = 128
BINS = NF * NDIR

COURANT = 0.4
RATIO = 0.93
TURN = 0.1
STRESS = 0.1
CORIOLIS = 0.2
PRESS = 0.1
VISC = 0.15
ADVECT = 0.5
DIFFUSE = 0.15

F32 = jnp.float32
BF16 = jnp.bfloat16
VM = pl.BlockSpec(memory_space=pltpu.VMEM)
PARAMS = pltpu.CompilerParams(vmem_limit_bytes=16 * 1024 * 1024)

SPECTRA = 2 * HALF * NF
OCEAN = 3 * NZ
XROWS = SPECTRA + 2 * OCEAN
YROWS = HALF * 8 + 16

ANGLES = -0.5 * math.pi + (np.arange(NDIR, dtype=np.float32) + np.float32(0.5)) * np.float32(
    2.0 * math.pi / NDIR
)
COS = np.cos(ANGLES).astype(np.float32)
SIN = np.sin(ANGLES).astype(np.float32)
SPEEDS = (COURANT * RATIO ** np.arange(NF, dtype=np.float64)).astype(np.float32)


def stress_table():
    table = np.zeros((ROWS, 16, NDIR, NF), np.float32)
    for c, part in enumerate((COS, SIN)):
        weights = np.float32(STRESS) * SPEEDS[None, :] * part[:, None]
        for x in range(ROWS):
            table[x, c * 8 + 1 + x] = weights
    return table.reshape(ROWS, 16, BINS)


def is_even(axis):
    return lax.rem(lax.axis_index(axis), 2) == 0


def split(v):
    high = v.astype(BF16).astype(F32)
    return high, v - high


def roll(v, shift, axis):
    return pltpu.roll(v, shift % v.shape[axis], axis)


def lane_of(shape):
    return lax.broadcasted_iota(jnp.int32, shape, len(shape) - 1)


def edge_tables():
    table = np.zeros((2, ROWS, LANES, LANES), np.float32)
    for side, start in enumerate((0, LANES - 2)):
        for x in range(ROWS):
            for g in range(4):
                for j in range(2):
                    table[side, x, start + j, 8 * g + 2 * x + j] = 1.0
    return table.reshape(2, ROWS * LANES, LANES)


def shift_tables():
    table = np.zeros((2, ROWS, 2 * LANES, 2 * LANES), np.float32)
    for side, sign in enumerate((1, -1)):
        for x in range(ROWS):
            for far in range(2):
                for lane in range(LANES):
                    source = lane + sign * (1 + far)
                    if 0 <= source < LANES:
                        table[side, x, source, far * LANES + lane] = 1.0
                    else:
                        j = source - LANES if sign > 0 else source + 2
                        for g in range(4):
                            table[side, x, LANES + 8 * g + 2 * x + j, far * LANES + lane] = 1.0
    return table


def pack_y_edges(n_ref, quarter, tables_ref, out_ref):
    south = quarter in (1, 2)
    first = quarter * QUARTER
    rows = [
        n_ref[x, first : first + QUARTER].reshape(QUARTER * NF, LANES).astype(BF16) for x in range(ROWS)
    ]
    found = jnp.dot(
        jnp.concatenate(rows, 1), tables_ref[1 if south else 0], preferred_element_type=F32
    ).reshape(QUARTER, 4, 8, LANES)
    group = lane_of((QUARTER, 8, LANES)) // 8
    packed = found[:, 0]
    for g in range(1, 4):
        packed = jnp.where(group == g, found[:, g], packed)
    at = 0 if quarter < 2 else QUARTER
    out_ref[1 if south else 0, at : at + QUARTER] = packed


def pack_ocean_columns(blocks, lanes):
    first = jnp.zeros((8, LANES), F32)
    last = jnp.zeros((8, LANES), F32)
    for c in range(3):
        for z in range(NZ):
            block = blocks[c][8 * z : 8 * z + 8]
            at = c * NZ + z
            first = jnp.where(lanes == at, roll(block, at, 1), first)
            last = jnp.where(lanes == at, roll(block, at - (LANES - 1), 1), last)
    return first, last


def send_x(n_ref, ocean_rows, mine_ref, low_side):
    row = jnp.where(low_side, 0, 2)
    first = jnp.where(low_side, HALF, 0)
    edge = n_ref[pl.ds(row, 2), pl.ds(first, HALF)]
    mine_ref[0:SPECTRA, :] = edge.reshape(SPECTRA, LANES).astype(BF16)
    low, high = ocean_rows
    whole, rest = split(jnp.where(low_side, low, high))
    mine_ref[SPECTRA : SPECTRA + OCEAN, :] = whole.astype(BF16)
    mine_ref[SPECTRA + OCEAN : XROWS, :] = rest.astype(BF16)


def send_y(edges_ref, first, last, even, outs):
    for slot, out_ref in enumerate(outs):
        takes_last = even if slot == 0 else jnp.logical_not(even)
        which = takes_last.astype(jnp.int32)
        out_ref[0 : HALF * 8, :] = edges_ref[which].reshape(HALF * 8, LANES).astype(BF16)
        whole, rest = split(jnp.where(takes_last, last, first))
        out_ref[HALF * 8 : YROWS, :] = jnp.concatenate([whole, rest], 0).astype(BF16)


def start_kernel(s_hbm, o_hbm, mask_hbm, edge_hbm, n_ref, xe_ref, xo_ref, ye_ref, yo_ref,
                 s_ref, o_ref, mask_ref, edge_ref, t_ref, e_ref, sems):
    copies = [pltpu.make_async_copy(mask_hbm, mask_ref, sems.at[ROWS])]
    copies += [pltpu.make_async_copy(s_hbm.at[x], s_ref.at[x], sems.at[x]) for x in range(ROWS)]
    copies += [
        pltpu.make_async_copy(o_hbm, o_ref, sems.at[ROWS + 1]),
        pltpu.make_async_copy(edge_hbm, edge_ref, sems.at[ROWS + 2]),
    ]
    for copy in copies:
        copy.start()
    copies[0].wait()
    wet = mask_ref[...].astype(F32)
    for x in range(ROWS):
        copies[1 + x].wait()
        t_ref[x] = jnp.transpose(s_ref[x].astype(F32))

    def body(k, carry):
        for x in range(ROWS):
            n_ref[x, k] = t_ref[x, pl.ds(k, NF, stride=NDIR), :] * wet[x : x + 1]
        return carry

    lax.fori_loop(0, NDIR, body, 0, unroll=2)
    even_x, even_y = is_even("gx"), is_even("gy")
    copies[-2].wait()
    rows = tuple(o_ref[:, :, r, :].reshape(OCEAN, LANES) for r in (0, ROWS - 1))
    send_x(n_ref, rows, xe_ref, jnp.logical_not(even_x))
    send_x(n_ref, rows, xo_ref, even_x)
    copies[-1].wait()
    for quarter in range(4):
        pack_y_edges(n_ref, quarter, edge_ref, e_ref)
    pad = jnp.zeros((1, LANES), F32)
    blocks = [
        jnp.concatenate(
            [part for z in range(NZ) for part in (pad, o_ref[c, z], pad, pad, pad)], 0
        )
        for c in range(3)
    ]
    first, last = pack_ocean_columns(blocks, lane_of((8, LANES)))
    send_y(e_ref, first, last, even_y, (ye_ref, yo_ref))


def tables_kernel(speed_ref, tab_ref):
    speed = speed_ref[...]
    for k in range(NDIR):
        cx, cy = speed * abs(float(COS[k])), speed * abs(float(SIN[k]))
        near_x, far_x = cx * (2.0 - cx), (0.5 * cx) * (cx - 1.0)
        near_y, far_y = cy * (2.0 - cy), (0.5 * cy) * (cy - 1.0)
        tab_ref[0, k] = 1.0 - ((near_x + far_x) + (near_y + far_y))
        tab_ref[1, k] = near_x
        tab_ref[2, k] = far_x
        tab_ref[3, k] = near_y
        tab_ref[4, k] = far_y


def land_halos(even_x, even_y, xe_ref, xo_ref, ye_ref, yo_ref, xh_ref, yh_ref):
    side = even_x.astype(jnp.int32)
    shape = (2, HALF, NF, LANES)
    xh_ref[side] = xe_ref[0:SPECTRA, :].astype(F32).reshape(shape)
    xh_ref[1 - side] = xo_ref[0:SPECTRA, :].astype(F32).reshape(shape)

    def rows(ref):
        return ref[SPECTRA : SPECTRA + OCEAN, :].astype(F32) + ref[SPECTRA + OCEAN : XROWS, :].astype(F32)

    a, b = rows(xe_ref), rows(xo_ref)
    left, right = jnp.where(even_x, b, a), jnp.where(even_x, a, b)
    shape = (HALF, 8, LANES)
    a = ye_ref[0 : HALF * 8, :].astype(F32)
    b = yo_ref[0 : HALF * 8, :].astype(F32)
    group = lane_of(shape) // 8
    for to, pair in ((0, (a, b)), (1, (b, a))):
        edge = jnp.where(even_y, *pair).reshape(shape)
        parts = [jnp.where(group == g, edge, 0.0)[:, None] for g in range(4)]
        yh_ref[to] = jnp.concatenate(parts, 1).reshape(HALF * NF, LANES).astype(BF16)

    def columns(ref):
        both = ref[HALF * 8 : YROWS, :].astype(F32)
        return both[0:8] + both[8:16]

    a, b = columns(ye_ref), columns(yo_ref)
    above, below = jnp.where(even_y, a, b), jnp.where(even_y, b, a)
    return left, right, below, above


def extend_ocean(o_ref, left, right, ext_ref):
    for c in range(3):
        for z in range(NZ):
            at = c * NZ + z
            ext_ref[c, 8 * z : 8 * z + 1, :] = left[at : at + 1]
            ext_ref[c, 8 * z + 1 : 8 * z + 5, :] = o_ref[c, z]
            ext_ref[c, 8 * z + 5 : 8 * z + 6, :] = right[at : at + 1]
            ext_ref[c, 8 * z + 6 : 8 * z + 8, :] = jnp.zeros((2, LANES), F32)


def neighbours(c, q, below, above, levels):
    lanes = lane_of(q.shape)
    low = jnp.concatenate([roll(below, -(c * NZ + z), 1) for z in range(levels)], 0)
    high = jnp.concatenate([roll(above, LANES - 1 - (c * NZ + z), 1) for z in range(levels)], 0)
    return (
        roll(q, 1, 0),
        roll(q, -1, 0),
        jnp.where(lanes == 0, low, roll(q, 1, 1)),
        jnp.where(lanes == LANES - 1, high, roll(q, -1, 1)),
    )


def refraction_rates(ext_ref, below, above, rate_ref):
    grads = []
    for c in range(2):
        xm, xp, ym, yp = neighbours(c, ext_ref[c, 0:8, :], below, above, 1)
        grads.append(((xp - xm) * 0.5, (yp - ym) * 0.5))
    (ux, uy), (vx, vy) = grads
    stretch = ux - vy
    for k in range(NDIR):
        c, s = float(COS[k]), float(SIN[k])
        rate_ref[k] = (TURN * c * s) * stretch + (TURN * s * s) * vx - (TURN * c * c) * uy


def advance_ocean(ext_ref, below, above, stress, wet8, out_ref):
    zonal, north, heat = (ext_ref[c] for c in range(3))
    wet = jnp.concatenate([wet8] * NZ, 0)

    def stencil(c, q):
        xm, xp, ym, yp = neighbours(c, q, below, above, NZ)
        return (xp - xm) * 0.5, (yp - ym) * 0.5, xp + xm + yp + ym - 4.0 * q

    _, _, zonal_lap = stencil(0, zonal)
    _, _, north_lap = stencil(1, north)
    heat_x, heat_y, heat_lap = stencil(2, heat)

    def running(v):
        total = v[0:8]
        sums = [total]
        for z in range(1, NZ):
            total = total + v[8 * z : 8 * z + 8]
            sums.append(total)
        return jnp.concatenate(sums, 0)

    rest = jnp.zeros((8 * (NZ - 1), LANES), F32)
    push_u = jnp.concatenate([stress[0:8], rest], 0)
    push_v = jnp.concatenate([stress[8:16], rest], 0)
    new = (
        wet * (zonal + CORIOLIS * north - PRESS * running(heat_x) + VISC * zonal_lap + push_u),
        wet * (north - CORIOLIS * zonal - PRESS * running(heat_y) + VISC * north_lap + push_v),
        heat + wet * (DIFFUSE * heat_lap - ADVECT * (zonal * heat_x + north * heat_y)),
    )
    for c in range(3):
        for z in range(NZ):
            out_ref[c, z] = new[c][8 * z + 1 : 8 * z + 5]
    return new


def stress_of(n_ref, weights_ref):
    total = jnp.zeros((16, LANES), F32)
    for x in range(ROWS):
        cells = n_ref[x].reshape(BINS, LANES).astype(BF16)
        total = total + jnp.dot(weights_ref[x], cells, preferred_element_type=F32)
    return total


def advance_waves(n_ref, xh_ref, yh_ref, rate_ref, wet, tab_ref, shift_ref, ys_ref, quarter, rows, emit):
    half = quarter // 2
    side = 1 if quarter in (1, 2) else 0
    size = QUARTER * NF
    first = quarter * QUARTER
    edges = yh_ref[side, 0:size, :] if quarter < 2 else yh_ref[side, size : 2 * size, :]
    for x in rows:
        cells = n_ref[x, first : first + QUARTER].reshape(size, LANES).astype(BF16)
        ys_ref[x] = jnp.dot(
            jnp.concatenate([cells, edges], 1), shift_ref[side, x], preferred_element_type=F32
        )

    def body(j, carry):
        k = first + j
        below = jnp.where(k == 0, NDIR - 1, k - 1) if quarter == 0 else k - 1
        above = jnp.where(k == NDIR - 1, 0, k + 1) if quarter == 3 else k + 1
        kk = k - half * HALF
        weights = [tab_ref[t, k] for t in range(5)]
        at = pl.ds(pl.multiple_of(j * NF, NF), NF)

        def row(r):
            if r < 0:
                return xh_ref[0, r + 2, kk]
            return n_ref[r, k] if r < ROWS else xh_ref[1, r - ROWS, kk]

        results = []
        for x in rows:
            cell = n_ref[x, k]
            step = 1 if half else -1
            near_y, far_y = ys_ref[x, at, 0:LANES], ys_ref[x, at, LANES : 2 * LANES]
            rate = jnp.broadcast_to(rate_ref[k, x + 1 : x + 2, :], (NF, LANES))
            upwind = jnp.where(rate > 0.0, n_ref[x, below], n_ref[x, above])
            total = cell * weights[0] + row(x + step) * weights[1] + row(x + 2 * step) * weights[2]
            total = total + (near_y * weights[3] + far_y * weights[4])
            total = total + jnp.abs(rate) * (upwind - cell)
            results.append((x, total * wet[x]))
        emit(k, results)
        return carry

    lax.fori_loop(0, QUARTER, body, 0)


def wet_rows(mask_ref):
    wet = mask_ref[...].astype(F32)
    pad = jnp.zeros((1, LANES), F32)
    wet8 = jnp.concatenate([pad, wet, pad, pad, pad], 0)
    return [jnp.broadcast_to(wet[x : x + 1], (NF, LANES)) for x in range(ROWS)], wet8


def middle_kernel(n_ref, o_ref, mask_ref, tab_ref, w_ref, shift_ref, edge_ref, xe_in, xo_in, ye_in, yo_in,
                  new_ref, ocean_ref, xe_ref, xo_ref, ye_ref, yo_ref,
                  xh_ref, yh_ref, ext_ref, rate_ref, ys_ref, e_ref):
    lanes = lane_of((8, LANES))
    even_x, even_y = is_even("gx"), is_even("gy")
    wet, wet8 = wet_rows(mask_ref)
    left, right, below, above = land_halos(even_x, even_y, xe_in, xo_in, ye_in, yo_in, xh_ref, yh_ref)
    extend_ocean(o_ref, left, right, ext_ref)
    refraction_rates(ext_ref, below, above, rate_ref)
    def emit(k, results):
        for x, cell in results:
            new_ref[x, k] = cell.astype(BF16).astype(F32)

    for quarter in range(4):
        advance_waves(n_ref, xh_ref, yh_ref, rate_ref, wet, tab_ref, shift_ref, ys_ref, quarter, range(ROWS), emit)
        pack_y_edges(new_ref, quarter, edge_ref, e_ref)
    new = advance_ocean(ext_ref, below, above, stress_of(n_ref, w_ref), wet8, ocean_ref)
    rows = tuple(
        jnp.concatenate([new[c][8 * z + r : 8 * z + r + 1] for c in range(3) for z in range(NZ)], 0)
        for r in (1, ROWS)
    )
    send_x(new_ref, rows, xe_ref, jnp.logical_not(even_x))
    send_x(new_ref, rows, xo_ref, even_x)
    first, last = pack_ocean_columns(new, lanes)
    send_y(e_ref, first, last, even_y, (ye_ref, yo_ref))


def last_kernel(n_ref, o_ref, mask_ref, tab_ref, w_ref, shift_ref, xe_in, xo_in, ye_in, yo_in,
                out_ref, ocean_ref, xh_ref, yh_ref, ext_ref, rate_ref, ys_ref, t_ref):
    even_x, even_y = is_even("gx"), is_even("gy")
    wet, wet8 = wet_rows(mask_ref)
    left, right, below, above = land_halos(even_x, even_y, xe_in, xo_in, ye_in, yo_in, xh_ref, yh_ref)
    extend_ocean(o_ref, left, right, ext_ref)
    refraction_rates(ext_ref, below, above, rate_ref)

    def emit(k, results):
        for x, cell in results:
            t_ref[x, pl.ds(k, NF, stride=NDIR), :] = cell

    for quarter in range(4):
        advance_waves(n_ref, xh_ref, yh_ref, rate_ref, wet, tab_ref, shift_ref, ys_ref, quarter, range(ROWS), emit)
    advance_ocean(ext_ref, below, above, stress_of(n_ref, w_ref), wet8, ocean_ref)
    for x in range(ROWS):
        out_ref[x] = jnp.transpose(t_ref[x]).astype(BF16)


def swap_pairs(axis, odd):
    size = lax.axis_size(axis)
    pairs = []
    for i in range(odd, size - 1, 2):
        pairs += [(i, i + 1), (i + 1, i)]
    return pairs


def exchange(xe, xo, ye, yo):
    xo = lax.ppermute(xo, "gx", swap_pairs("gx", 1))
    xe = lax.ppermute(xe, "gx", swap_pairs("gx", 0))
    ye = lax.ppermute(ye, "gy", swap_pairs("gy", 0))
    yo = lax.ppermute(yo, "gy", swap_pairs("gy", 1))
    return xe, xo, ye, yo


def shapes(*wanted):
    return [jax.ShapeDtypeStruct(shape, dtype) for shape, dtype in wanted]


EDGES = (((XROWS, LANES), BF16), ((XROWS, LANES), BF16), ((YROWS, LANES), BF16), ((YROWS, LANES), BF16))
GRID = ((ROWS, NDIR, NF, LANES), F32)
SCRATCH = [
    pltpu.VMEM((2, 2, HALF, NF, LANES), F32),
    pltpu.VMEM((2, HALF * NF, LANES), BF16),
    pltpu.VMEM((3, 8 * NZ, LANES), F32),
    pltpu.VMEM((NDIR, 8, LANES), F32),
    pltpu.VMEM((ROWS, QUARTER * NF, 2 * LANES), F32),
]


def local(spectrum, ocean_state, sea_mask):
    ocean_shape = (ocean_state.shape, F32)
    edge_table = jnp.asarray(edge_tables(), dtype=BF16)
    n, *edges = pl.pallas_call(
        start_kernel,
        out_shape=shapes(GRID, *EDGES),
        in_specs=[pl.BlockSpec(memory_space=pl.ANY)] * 4,
        out_specs=[VM] * 5,
        scratch_shapes=[
            pltpu.VMEM(spectrum.shape, BF16),
            pltpu.VMEM(ocean_state.shape, F32),
            pltpu.VMEM(sea_mask.shape, jnp.int32),
            pltpu.VMEM(edge_table.shape, BF16),
            pltpu.VMEM((ROWS, BINS, LANES), F32),
            pltpu.VMEM((2, HALF, 8, LANES), F32),
            pltpu.SemaphoreType.DMA((ROWS + 3,)),
        ],
        compiler_params=pltpu.CompilerParams(vmem_limit_bytes=56 * 1024 * 1024),
        name="start",
    )(spectrum, ocean_state, sea_mask, edge_table)
    speed = jnp.asarray(np.broadcast_to(SPEEDS[:, None], (NF, LANES)).copy())
    weights = jnp.asarray(stress_table(), dtype=BF16)
    shift_table = jnp.asarray(shift_tables(), dtype=BF16)
    tab = pl.pallas_call(
        tables_kernel,
        out_shape=shapes(((5, NDIR, NF, LANES), F32))[0],
        in_specs=[VM],
        out_specs=VM,
        compiler_params=PARAMS,
        name="tables",
    )(speed)
    edges = exchange(*edges)
    n, ocean, *edges = pl.pallas_call(
        middle_kernel,
        out_shape=shapes(GRID, ocean_shape, *EDGES),
        in_specs=[VM] * 11,
        out_specs=[VM] * 6,
        scratch_shapes=SCRATCH + [pltpu.VMEM((2, HALF, 8, LANES), F32)],
        compiler_params=PARAMS,
        name="middle",
    )(n, ocean_state, sea_mask, tab, weights, shift_table, edge_table, *edges)
    edges = exchange(*edges)
    return pl.pallas_call(
        last_kernel,
        out_shape=shapes((spectrum.shape, BF16), ocean_shape),
        in_specs=[VM] * 10,
        out_specs=[VM] * 2,
        scratch_shapes=SCRATCH + [pltpu.VMEM((ROWS, BINS, LANES), F32)],
        compiler_params=PARAMS,
        name="last",
    )(n, ocean, sea_mask, tab, weights, shift_table, *edges)


def solution(mesh):
    placed = (P("gx", "gy", None), P(None, None, "gx", "gy"), P("gx", "gy"))
    return jax.shard_map(
        local,
        mesh=mesh,
        in_specs=placed,
        out_specs=(P("gx", "gy", None), P(None, None, "gx", "gy")),
        check_vma=False,
    )
```

```python
import math

import jax
import jax.numpy as jnp
import numpy as np
from jax import lax
from jax.experimental import pallas as pl
from jax.experimental.pallas import tpu as pltpu
from jax.sharding import PartitionSpec as P

NF = 32
NDIR = 36
NZ = 16
HALF = NDIR // 2
QUARTER = NDIR // 4
ROWS = 4
LANES = 128
BINS = NF * NDIR

COURANT = 0.4
RATIO = 0.93
TURN = 0.1
STRESS = 0.1
CORIOLIS = 0.2
PRESS = 0.1
VISC = 0.15
ADVECT = 0.5
DIFFUSE = 0.15

F32 = jnp.float32
BF16 = jnp.bfloat16
VM = pl.BlockSpec(memory_space=pltpu.VMEM)
HBM = pl.BlockSpec(memory_space=pl.ANY)
FIRST = pltpu.CompilerParams(vmem_limit_bytes=56 * 1024 * 1024)
PARAMS = pltpu.CompilerParams(vmem_limit_bytes=16 * 1024 * 1024)

SPECTRA = 2 * HALF * NF
OCEAN = 3 * NZ
XROWS = SPECTRA + 2 * OCEAN
YROWS = HALF * 8 + 16

ANGLES = -0.5 * math.pi + (np.arange(NDIR, dtype=np.float32) + np.float32(0.5)) * np.float32(
    2.0 * math.pi / NDIR
)
COS = np.cos(ANGLES).astype(np.float32)
SIN = np.sin(ANGLES).astype(np.float32)
SPEEDS = (COURANT * RATIO ** np.arange(NF, dtype=np.float64)).astype(np.float32)


def stress_table():
    table = np.zeros((ROWS, 16, NDIR, NF), np.float32)
    for c, part in enumerate((COS, SIN)):
        weights = np.float32(STRESS) * SPEEDS[None, :] * part[:, None]
        for x in range(ROWS):
            table[x, c * 8 + 1 + x] = weights
    return table.reshape(ROWS, 16, BINS)


def is_even(axis):
    return lax.rem(lax.axis_index(axis), 2) == 0


def inside(axis):
    i = lax.axis_index(axis)
    return jnp.logical_and(i > 0, i < lax.axis_size(axis) - 1)


def split(v):
    high = v.astype(BF16).astype(F32)
    return high, v - high


def roll(v, shift, axis):
    return pltpu.roll(v, shift % v.shape[axis], axis)


def lane_of(shape):
    return lax.broadcasted_iota(jnp.int32, shape, len(shape) - 1)


def edge_tables():
    table = np.zeros((2, ROWS, LANES, LANES), np.float32)
    for side, start in enumerate((0, LANES - 2)):
        for x in range(ROWS):
            for g in range(4):
                for j in range(2):
                    table[side, x, start + j, 8 * g + 2 * x + j] = 1.0
    return table.reshape(2, ROWS * LANES, LANES)


def shift_tables():
    table = np.zeros((2, 2 * LANES, 2 * LANES), np.float32)
    for side, sign in enumerate((1, -1)):
        for far in range(2):
            for lane in range(LANES):
                source = lane + sign * (1 + far)
                if 0 <= source < LANES:
                    table[side, source, far * LANES + lane] = 1.0
                else:
                    j = source - LANES if sign > 0 else source + 2
                    for x in range(ROWS):
                        for g in range(4):
                            table[side, LANES + 32 * x + 8 * g + 2 * x + j, far * LANES + lane] = 1.0
    return table


def pack_y_edges(n_ref, quarter, tables_ref, out_ref):
    south = quarter in (1, 2)
    first = quarter * QUARTER
    rows = [
        n_ref[x, first : first + QUARTER].reshape(QUARTER * NF, LANES).astype(BF16) for x in range(ROWS)
    ]
    found = jnp.dot(
        jnp.concatenate(rows, 1), tables_ref[1 if south else 0], preferred_element_type=F32
    ).reshape(QUARTER, 4, 8, LANES)
    group = lane_of((QUARTER, 8, LANES)) // 8
    packed = found[:, 0]
    for g in range(1, 4):
        packed = jnp.where(group == g, found[:, g], packed)
    at = 0 if quarter < 2 else QUARTER
    out_ref[1 if south else 0, at : at + QUARTER] = packed


def pack_ocean_columns(blocks, lanes):
    first = jnp.zeros((8, LANES), F32)
    last = jnp.zeros((8, LANES), F32)
    for c in range(3):
        for z in range(NZ):
            block = blocks[c][8 * z : 8 * z + 8]
            at = c * NZ + z
            first = jnp.where(lanes == at, roll(block, at, 1), first)
            last = jnp.where(lanes == at, roll(block, at - (LANES - 1), 1), last)
    return first, last


def send_x(n_ref, ocean_rows, mine_ref, low_side):
    row = jnp.where(low_side, 0, 2)
    first = jnp.where(low_side, HALF, 0)
    edge = n_ref[pl.ds(row, 2), pl.ds(first, HALF)]
    mine_ref[0:SPECTRA, :] = edge.reshape(SPECTRA, LANES).astype(BF16)
    send_ocean_row(ocean_rows, mine_ref, low_side)


def send_ocean_row(ocean_rows, mine_ref, low_side):
    low, high = ocean_rows
    whole, rest = split(jnp.where(low_side, low, high))
    mine_ref[SPECTRA : SPECTRA + OCEAN, :] = whole.astype(BF16)
    mine_ref[SPECTRA + OCEAN : XROWS, :] = rest.astype(BF16)


def send_y(edges_ref, first, last, even, outs):
    for slot, out_ref in enumerate(outs):
        takes_last = even if slot == 0 else jnp.logical_not(even)
        which = takes_last.astype(jnp.int32)
        out_ref[0 : HALF * 8, :] = edges_ref[which].reshape(HALF * 8, LANES).astype(BF16)
        whole, rest = split(jnp.where(takes_last, last, first))
        out_ref[HALF * 8 : YROWS, :] = jnp.concatenate([whole, rest], 0).astype(BF16)


def first_kernel(s_hbm, o_hbm, mask_hbm, xo_ref, s_ref, o_ref, mask_ref, t_ref, sems):
    low_side = is_even("gx")
    row = jnp.where(low_side, 0, 2)
    first = jnp.where(low_side, HALF, 0)
    copies = [pltpu.make_async_copy(s_hbm.at[row + r], s_ref.at[r], sems.at[r]) for r in range(2)]
    copies.append(pltpu.make_async_copy(mask_hbm, mask_ref, sems.at[2]))
    copies.append(pltpu.make_async_copy(o_hbm, o_ref, sems.at[3]))
    for copy in copies:
        copy.start()
    copies[2].wait()
    for r in range(2):
        copies[r].wait()
        t_ref[r] = jnp.transpose(s_ref[r].astype(F32))
        wet = mask_ref[pl.ds(row + r, 1), :].astype(F32)

        def body(kk, carry, r=r, wet=wet):
            at = pl.ds(pl.multiple_of((r * HALF + kk) * NF, NF), NF)
            xo_ref[at, :] = (t_ref[r, pl.ds(first + kk, NF, stride=NDIR), :] * wet).astype(BF16)
            return carry

        lax.fori_loop(0, HALF, body, 0, unroll=2)
    copies[3].wait()
    rows = tuple(o_ref[:, :, r, :].reshape(OCEAN, LANES) for r in (0, ROWS - 1))
    send_ocean_row(rows, xo_ref, low_side)


def start_kernel(s_ref, o_ref, mask_ref, edge_ref, speed_ref,
                 n_ref, xe_ref, ye_ref, yo_ref, tab_ref, t_ref, e_ref):
    wet = mask_ref[...].astype(F32)
    for x in range(ROWS):
        t_ref[x] = jnp.transpose(s_ref[x].astype(F32))

    def body(k, carry):
        for x in range(ROWS):
            n_ref[x, k] = t_ref[x, pl.ds(k, NF, stride=NDIR), :] * wet[x : x + 1]
        return carry

    lax.fori_loop(0, NDIR, body, 0, unroll=2)
    even_x, even_y = is_even("gx"), is_even("gy")
    rows = tuple(o_ref[:, :, r, :].reshape(OCEAN, LANES) for r in (0, ROWS - 1))
    send_x(n_ref, rows, xe_ref, jnp.logical_not(even_x))
    for quarter in range(4):
        pack_y_edges(n_ref, quarter, edge_ref, e_ref)
    pad = jnp.zeros((1, LANES), F32)
    blocks = [
        jnp.concatenate(
            [part for z in range(NZ) for part in (pad, o_ref[c, z], pad, pad, pad)], 0
        )
        for c in range(3)
    ]
    first, last = pack_ocean_columns(blocks, lane_of((8, LANES)))
    send_y(e_ref, first, last, even_y, (ye_ref, yo_ref))
    make_tables(speed_ref, tab_ref)


def make_tables(speed_ref, tab_ref):
    speed = speed_ref[...]
    for k in range(NDIR):
        cx, cy = speed * abs(float(COS[k])), speed * abs(float(SIN[k]))
        near_x, far_x = cx * (2.0 - cx), (0.5 * cx) * (cx - 1.0)
        near_y, far_y = cy * (2.0 - cy), (0.5 * cy) * (cy - 1.0)
        tab_ref[0, k] = 1.0 - ((near_x + far_x) + (near_y + far_y))
        tab_ref[1, k] = near_x
        tab_ref[2, k] = far_x
        tab_ref[3, k] = near_y
        tab_ref[4, k] = far_y


def y_spectra(even_y, ye_ref, yo_ref, yh_ref):
    shape = (HALF, 8, LANES)
    a = ye_ref[0 : HALF * 8, :].astype(F32)
    b = jnp.where(inside("gy"), yo_ref[0 : HALF * 8, :].astype(F32), 0.0)
    group = lane_of(shape) // 8
    for to, pair in ((0, (a, b)), (1, (b, a))):
        edge = jnp.where(even_y, *pair).reshape(shape)
        parts = [jnp.where(group == g, edge, 0.0)[:, None] for g in range(4)]
        yh_ref[to] = jnp.concatenate(parts, 1).reshape(HALF * NF, LANES).astype(BF16)


def y_ocean(even_y, ye_ref, yo_ref):
    def columns(ref):
        both = ref[HALF * 8 : YROWS, :].astype(F32)
        return both[0:8] + both[8:16]

    a, b = columns(ye_ref), jnp.where(inside("gy"), columns(yo_ref), 0.0)
    return jnp.where(even_y, b, a), jnp.where(even_y, a, b)


def x_ocean(even_x, xe_ref, xo_ref):
    def rows(ref):
        return ref[SPECTRA : SPECTRA + OCEAN, :].astype(F32) + ref[SPECTRA + OCEAN : XROWS, :].astype(F32)

    a, b = rows(xe_ref), jnp.where(inside("gx"), rows(xo_ref), 0.0)
    return jnp.where(even_x, b, a), jnp.where(even_x, a, b)


def extend_ocean(o_ref, left, right, ext_ref, levels=NZ):
    for c in range(3):
        for z in range(levels):
            at = c * NZ + z
            ext_ref[c, 8 * z : 8 * z + 1, :] = left[at : at + 1]
            ext_ref[c, 8 * z + 1 : 8 * z + 5, :] = o_ref[c, z]
            ext_ref[c, 8 * z + 5 : 8 * z + 6, :] = right[at : at + 1]
            ext_ref[c, 8 * z + 6 : 8 * z + 8, :] = jnp.zeros((2, LANES), F32)


def neighbours(c, q, below, above, levels):
    lanes = lane_of(q.shape)
    low = jnp.concatenate([roll(below, -(c * NZ + z), 1) for z in range(levels)], 0)
    high = jnp.concatenate([roll(above, LANES - 1 - (c * NZ + z), 1) for z in range(levels)], 0)
    return (
        roll(q, 1, 0),
        roll(q, -1, 0),
        jnp.where(lanes == 0, low, roll(q, 1, 1)),
        jnp.where(lanes == LANES - 1, high, roll(q, -1, 1)),
    )


def refraction_rates(ext_ref, below, above, rate_ref):
    grads = []
    for c in range(2):
        xm, xp, ym, yp = neighbours(c, ext_ref[c, 0:8, :], below, above, 1)
        grads.append(((xp - xm) * 0.5, (yp - ym) * 0.5))
    (ux, uy), (vx, vy) = grads
    stretch = ux - vy
    for k in range(NDIR):
        c, s = float(COS[k]), float(SIN[k])
        rate_ref[k] = (TURN * c * s) * stretch + (TURN * s * s) * vx - (TURN * c * c) * uy


def advance_ocean(ext_ref, below, above, stress, wet8, out_ref):
    zonal, north, heat = (ext_ref[c] for c in range(3))
    wet = jnp.concatenate([wet8] * NZ, 0)

    def stencil(c, q):
        xm, xp, ym, yp = neighbours(c, q, below, above, NZ)
        return (xp - xm) * 0.5, (yp - ym) * 0.5, xp + xm + yp + ym - 4.0 * q

    _, _, zonal_lap = stencil(0, zonal)
    _, _, north_lap = stencil(1, north)
    heat_x, heat_y, heat_lap = stencil(2, heat)

    def running(v):
        total = v[0:8]
        sums = [total]
        for z in range(1, NZ):
            total = total + v[8 * z : 8 * z + 8]
            sums.append(total)
        return jnp.concatenate(sums, 0)

    rest = jnp.zeros((8 * (NZ - 1), LANES), F32)
    push_u = jnp.concatenate([stress[0:8], rest], 0)
    push_v = jnp.concatenate([stress[8:16], rest], 0)
    new = (
        wet * (zonal + CORIOLIS * north - PRESS * running(heat_x) + VISC * zonal_lap + push_u),
        wet * (north - CORIOLIS * zonal - PRESS * running(heat_y) + VISC * north_lap + push_v),
        heat + wet * (DIFFUSE * heat_lap - ADVECT * (zonal * heat_x + north * heat_y)),
    )
    for c in range(3):
        for z in range(NZ):
            out_ref[c, z] = new[c][8 * z + 1 : 8 * z + 5]
    return new


def stress_of(n_ref, weights_ref):
    total = jnp.zeros((16, LANES), F32)
    for x in range(ROWS):
        cells = n_ref[x].reshape(BINS, LANES).astype(BF16)
        total = total + jnp.dot(weights_ref[x], cells, preferred_element_type=F32)
    return total


def refraction(n_ref, rate_ref, x, k):
    below = jnp.where(k == 0, NDIR - 1, k - 1)
    above = jnp.where(k == NDIR - 1, 0, k + 1)
    rate = jnp.broadcast_to(rate_ref[k, pl.ds(x + 1, 1), :], (NF, LANES))
    upwind = jnp.where(rate > 0.0, n_ref[x, below], n_ref[x, above])
    return jnp.abs(rate) * (upwind - n_ref[x, k])


def inner_waves(n_ref, yh_ref, rate_ref, wet, tab_ref, shift_ref, ys_ref, acc_ref, keep):
    size = QUARTER * NF
    for quarter in range(4):
        step = 1 if quarter >= 2 else -1
        side = 1 if quarter in (1, 2) else 0
        first = quarter * QUARTER
        edges = yh_ref[side, 0:size, :] if quarter < 2 else yh_ref[side, size : 2 * size, :]
        blank = jnp.zeros((LANES - 32, 2 * LANES), BF16)
        for x in range(ROWS):
            cells = n_ref[x, first : first + QUARTER].reshape(size, LANES).astype(BF16)
            edge_rows = shift_ref[side, LANES + 32 * x : LANES + 32 * x + 32, :]
            moves = jnp.concatenate([shift_ref[side, 0:LANES, :], edge_rows, blank], 0)
            ys_ref[x] = jnp.dot(jnp.concatenate([cells, edges], 1), moves, preferred_element_type=F32)

        def body(j, carry, first=first, step=step):
            k = first + j
            weights = [tab_ref[t, k] for t in range(5)]
            at = pl.ds(pl.multiple_of(j * NF, NF), NF)
            cells = [n_ref[x, k] for x in range(ROWS)]
            for x in range(ROWS):
                total = cells[x] * weights[0]
                for weight, other in zip(weights[1:3], (x + step, x + 2 * step)):
                    if 0 <= other < ROWS:
                        total = total + cells[other] * weight
                near_y, far_y = ys_ref[x, at, 0:LANES], ys_ref[x, at, LANES : 2 * LANES]
                total = total + (near_y * weights[3] + far_y * weights[4])
                if x in (1, 2):
                    total = total + refraction(n_ref, rate_ref, x, k)
                    if 0 <= x + 2 * step < ROWS:
                        total = keep(total * wet[x])
                acc_ref[x, k] = total
            return carry

        lax.fori_loop(0, QUARTER, body, 0)


def wet_row(mask_ref, x):
    return jnp.broadcast_to(mask_ref[pl.ds(x, 1), :].astype(F32), (NF, LANES))


def finish_far_half(n_ref, acc_ref, rate_ref, mask_ref, side, keep):
    x = 3 * side
    wet = wet_row(mask_ref, x)
    first = HALF * (1 - side)

    def body(kk, carry):
        k = first + kk
        acc_ref[x, k] = keep(wet * (acc_ref[x, k] + refraction(n_ref, rate_ref, x, k)))
        return carry

    lax.fori_loop(0, HALF, body, 0, unroll=2)


def finish_near_half(n_ref, acc_ref, rate_ref, mask_ref, tab_ref, halo_ref, known, side, keep):
    x, inner = 3 * side, 1 + side
    wet, wet_inner = wet_row(mask_ref, x), wet_row(mask_ref, inner)
    first = HALF * side

    def body(kk, carry):
        k = first + kk
        near = halo_ref[pl.ds(pl.multiple_of(((1 - side) * HALF + kk) * NF, NF), NF), :].astype(F32)
        far = halo_ref[pl.ds(pl.multiple_of((side * HALF + kk) * NF, NF), NF), :].astype(F32)
        near, far = jnp.where(known, near, 0.0), jnp.where(known, far, 0.0)
        total = acc_ref[x, k] + (near * tab_ref[1, k] + far * tab_ref[2, k])
        acc_ref[x, k] = keep(wet * (total + refraction(n_ref, rate_ref, x, k)))
        acc_ref[inner, k] = keep(wet_inner * (acc_ref[inner, k] + near * tab_ref[2, k]))
        return carry

    lax.fori_loop(0, HALF, body, 0, unroll=2)


def rounded(v):
    return v.astype(BF16).astype(F32)


def exact(v):
    return v


def wet_rows(mask_ref):
    wet = mask_ref[...].astype(F32)
    pad = jnp.zeros((1, LANES), F32)
    wet8 = jnp.concatenate([pad, wet, pad, pad, pad], 0)
    return [jnp.broadcast_to(wet[x : x + 1], (NF, LANES)) for x in range(ROWS)], wet8


def inner_kernel(n_ref, o_ref, mask_ref, tab_ref, w_ref, shift_ref, ye_in, yo_in,
                 acc_ref, stress_ref, yh_ref, ext_ref, rate_ref, ys_ref):
    even_y = is_even("gy")
    wet, _ = wet_rows(mask_ref)
    y_spectra(even_y, ye_in, yo_in, yh_ref)
    below, above = y_ocean(even_y, ye_in, yo_in)
    unknown = jnp.zeros((OCEAN, LANES), F32)
    extend_ocean(o_ref, unknown, unknown, ext_ref, 1)
    refraction_rates(ext_ref, below, above, rate_ref)
    stress_ref[...] = stress_of(n_ref, w_ref)
    inner_waves(n_ref, yh_ref, rate_ref, wet, tab_ref, shift_ref, ys_ref, acc_ref, rounded)


def send_kernel(n_ref, acc_in, o_ref, mask_ref, stress_ref, xe_in, xo_in, ye_in, yo_in,
                acc_ref, ocean_ref, rate_ref, xo_ref, xrow_ref, ycol_ref, ext_ref):
    even_x, even_y = is_even("gx"), is_even("gy")
    below, above = y_ocean(even_y, ye_in, yo_in)
    left, right = x_ocean(even_x, xe_in, xo_in)
    extend_ocean(o_ref, left, right, ext_ref)
    refraction_rates(ext_ref, below, above, rate_ref)
    finish_far_half(n_ref, acc_ref, rate_ref, mask_ref, 1 - even_x.astype(jnp.int32), rounded)
    _, wet8 = wet_rows(mask_ref)
    new = advance_ocean(ext_ref, below, above, stress_ref[...], wet8, ocean_ref)
    rows = tuple(
        jnp.concatenate([new[c][8 * z + r : 8 * z + r + 1] for c in range(3) for z in range(NZ)], 0)
        for r in (1, ROWS)
    )
    send_x(acc_ref, rows, xo_ref, even_x)
    xrow_ref[...] = jnp.where(even_x, rows[1], rows[0])
    ycol_ref[0], ycol_ref[1] = pack_ocean_columns(new, lane_of((8, LANES)))


def rest_kernel(n_ref, acc_in, mask_ref, tab_ref, rate_ref, edge_ref, xrow_ref, ycol_ref, xe_in, xo_in,
                acc_ref, xe_ref, ye_ref, yo_ref, e_ref):
    even_x, even_y = is_even("gx"), is_even("gy")
    side = even_x.astype(jnp.int32)
    finish_near_half(n_ref, acc_ref, rate_ref, mask_ref, tab_ref, xo_in, inside("gx"), 1 - side, rounded)
    finish_near_half(n_ref, acc_ref, rate_ref, mask_ref, tab_ref, xe_in, True, side, rounded)
    finish_far_half(n_ref, acc_ref, rate_ref, mask_ref, side, rounded)
    row = xrow_ref[...]
    send_x(acc_ref, (row, row), xe_ref, jnp.logical_not(even_x))
    for quarter in range(4):
        pack_y_edges(acc_ref, quarter, edge_ref, e_ref)
    send_y(e_ref, ycol_ref[0], ycol_ref[1], even_y, (ye_ref, yo_ref))


def write_rows(acc_ref, first, t_ref, block_ref, out_hbm, sems):
    copies = []
    for r in range(2):

        def body(k, carry, r=r):
            t_ref[r, pl.ds(k, NF, stride=NDIR), :] = acc_ref[first + r, k]
            return carry

        lax.fori_loop(0, NDIR, body, 0, unroll=2)
        block_ref[r] = jnp.transpose(t_ref[r]).astype(BF16)
        copies.append(pltpu.make_async_copy(block_ref.at[r], out_hbm.at[first + r], sems.at[r]))
        copies[-1].start()
    for copy in copies:
        copy.wait()


def inner_last_kernel(n_ref, o_ref, mask_ref, tab_ref, w_ref, shift_ref, xe_in, ye_in, yo_in,
                      acc_ref, stress_ref, out_hbm,
                      yh_ref, ext_ref, rate_ref, ys_ref, t_ref, block_ref, sems):
    even_x, even_y = is_even("gx"), is_even("gy")
    wet, _ = wet_rows(mask_ref)
    y_spectra(even_y, ye_in, yo_in, yh_ref)
    below, above = y_ocean(even_y, ye_in, yo_in)
    left, right = x_ocean(even_x, xe_in, xe_in)
    extend_ocean(o_ref, left, right, ext_ref, 1)
    refraction_rates(ext_ref, below, above, rate_ref)
    stress_ref[...] = stress_of(n_ref, w_ref)
    inner_waves(n_ref, yh_ref, rate_ref, wet, tab_ref, shift_ref, ys_ref, acc_ref, exact)
    side = even_x.astype(jnp.int32)
    finish_near_half(n_ref, acc_ref, rate_ref, mask_ref, tab_ref, xe_in, True, side, exact)
    finish_far_half(n_ref, acc_ref, rate_ref, mask_ref, side, exact)
    write_rows(acc_ref, 2 * side, t_ref, block_ref, out_hbm, sems)


def last_kernel(n_ref, acc_in, o_ref, mask_ref, tab_ref, stress_ref, xe_in, xo_in, ye_in, yo_in, out_in,
                acc_ref, ocean_ref, out_hbm, ext_ref, rate_ref, t_ref, block_ref, sems):
    even_x, even_y = is_even("gx"), is_even("gy")
    below, above = y_ocean(even_y, ye_in, yo_in)
    left, right = x_ocean(even_x, xe_in, xo_in)
    extend_ocean(o_ref, left, right, ext_ref)
    refraction_rates(ext_ref, below, above, rate_ref)
    side = 1 - even_x.astype(jnp.int32)
    finish_near_half(n_ref, acc_ref, rate_ref, mask_ref, tab_ref, xo_in, inside("gx"), side, exact)
    finish_far_half(n_ref, acc_ref, rate_ref, mask_ref, side, exact)
    write_rows(acc_ref, 2 * side, t_ref, block_ref, out_hbm, sems)
    _, wet8 = wet_rows(mask_ref)
    advance_ocean(ext_ref, below, above, stress_ref[...], wet8, ocean_ref)


def swap(array, axis, odd):
    nx, ny = lax.axis_size("gx"), lax.axis_size("gy")
    pairs = []
    for i in range(nx):
        for j in range(ny):
            to = (i ^ 1, j) if axis == "gx" else (i, j ^ 1)
            if odd and axis == "gx":
                to = (((i + 1) ^ 1) - 1, j) if 0 < i < nx - 1 else (i, j ^ 1)
            if odd and axis == "gy":
                to = (i, ((j + 1) ^ 1) - 1) if 0 < j < ny - 1 else (i ^ 1, j)
            pairs.append((i * ny + j, to[0] * ny + to[1]))
    return lax.ppermute(array, ("gx", "gy"), pairs)


def call(kernel, outs, ins, scratch, params=None, any_in=(), any_out=(), aliases=None, moved=8):
    places = [HBM if i in any_in else VM for i in range(len(ins))]
    return pl.pallas_call(
        kernel,
        out_shape=[jax.ShapeDtypeStruct(shape, dtype) for shape, dtype in outs],
        in_specs=places,
        out_specs=[HBM if i in any_out else VM for i in range(len(outs))],
        scratch_shapes=scratch,
        compiler_params=params or PARAMS,
        input_output_aliases=aliases or {},
        cost_estimate=pl.CostEstimate(flops=0, bytes_accessed=moved * 1024 * 1024, transcendentals=0),
        name=kernel.__name__.removesuffix("_kernel"),
    )(*ins)


GRID = ((ROWS, NDIR, NF, LANES), F32)
XEDGE = ((XROWS, LANES), BF16)
YEDGE = ((YROWS, LANES), BF16)
DRIVE = ((16, LANES), F32)
RATES = ((NDIR, 8, LANES), F32)
YH = pltpu.VMEM((2, HALF * NF, LANES), BF16)
EXT = pltpu.VMEM((3, 8 * NZ, LANES), F32)
RATE = pltpu.VMEM(*RATES)
SHIFTED = pltpu.VMEM((ROWS, QUARTER * NF, 2 * LANES), F32)
EDGES = pltpu.VMEM((2, HALF, 8, LANES), F32)
TURNED = pltpu.VMEM((2, BINS, LANES), F32)
BLOCK = pltpu.VMEM((2, LANES, BINS), BF16)


def local(spectrum, ocean_state, sea_mask):
    ocean_shape = (ocean_state.shape, F32)
    edge_table = jnp.asarray(edge_tables(), dtype=BF16)
    speed = jnp.asarray(np.broadcast_to(SPEEDS[:, None], (NF, LANES)).copy())
    weights = jnp.asarray(stress_table(), dtype=BF16)
    shift_table = jnp.asarray(shift_tables(), dtype=BF16)
    (xo,) = call(
        first_kernel,
        (XEDGE,),
        (spectrum, ocean_state, sea_mask),
        [
            pltpu.VMEM((2, *spectrum.shape[1:]), BF16),
            pltpu.VMEM(ocean_state.shape, F32),
            pltpu.VMEM(sea_mask.shape, jnp.int32),
            TURNED,
            pltpu.SemaphoreType.DMA((4,)),
        ],
        FIRST,
        any_in=(0, 1, 2),
        moved=32,
    )
    xo = swap(xo, "gx", 1)
    n, xe, ye, yo, tab = call(
        start_kernel,
        (GRID, XEDGE, YEDGE, YEDGE, ((5, NDIR, NF, LANES), F32)),
        (spectrum, ocean_state, sea_mask, edge_table, speed),
        [pltpu.VMEM((ROWS, BINS, LANES), F32), EDGES],
    )
    xe = swap(xe, "gx", 0)
    ye = swap(ye, "gy", 0)
    yo = swap(yo, "gy", 1)
    acc, stress = call(
        inner_kernel,
        (GRID, DRIVE),
        (n, ocean_state, sea_mask, tab, weights, shift_table, ye, yo),
        [YH, EXT, RATE, SHIFTED],
    )
    acc, ocean, rate, xo2, xrow, ycol = call(
        send_kernel,
        (GRID, ocean_shape, RATES, XEDGE, ((OCEAN, LANES), F32), ((2, 8, LANES), F32)),
        (n, acc, ocean_state, sea_mask, stress, xe, xo, ye, yo),
        [EXT],
        aliases={1: 0},
    )
    xo2 = swap(xo2, "gx", 1)
    n, xe, ye, yo = call(
        rest_kernel,
        (GRID, XEDGE, YEDGE, YEDGE),
        (n, acc, sea_mask, tab, rate, edge_table, xrow, ycol, xe, xo),
        [EDGES],
        aliases={1: 0},
        moved=64,
    )
    xe = swap(xe, "gx", 0)
    ye = swap(ye, "gy", 0)
    yo = swap(yo, "gy", 1)
    acc, stress, out = call(
        inner_last_kernel,
        (GRID, DRIVE, (spectrum.shape, BF16)),
        (n, ocean, sea_mask, tab, weights, shift_table, xe, ye, yo),
        [YH, EXT, RATE, SHIFTED, TURNED, BLOCK, pltpu.SemaphoreType.DMA((2,))],
        any_out=(2,),
    )
    _, ocean, out = call(
        last_kernel,
        (GRID, ocean_shape, (spectrum.shape, BF16)),
        (n, acc, ocean, sea_mask, tab, stress, xe, xo2, ye, yo, out),
        [EXT, RATE, TURNED, BLOCK, pltpu.SemaphoreType.DMA((2,))],
        any_in=(10,),
        any_out=(2,),
        aliases={1: 0, 10: 2},
    )
    return out, ocean


def solution(mesh):
    placed = (P("gx", "gy", None), P(None, None, "gx", "gy"), P("gx", "gy"))
    return jax.shard_map(
        local,
        mesh=mesh,
        in_specs=placed,
        out_specs=(P("gx", "gy", None), P(None, None, "gx", "gy")),
        check_vma=False,
    )
```

```python
import math

import jax
import jax.numpy as jnp
import numpy as np
from jax import lax
from jax.experimental import pallas as pl
from jax.experimental.pallas import tpu as pltpu
from jax.sharding import PartitionSpec as P

NF = 32
NDIR = 36
NZ = 16
HALF = NDIR // 2
QUARTER = NDIR // 4
ROWS = 4
LANES = 128
BINS = NF * NDIR

COURANT = 0.4
RATIO = 0.93
TURN = 0.1
STRESS = 0.1
CORIOLIS = 0.2
PRESS = 0.1
VISC = 0.15
ADVECT = 0.5
DIFFUSE = 0.15

F32 = jnp.float32
BF16 = jnp.bfloat16
VM = pl.BlockSpec(memory_space=pltpu.VMEM)
HBM = pl.BlockSpec(memory_space=pl.ANY)
FIRST = pltpu.CompilerParams(vmem_limit_bytes=56 * 1024 * 1024)
PARAMS = pltpu.CompilerParams(vmem_limit_bytes=16 * 1024 * 1024)

SPECTRA = 2 * HALF * NF
OCEAN = 3 * NZ
XROWS = SPECTRA + 2 * OCEAN
YROWS = HALF * 8 + 16

ANGLES = -0.5 * math.pi + (np.arange(NDIR, dtype=np.float32) + np.float32(0.5)) * np.float32(
    2.0 * math.pi / NDIR
)
COS = np.cos(ANGLES).astype(np.float32)
SIN = np.sin(ANGLES).astype(np.float32)
SPEEDS = (COURANT * RATIO ** np.arange(NF, dtype=np.float64)).astype(np.float32)


def stress_table():
    table = np.zeros((ROWS, 16, NDIR, NF), np.float32)
    for c, part in enumerate((COS, SIN)):
        weights = np.float32(STRESS) * SPEEDS[None, :] * part[:, None]
        for x in range(ROWS):
            table[x, c * 8 + 1 + x] = weights
    return table.reshape(ROWS, 16, BINS)


def is_even(axis):
    return lax.rem(lax.axis_index(axis), 2) == 0


def inside(axis):
    i = lax.axis_index(axis)
    return jnp.logical_and(i > 0, i < lax.axis_size(axis) - 1)


def split(v):
    high = v.astype(BF16).astype(F32)
    return high, v - high


def roll(v, shift, axis):
    return pltpu.roll(v, shift % v.shape[axis], axis)


def lane_of(shape):
    return lax.broadcasted_iota(jnp.int32, shape, len(shape) - 1)


def make_edge_tables(table_ref):
    source = lax.broadcasted_iota(jnp.int32, (LANES, LANES), 0)
    lane = lane_of((LANES, LANES)) % 8
    for side, start in enumerate((0, LANES - 2)):
        for x in range(ROWS):
            found = (lane == source + (2 * x - start)) & (lane >= 2 * x) & (lane < 2 * x + 2)
            table_ref[side, LANES * x : LANES * (x + 1), :] = jnp.where(found, 1.0, 0.0).astype(BF16)


def shift_tables():
    table = np.zeros((2, 2 * LANES, 2 * LANES), np.float32)
    for side, sign in enumerate((1, -1)):
        for far in range(2):
            for lane in range(LANES):
                source = lane + sign * (1 + far)
                if 0 <= source < LANES:
                    table[side, source, far * LANES + lane] = 1.0
                else:
                    j = source - LANES if sign > 0 else source + 2
                    for x in range(ROWS):
                        for g in range(4):
                            table[side, LANES + 32 * x + 8 * g + 2 * x + j, far * LANES + lane] = 1.0
    return table


def pack_y_edges(n_ref, quarter, tables_ref, out_ref):
    south = quarter in (1, 2)
    first = quarter * QUARTER
    rows = [
        n_ref[x, first : first + QUARTER].reshape(QUARTER * NF, LANES).astype(BF16) for x in range(ROWS)
    ]
    found = jnp.dot(
        jnp.concatenate(rows, 1), tables_ref[1 if south else 0], preferred_element_type=F32
    ).reshape(QUARTER, 4, 8, LANES)
    group = lane_of((QUARTER, 8, LANES)) // 8
    packed = found[:, 0]
    for g in range(1, 4):
        packed = jnp.where(group == g, found[:, g], packed)
    at = 0 if quarter < 2 else QUARTER
    out_ref[1 if south else 0, at : at + QUARTER] = packed


def pack_ocean_columns(blocks, lanes):
    first = jnp.zeros((8, LANES), F32)
    last = jnp.zeros((8, LANES), F32)
    for c in range(3):
        for z in range(NZ):
            block = blocks[c][8 * z : 8 * z + 8]
            at = c * NZ + z
            first = jnp.where(lanes == at, roll(block, at, 1), first)
            last = jnp.where(lanes == at, roll(block, at - (LANES - 1), 1), last)
    return first, last


def send_x(n_ref, ocean_rows, mine_ref, low_side):
    row = jnp.where(low_side, 0, 2)
    first = jnp.where(low_side, HALF, 0)
    edge = n_ref[pl.ds(row, 2), pl.ds(first, HALF)]
    mine_ref[0:SPECTRA, :] = edge.reshape(SPECTRA, LANES).astype(BF16)
    send_ocean_row(ocean_rows, mine_ref, low_side)


def send_ocean_row(ocean_rows, mine_ref, low_side):
    low, high = ocean_rows
    whole, rest = split(jnp.where(low_side, low, high))
    mine_ref[SPECTRA : SPECTRA + OCEAN, :] = whole.astype(BF16)
    mine_ref[SPECTRA + OCEAN : XROWS, :] = rest.astype(BF16)


def send_y(edges_ref, first, last, even, outs):
    for slot, out_ref in enumerate(outs):
        takes_last = even if slot == 0 else jnp.logical_not(even)
        which = takes_last.astype(jnp.int32)
        out_ref[0 : HALF * 8, :] = edges_ref[which].reshape(HALF * 8, LANES).astype(BF16)
        whole, rest = split(jnp.where(takes_last, last, first))
        out_ref[HALF * 8 : YROWS, :] = jnp.concatenate([whole, rest], 0).astype(BF16)


def first_kernel(s_hbm, o_hbm, mask_hbm, xo_ref, s_ref, o_ref, mask_ref, t_ref, sems):
    low_side = is_even("gx")
    row = jnp.where(low_side, 0, 2)
    first = jnp.where(low_side, HALF, 0)
    copies = [pltpu.make_async_copy(s_hbm.at[row + r], s_ref.at[r], sems.at[r]) for r in range(2)]
    copies.append(pltpu.make_async_copy(mask_hbm, mask_ref, sems.at[2]))
    copies.append(pltpu.make_async_copy(o_hbm, o_ref, sems.at[3]))
    for copy in copies:
        copy.start()
    copies[2].wait()
    for r in range(2):
        copies[r].wait()
        t_ref[r] = jnp.transpose(s_ref[r].astype(F32))
        wet = mask_ref[pl.ds(row + r, 1), :].astype(F32)

        def body(kk, carry, r=r, wet=wet):
            at = pl.ds(pl.multiple_of((r * HALF + kk) * NF, NF), NF)
            xo_ref[at, :] = (t_ref[r, pl.ds(first + kk, NF, stride=NDIR), :] * wet).astype(BF16)
            return carry

        lax.fori_loop(0, HALF, body, 0, unroll=6)
    copies[3].wait()
    rows = tuple(o_ref[:, :, r, :].reshape(OCEAN, LANES) for r in (0, ROWS - 1))
    send_ocean_row(rows, xo_ref, low_side)


def start_kernel(s_ref, o_ref, mask_ref,
                 n_ref, xe_ref, ye_ref, yo_ref, tab_ref, edge_ref, t_ref, e_ref):
    wet = mask_ref[...].astype(F32)
    for x in range(ROWS):
        t_ref[x] = jnp.transpose(s_ref[x].astype(F32))

    def body(k, carry):
        for x in range(ROWS):
            n_ref[x, k] = t_ref[x, pl.ds(k, NF, stride=NDIR), :] * wet[x : x + 1]
        return carry

    lax.fori_loop(0, NDIR, body, 0, unroll=6)
    even_x, even_y = is_even("gx"), is_even("gy")
    rows = tuple(o_ref[:, :, r, :].reshape(OCEAN, LANES) for r in (0, ROWS - 1))
    send_x(n_ref, rows, xe_ref, jnp.logical_not(even_x))
    make_edge_tables(edge_ref)
    for quarter in range(4):
        pack_y_edges(n_ref, quarter, edge_ref, e_ref)
    pad = jnp.zeros((1, LANES), F32)
    blocks = [
        jnp.concatenate(
            [part for z in range(NZ) for part in (pad, o_ref[c, z], pad, pad, pad)], 0
        )
        for c in range(3)
    ]
    first, last = pack_ocean_columns(blocks, lane_of((8, LANES)))
    send_y(e_ref, first, last, even_y, (ye_ref, yo_ref))
    make_tables(tab_ref)


def make_tables(tab_ref):
    row = lax.broadcasted_iota(jnp.int32, (8, LANES), 0)
    blocks = []
    for g in range(4):
        block = jnp.full((8, LANES), float(SPEEDS[8 * g]), F32)
        for i in range(1, 8):
            block = jnp.where(row == i, float(SPEEDS[8 * g + i]), block)
        blocks.append(block)
    speed = jnp.concatenate(blocks, 0)
    for k in range(NDIR):
        cx, cy = speed * abs(float(COS[k])), speed * abs(float(SIN[k]))
        near_x, far_x = cx * (2.0 - cx), (0.5 * cx) * (cx - 1.0)
        near_y, far_y = cy * (2.0 - cy), (0.5 * cy) * (cy - 1.0)
        tab_ref[0, k] = 1.0 - ((near_x + far_x) + (near_y + far_y))
        tab_ref[1, k] = near_x
        tab_ref[2, k] = far_x
        tab_ref[3, k] = near_y
        tab_ref[4, k] = far_y


def y_spectra(even_y, ye_ref, yo_ref, yh_ref):
    shape = (HALF, 8, LANES)
    a = ye_ref[0 : HALF * 8, :].astype(F32)
    b = jnp.where(inside("gy"), yo_ref[0 : HALF * 8, :].astype(F32), 0.0)
    group = lane_of(shape) // 8
    for to, pair in ((0, (a, b)), (1, (b, a))):
        edge = jnp.where(even_y, *pair).reshape(shape)
        parts = [jnp.where(group == g, edge, 0.0)[:, None] for g in range(4)]
        yh_ref[to] = jnp.concatenate(parts, 1).reshape(HALF * NF, LANES).astype(BF16)


def y_ocean(even_y, ye_ref, yo_ref):
    def columns(ref):
        both = ref[HALF * 8 : YROWS, :].astype(F32)
        return both[0:8] + both[8:16]

    a, b = columns(ye_ref), jnp.where(inside("gy"), columns(yo_ref), 0.0)
    return jnp.where(even_y, b, a), jnp.where(even_y, a, b)


def x_ocean(even_x, xe_ref, xo_ref):
    def rows(ref):
        return ref[SPECTRA : SPECTRA + OCEAN, :].astype(F32) + ref[SPECTRA + OCEAN : XROWS, :].astype(F32)

    a, b = rows(xe_ref), jnp.where(inside("gx"), rows(xo_ref), 0.0)
    return jnp.where(even_x, b, a), jnp.where(even_x, a, b)


def extend_ocean(o_ref, left, right, ext_ref, levels=NZ):
    for c in range(3):
        for z in range(levels):
            at = c * NZ + z
            ext_ref[c, 8 * z : 8 * z + 1, :] = left[at : at + 1]
            ext_ref[c, 8 * z + 1 : 8 * z + 5, :] = o_ref[c, z]
            ext_ref[c, 8 * z + 5 : 8 * z + 6, :] = right[at : at + 1]
            ext_ref[c, 8 * z + 6 : 8 * z + 8, :] = jnp.zeros((2, LANES), F32)


def neighbours(c, q, below, above, levels):
    lanes = lane_of(q.shape)
    low = jnp.concatenate([roll(below, -(c * NZ + z), 1) for z in range(levels)], 0)
    high = jnp.concatenate([roll(above, LANES - 1 - (c * NZ + z), 1) for z in range(levels)], 0)
    return (
        roll(q, 1, 0),
        roll(q, -1, 0),
        jnp.where(lanes == 0, low, roll(q, 1, 1)),
        jnp.where(lanes == LANES - 1, high, roll(q, -1, 1)),
    )


def refraction_rates(ext_ref, below, above, rate_ref):
    grads = []
    for c in range(2):
        xm, xp, ym, yp = neighbours(c, ext_ref[c, 0:8, :], below, above, 1)
        grads.append(((xp - xm) * 0.5, (yp - ym) * 0.5))
    (ux, uy), (vx, vy) = grads
    stretch = ux - vy
    for k in range(NDIR):
        c, s = float(COS[k]), float(SIN[k])
        rate_ref[k] = (TURN * c * s) * stretch + (TURN * s * s) * vx - (TURN * c * c) * uy


def advance_ocean(ext_ref, below, above, stress, wet8, out_ref):
    zonal, north, heat = (ext_ref[c] for c in range(3))
    wet = jnp.concatenate([wet8] * NZ, 0)

    def stencil(c, q):
        xm, xp, ym, yp = neighbours(c, q, below, above, NZ)
        return (xp - xm) * 0.5, (yp - ym) * 0.5, xp + xm + yp + ym - 4.0 * q

    _, _, zonal_lap = stencil(0, zonal)
    _, _, north_lap = stencil(1, north)
    heat_x, heat_y, heat_lap = stencil(2, heat)

    def running(v):
        total = v[0:8]
        sums = [total]
        for z in range(1, NZ):
            total = total + v[8 * z : 8 * z + 8]
            sums.append(total)
        return jnp.concatenate(sums, 0)

    rest = jnp.zeros((8 * (NZ - 1), LANES), F32)
    push_u = jnp.concatenate([stress[0:8], rest], 0)
    push_v = jnp.concatenate([stress[8:16], rest], 0)
    new = (
        wet * (zonal + CORIOLIS * north - PRESS * running(heat_x) + VISC * zonal_lap + push_u),
        wet * (north - CORIOLIS * zonal - PRESS * running(heat_y) + VISC * north_lap + push_v),
        heat + wet * (DIFFUSE * heat_lap - ADVECT * (zonal * heat_x + north * heat_y)),
    )
    for c in range(3):
        for z in range(NZ):
            out_ref[c, z] = new[c][8 * z + 1 : 8 * z + 5]
    return new


def stress_of(n_ref, weights_ref):
    total = jnp.zeros((16, LANES), F32)
    for x in range(ROWS):
        cells = n_ref[x].reshape(BINS, LANES).astype(BF16)
        total = total + jnp.dot(weights_ref[x], cells, preferred_element_type=F32)
    return total


def refraction(n_ref, rate_ref, x, k):
    below = jnp.where(k == 0, NDIR - 1, k - 1)
    above = jnp.where(k == NDIR - 1, 0, k + 1)
    rate = jnp.broadcast_to(rate_ref[k, pl.ds(x + 1, 1), :], (NF, LANES))
    upwind = jnp.where(rate > 0.0, n_ref[x, below], n_ref[x, above])
    return jnp.abs(rate) * (upwind - n_ref[x, k])


def inner_waves(n_ref, yh_ref, rate_ref, wet, tab_ref, shift_ref, ys_ref, acc_ref, keep):
    size = QUARTER * NF
    for quarter in range(4):
        step = 1 if quarter >= 2 else -1
        side = 1 if quarter in (1, 2) else 0
        first = quarter * QUARTER
        edges = yh_ref[side, 0:size, :] if quarter < 2 else yh_ref[side, size : 2 * size, :]
        blank = jnp.zeros((LANES - 32, 2 * LANES), BF16)
        for x in range(ROWS):
            cells = n_ref[x, first : first + QUARTER].reshape(size, LANES).astype(BF16)
            edge_rows = shift_ref[side, LANES + 32 * x : LANES + 32 * x + 32, :]
            moves = jnp.concatenate([shift_ref[side, 0:LANES, :], edge_rows, blank], 0)
            ys_ref[x] = jnp.dot(jnp.concatenate([cells, edges], 1), moves, preferred_element_type=F32)

        def body(j, carry, first=first, step=step):
            k = first + j
            weights = [tab_ref[t, k] for t in range(5)]
            at = pl.ds(pl.multiple_of(j * NF, NF), NF)
            cells = [n_ref[x, k] for x in range(ROWS)]
            for x in range(ROWS):
                total = cells[x] * weights[0]
                for weight, other in zip(weights[1:3], (x + step, x + 2 * step)):
                    if 0 <= other < ROWS:
                        total = total + cells[other] * weight
                near_y, far_y = ys_ref[x, at, 0:LANES], ys_ref[x, at, LANES : 2 * LANES]
                total = total + (near_y * weights[3] + far_y * weights[4])
                if x in (1, 2):
                    total = total + refraction(n_ref, rate_ref, x, k)
                    if 0 <= x + 2 * step < ROWS:
                        total = keep(total * wet[x])
                acc_ref[x, k] = total
            return carry

        lax.fori_loop(0, QUARTER, body, 0, unroll=QUARTER)


def wet_row(mask_ref, x):
    return jnp.broadcast_to(mask_ref[pl.ds(x, 1), :].astype(F32), (NF, LANES))


def finish_far_half(n_ref, acc_ref, rate_ref, mask_ref, side, keep):
    x = 3 * side
    wet = wet_row(mask_ref, x)
    first = HALF * (1 - side)

    def body(kk, carry):
        k = first + kk
        acc_ref[x, k] = keep(wet * (acc_ref[x, k] + refraction(n_ref, rate_ref, x, k)))
        return carry

    lax.fori_loop(0, HALF, body, 0, unroll=6)


def finish_near_half(n_ref, acc_ref, rate_ref, mask_ref, tab_ref, halo_ref, known, side, keep):
    x, inner = 3 * side, 1 + side
    wet, wet_inner = wet_row(mask_ref, x), wet_row(mask_ref, inner)
    first = HALF * side

    def body(kk, carry):
        k = first + kk
        near = halo_ref[pl.ds(pl.multiple_of(((1 - side) * HALF + kk) * NF, NF), NF), :].astype(F32)
        far = halo_ref[pl.ds(pl.multiple_of((side * HALF + kk) * NF, NF), NF), :].astype(F32)
        near, far = jnp.where(known, near, 0.0), jnp.where(known, far, 0.0)
        total = acc_ref[x, k] + (near * tab_ref[1, k] + far * tab_ref[2, k])
        acc_ref[x, k] = keep(wet * (total + refraction(n_ref, rate_ref, x, k)))
        acc_ref[inner, k] = keep(wet_inner * (acc_ref[inner, k] + near * tab_ref[2, k]))
        return carry

    lax.fori_loop(0, HALF, body, 0, unroll=6)


def rounded(v):
    return v.astype(BF16).astype(F32)


def exact(v):
    return v


def wet_rows(mask_ref):
    wet = mask_ref[...].astype(F32)
    pad = jnp.zeros((1, LANES), F32)
    wet8 = jnp.concatenate([pad, wet, pad, pad, pad], 0)
    return [jnp.broadcast_to(wet[x : x + 1], (NF, LANES)) for x in range(ROWS)], wet8


def inner_kernel(n_ref, o_ref, mask_ref, tab_ref, w_ref, shift_ref, ye_in, yo_in,
                 acc_ref, stress_ref, yh_ref, ext_ref, rate_ref, ys_ref):
    even_y = is_even("gy")
    wet, _ = wet_rows(mask_ref)
    y_spectra(even_y, ye_in, yo_in, yh_ref)
    below, above = y_ocean(even_y, ye_in, yo_in)
    unknown = jnp.zeros((OCEAN, LANES), F32)
    extend_ocean(o_ref, unknown, unknown, ext_ref, 1)
    refraction_rates(ext_ref, below, above, rate_ref)
    stress_ref[...] = stress_of(n_ref, w_ref)
    inner_waves(n_ref, yh_ref, rate_ref, wet, tab_ref, shift_ref, ys_ref, acc_ref, rounded)


def send_kernel(n_ref, acc_in, o_ref, mask_ref, stress_ref, xe_in, xo_in, ye_in, yo_in,
                acc_ref, ocean_ref, rate_ref, xo_ref, xrow_ref, ycol_ref, ext_ref):
    even_x, even_y = is_even("gx"), is_even("gy")
    below, above = y_ocean(even_y, ye_in, yo_in)
    left, right = x_ocean(even_x, xe_in, xo_in)
    extend_ocean(o_ref, left, right, ext_ref)
    refraction_rates(ext_ref, below, above, rate_ref)
    finish_far_half(n_ref, acc_ref, rate_ref, mask_ref, 1 - even_x.astype(jnp.int32), rounded)
    _, wet8 = wet_rows(mask_ref)
    new = advance_ocean(ext_ref, below, above, stress_ref[...], wet8, ocean_ref)
    rows = tuple(
        jnp.concatenate([new[c][8 * z + r : 8 * z + r + 1] for c in range(3) for z in range(NZ)], 0)
        for r in (1, ROWS)
    )
    send_x(acc_ref, rows, xo_ref, even_x)
    xo_ref[XROWS:, :] = jnp.zeros((16, LANES), BF16)
    xrow_ref[...] = jnp.where(even_x, rows[1], rows[0])
    ycol_ref[0], ycol_ref[1] = pack_ocean_columns(new, lane_of((8, LANES)))


def rest_kernel(n_ref, acc_in, mask_ref, tab_ref, rate_ref, edge_ref, xrow_ref, ycol_ref, xe_in, xo_in,
                acc_ref, xe_ref, ye_ref, yo_ref, e_ref):
    even_x, even_y = is_even("gx"), is_even("gy")
    side = even_x.astype(jnp.int32)
    finish_near_half(n_ref, acc_ref, rate_ref, mask_ref, tab_ref, xo_in, inside("gx"), 1 - side, rounded)
    finish_near_half(n_ref, acc_ref, rate_ref, mask_ref, tab_ref, xe_in, True, side, rounded)
    finish_far_half(n_ref, acc_ref, rate_ref, mask_ref, side, rounded)
    row = xrow_ref[...]
    send_x(acc_ref, (row, row), xe_ref, jnp.logical_not(even_x))
    for quarter in range(4):
        pack_y_edges(acc_ref, quarter, edge_ref, e_ref)
    send_y(e_ref, ycol_ref[0], ycol_ref[1], even_y, (ye_ref, yo_ref))


def write_rows(acc_ref, first, t_ref, block_ref, out_hbm, sems):
    copies = []
    for r in range(2):

        def body(k, carry, r=r):
            t_ref[r, pl.ds(k, NF, stride=NDIR), :] = acc_ref[first + r, k]
            return carry

        lax.fori_loop(0, NDIR, body, 0, unroll=6)
        block_ref[r] = jnp.transpose(t_ref[r]).astype(BF16)
        copies.append(pltpu.make_async_copy(block_ref.at[r], out_hbm.at[first + r], sems.at[r]))
        copies[-1].start()
    return copies


def wait_all(copies):
    for copy in copies:
        copy.wait()


def inner_last_kernel(n_ref, o_ref, mask_ref, tab_ref, w_ref, shift_ref, xe_in, ye_in, yo_in,
                      acc_ref, stress_ref, out_hbm,
                      yh_ref, ext_ref, rate_ref, ys_ref, t_ref, block_ref, sems):
    even_x, even_y = is_even("gx"), is_even("gy")
    wet, _ = wet_rows(mask_ref)
    y_spectra(even_y, ye_in, yo_in, yh_ref)
    below, above = y_ocean(even_y, ye_in, yo_in)
    left, right = x_ocean(even_x, xe_in, xe_in)
    extend_ocean(o_ref, left, right, ext_ref, 1)
    refraction_rates(ext_ref, below, above, rate_ref)
    inner_waves(n_ref, yh_ref, rate_ref, wet, tab_ref, shift_ref, ys_ref, acc_ref, exact)
    side = even_x.astype(jnp.int32)
    finish_near_half(n_ref, acc_ref, rate_ref, mask_ref, tab_ref, xe_in, True, side, exact)
    finish_far_half(n_ref, acc_ref, rate_ref, mask_ref, side, exact)
    copies = write_rows(acc_ref, 2 * side, t_ref, block_ref, out_hbm, sems)
    stress_ref[...] = stress_of(n_ref, w_ref)
    wait_all(copies)


def last_kernel(n_ref, acc_in, o_ref, mask_ref, tab_ref, stress_ref, xe_in, xo_in, ye_in, yo_in, out_in,
                acc_ref, ocean_ref, out_hbm, ext_ref, rate_ref, t_ref, block_ref, sems):
    even_x, even_y = is_even("gx"), is_even("gy")
    below, above = y_ocean(even_y, ye_in, yo_in)
    left, right = x_ocean(even_x, xe_in, xo_in)
    extend_ocean(o_ref, left, right, ext_ref)
    refraction_rates(ext_ref, below, above, rate_ref)
    side = 1 - even_x.astype(jnp.int32)
    finish_near_half(n_ref, acc_ref, rate_ref, mask_ref, tab_ref, xo_in, inside("gx"), side, exact)
    finish_far_half(n_ref, acc_ref, rate_ref, mask_ref, side, exact)
    copies = write_rows(acc_ref, 2 * side, t_ref, block_ref, out_hbm, sems)
    _, wet8 = wet_rows(mask_ref)
    advance_ocean(ext_ref, below, above, stress_ref[...], wet8, ocean_ref)
    wait_all(copies)


def swap(array, axis, odd):
    nx, ny = lax.axis_size("gx"), lax.axis_size("gy")
    pairs = []
    for i in range(nx):
        for j in range(ny):
            to = (i ^ 1, j) if axis == "gx" else (i, j ^ 1)
            if odd and axis == "gx":
                to = (((i + 1) ^ 1) - 1, j) if 0 < i < nx - 1 else (i, j ^ 1)
            if odd and axis == "gy":
                to = (i, ((j + 1) ^ 1) - 1) if 0 < j < ny - 1 else (i ^ 1, j)
            pairs.append((i * ny + j, to[0] * ny + to[1]))
    return lax.ppermute(array, ("gx", "gy"), pairs)


def call(kernel, outs, ins, scratch, params=None, any_in=(), any_out=(), aliases=None, moved=0):
    places = [HBM if i in any_in else VM for i in range(len(ins))]
    return pl.pallas_call(
        kernel,
        out_shape=[jax.ShapeDtypeStruct(shape, dtype) for shape, dtype in outs],
        in_specs=places,
        out_specs=[HBM if i in any_out else VM for i in range(len(outs))],
        scratch_shapes=scratch,
        compiler_params=params or PARAMS,
        input_output_aliases=aliases or {},
        cost_estimate=pl.CostEstimate(flops=0, bytes_accessed=moved * 1024 * 1024, transcendentals=0),
        name=kernel.__name__.removesuffix("_kernel"),
    )(*ins)


GRID = ((ROWS, NDIR, NF, LANES), F32)
XEDGE = ((XROWS, LANES), BF16)
XLONG = ((XROWS + 16, LANES), BF16)
YEDGE = ((YROWS, LANES), BF16)
DRIVE = ((16, LANES), F32)
RATES = ((NDIR, 8, LANES), F32)
YH = pltpu.VMEM((2, HALF * NF, LANES), BF16)
EXT = pltpu.VMEM((3, 8 * NZ, LANES), F32)
RATE = pltpu.VMEM(*RATES)
SHIFTED = pltpu.VMEM((ROWS, QUARTER * NF, 2 * LANES), F32)
EDGES = pltpu.VMEM((2, HALF, 8, LANES), F32)
TURNED = pltpu.VMEM((2, BINS, LANES), F32)
BLOCK = pltpu.VMEM((2, LANES, BINS), BF16)


def local(spectrum, ocean_state, sea_mask):
    ocean_shape = (ocean_state.shape, F32)
    weights = jnp.asarray(stress_table(), dtype=BF16)
    shift_table = jnp.asarray(shift_tables(), dtype=BF16)
    (xo,) = call(
        first_kernel,
        (XEDGE,),
        (spectrum, ocean_state, sea_mask),
        [
            pltpu.VMEM((2, *spectrum.shape[1:]), BF16),
            pltpu.VMEM(ocean_state.shape, F32),
            pltpu.VMEM(sea_mask.shape, jnp.int32),
            TURNED,
            pltpu.SemaphoreType.DMA((4,)),
        ],
        FIRST,
        any_in=(0, 1, 2),
        moved=32,
    )
    xo = swap(xo, "gx", 1)
    n, xe, ye, yo, tab, edge_table = call(
        start_kernel,
        (GRID, XEDGE, YEDGE, YEDGE, ((5, NDIR, NF, LANES), F32), ((2, ROWS * LANES, LANES), BF16)),
        (spectrum, ocean_state, sea_mask),
        [pltpu.VMEM((ROWS, BINS, LANES), F32), EDGES],
    )
    xe = swap(xe, "gx", 0)
    ye = swap(ye, "gy", 0)
    yo = swap(yo, "gy", 1)
    acc, stress = call(
        inner_kernel,
        (GRID, DRIVE),
        (n, ocean_state, sea_mask, tab, weights, shift_table, ye, yo),
        [YH, EXT, RATE, SHIFTED],
    )
    acc, ocean, rate, xo2, xrow, ycol = call(
        send_kernel,
        (GRID, ocean_shape, RATES, XLONG, ((OCEAN, LANES), F32), ((2, 8, LANES), F32)),
        (n, acc, ocean_state, sea_mask, stress, xe, xo, ye, yo),
        [EXT],
        aliases={1: 0},
    )
    xo2 = swap(xo2, "gx", 1)
    n, xe, ye, yo = call(
        rest_kernel,
        (GRID, XEDGE, YEDGE, YEDGE),
        (n, acc, sea_mask, tab, rate, edge_table, xrow, ycol, xe, xo),
        [EDGES],
        aliases={1: 0},
    )
    xe = swap(xe, "gx", 0)
    ye = swap(ye, "gy", 0)
    yo = swap(yo, "gy", 1)
    acc, stress, out = call(
        inner_last_kernel,
        (GRID, DRIVE, (spectrum.shape, BF16)),
        (n, ocean, sea_mask, tab, weights, shift_table, xe, ye, yo),
        [YH, EXT, RATE, SHIFTED, TURNED, BLOCK, pltpu.SemaphoreType.DMA((2,))],
        any_out=(2,),
    )
    _, ocean, out = call(
        last_kernel,
        (GRID, ocean_shape, (spectrum.shape, BF16)),
        (n, acc, ocean, sea_mask, tab, stress, xe, xo2, ye, yo, out),
        [EXT, RATE, TURNED, BLOCK, pltpu.SemaphoreType.DMA((2,))],
        any_in=(10,),
        any_out=(2,),
        aliases={1: 0, 10: 2},
    )
    return out, ocean


def solution(mesh):
    placed = (P("gx", "gy", None), P(None, None, "gx", "gy"), P("gx", "gy"))
    return jax.shard_map(
        local,
        mesh=mesh,
        in_specs=placed,
        out_specs=(P("gx", "gy", None), P(None, None, "gx", "gy")),
        check_vma=False,
    )
```

```python
import math

import jax
import jax.numpy as jnp
import numpy as np
from jax import lax
from jax.experimental import pallas as pl
from jax.experimental.pallas import tpu as pltpu
from jax.sharding import PartitionSpec as P

NF = 32
NDIR = 36
NZ = 16
HALF = NDIR // 2
QUARTER = NDIR // 4
ROWS = 4
LANES = 128
BINS = NF * NDIR

COURANT = 0.4
RATIO = 0.93
TURN = 0.1
STRESS = 0.1
CORIOLIS = 0.2
PRESS = 0.1
VISC = 0.15
ADVECT = 0.5
DIFFUSE = 0.15

F32 = jnp.float32
BF16 = jnp.bfloat16
VM = pl.BlockSpec(memory_space=pltpu.VMEM)
HBM = pl.BlockSpec(memory_space=pl.ANY)
FIRST = pltpu.CompilerParams(vmem_limit_bytes=56 * 1024 * 1024)
PARAMS = pltpu.CompilerParams(vmem_limit_bytes=16 * 1024 * 1024)

SPECTRA = 2 * HALF * NF
OCEAN = 3 * NZ
XROWS = SPECTRA + 2 * OCEAN
YROWS = HALF * 8 + 16

ANGLES = -0.5 * math.pi + (np.arange(NDIR, dtype=np.float32) + np.float32(0.5)) * np.float32(
    2.0 * math.pi / NDIR
)
COS = np.cos(ANGLES).astype(np.float32)
SIN = np.sin(ANGLES).astype(np.float32)
SPEEDS = (COURANT * RATIO ** np.arange(NF, dtype=np.float64)).astype(np.float32)


def stress_table():
    table = np.zeros((ROWS, 16, NDIR, NF), np.float32)
    for c, part in enumerate((COS, SIN)):
        weights = np.float32(STRESS) * SPEEDS[None, :] * part[:, None]
        for x in range(ROWS):
            table[x, c * 8 + 1 + x] = weights
    return table.reshape(ROWS, 16, BINS)


def is_even(axis):
    return lax.rem(lax.axis_index(axis), 2) == 0


def inside(axis):
    i = lax.axis_index(axis)
    return jnp.logical_and(i > 0, i < lax.axis_size(axis) - 1)


def split(v):
    high = v.astype(BF16).astype(F32)
    return high, v - high


def roll(v, shift, axis):
    return pltpu.roll(v, shift % v.shape[axis], axis)


def lane_of(shape):
    return lax.broadcasted_iota(jnp.int32, shape, len(shape) - 1)


def make_edge_tables(table_ref):
    source = lax.broadcasted_iota(jnp.int32, (LANES, LANES), 0)
    lane = lane_of((LANES, LANES)) % 8
    for side, start in enumerate((0, LANES - 2)):
        for x in range(ROWS):
            found = (lane == source + (2 * x - start)) & (lane >= 2 * x) & (lane < 2 * x + 2)
            table_ref[side, LANES * x : LANES * (x + 1), :] = jnp.where(found, 1.0, 0.0).astype(BF16)


def shift_tables():
    table = np.zeros((2, 2 * LANES, 2 * LANES), np.float32)
    for side, sign in enumerate((1, -1)):
        for far in range(2):
            for lane in range(LANES):
                source = lane + sign * (1 + far)
                if 0 <= source < LANES:
                    table[side, source, far * LANES + lane] = 1.0
                else:
                    j = source - LANES if sign > 0 else source + 2
                    for x in range(ROWS):
                        for g in range(4):
                            table[side, LANES + 32 * x + 8 * g + 2 * x + j, far * LANES + lane] = 1.0
    return table


def pack_y_edges(n_ref, quarter, tables_ref, out_ref):
    south = quarter in (1, 2)
    first = quarter * QUARTER
    rows = [
        n_ref[x, first : first + QUARTER].reshape(QUARTER * NF, LANES).astype(BF16) for x in range(ROWS)
    ]
    found = jnp.dot(
        jnp.concatenate(rows, 1), tables_ref[1 if south else 0], preferred_element_type=F32
    ).reshape(QUARTER, 4, 8, LANES)
    group = lane_of((QUARTER, 8, LANES)) // 8
    packed = found[:, 0]
    for g in range(1, 4):
        packed = jnp.where(group == g, found[:, g], packed)
    at = 0 if quarter < 2 else QUARTER
    out_ref[1 if south else 0, at : at + QUARTER] = packed


def pack_ocean_columns(blocks, lanes):
    first = jnp.zeros((8, LANES), F32)
    last = jnp.zeros((8, LANES), F32)
    for c in range(3):
        for z in range(NZ):
            block = blocks[c][8 * z : 8 * z + 8]
            at = c * NZ + z
            first = jnp.where(lanes == at, roll(block, at, 1), first)
            last = jnp.where(lanes == at, roll(block, at - (LANES - 1), 1), last)
    return first, last


def send_x(n_ref, ocean_rows, mine_ref, low_side):
    row = jnp.where(low_side, 0, 2)
    first = jnp.where(low_side, HALF, 0)
    edge = n_ref[pl.ds(row, 2), pl.ds(first, HALF)]
    mine_ref[0:SPECTRA, :] = edge.reshape(SPECTRA, LANES).astype(BF16)
    send_ocean_row(ocean_rows, mine_ref, low_side)


def send_ocean_row(ocean_rows, mine_ref, low_side):
    low, high = ocean_rows
    whole, rest = split(jnp.where(low_side, low, high))
    mine_ref[SPECTRA : SPECTRA + OCEAN, :] = whole.astype(BF16)
    mine_ref[SPECTRA + OCEAN : XROWS, :] = rest.astype(BF16)


def send_y(edges_ref, first, last, even, outs):
    for slot, out_ref in enumerate(outs):
        takes_last = even if slot == 0 else jnp.logical_not(even)
        which = takes_last.astype(jnp.int32)
        out_ref[0 : HALF * 8, :] = edges_ref[which].reshape(HALF * 8, LANES).astype(BF16)
        whole, rest = split(jnp.where(takes_last, last, first))
        out_ref[HALF * 8 : YROWS, :] = jnp.concatenate([whole, rest], 0).astype(BF16)


def first_kernel(s_hbm, o_hbm, mask_hbm, xo_ref, s_ref, o_ref, mask_ref, t_ref, sems):
    low_side = is_even("gx")
    row = jnp.where(low_side, 0, 2)
    first = jnp.where(low_side, HALF, 0)
    copies = [pltpu.make_async_copy(s_hbm.at[row + r], s_ref.at[r], sems.at[r]) for r in range(2)]
    copies.append(pltpu.make_async_copy(mask_hbm, mask_ref, sems.at[2]))
    copies.append(pltpu.make_async_copy(o_hbm, o_ref, sems.at[3]))
    for copy in copies:
        copy.start()
    copies[2].wait()
    for r in range(2):
        copies[r].wait()
        t_ref[r] = jnp.transpose(s_ref[r].astype(F32))
        wet = mask_ref[pl.ds(row + r, 1), :].astype(F32)

        def body(kk, carry, r=r, wet=wet):
            at = pl.ds(pl.multiple_of((r * HALF + kk) * NF, NF), NF)
            xo_ref[at, :] = (t_ref[r, pl.ds(first + kk, NF, stride=NDIR), :] * wet).astype(BF16)
            return carry

        lax.fori_loop(0, HALF, body, 0, unroll=6)
    copies[3].wait()
    rows = tuple(o_ref[:, :, r, :].reshape(OCEAN, LANES) for r in (0, ROWS - 1))
    send_ocean_row(rows, xo_ref, low_side)


def prepare_kernel(n_ref, w_ref, stress_ref, tab_ref):
    make_tables(tab_ref)
    stress_ref[...] = stress_of(n_ref, w_ref)


def start_kernel(s_ref, o_ref, mask_ref,
                 n_ref, xe_ref, ye_ref, yo_ref, edge_ref, t_ref, e_ref):
    wet = mask_ref[...].astype(F32)
    for x in range(ROWS):
        t_ref[x] = jnp.transpose(s_ref[x].astype(F32))

    def body(k, carry):
        for x in range(ROWS):
            n_ref[x, k] = t_ref[x, pl.ds(k, NF, stride=NDIR), :] * wet[x : x + 1]
        return carry

    lax.fori_loop(0, NDIR, body, 0, unroll=6)
    even_x, even_y = is_even("gx"), is_even("gy")
    rows = tuple(o_ref[:, :, r, :].reshape(OCEAN, LANES) for r in (0, ROWS - 1))
    send_x(n_ref, rows, xe_ref, jnp.logical_not(even_x))
    make_edge_tables(edge_ref)
    for quarter in range(4):
        pack_y_edges(n_ref, quarter, edge_ref, e_ref)
    pad = jnp.zeros((1, LANES), F32)
    blocks = [
        jnp.concatenate(
            [part for z in range(NZ) for part in (pad, o_ref[c, z], pad, pad, pad)], 0
        )
        for c in range(3)
    ]
    first, last = pack_ocean_columns(blocks, lane_of((8, LANES)))
    send_y(e_ref, first, last, even_y, (ye_ref, yo_ref))


def make_tables(tab_ref):
    row = lax.broadcasted_iota(jnp.int32, (8, LANES), 0)
    blocks = []
    for g in range(4):
        block = jnp.full((8, LANES), float(SPEEDS[8 * g]), F32)
        for i in range(1, 8):
            block = jnp.where(row == i, float(SPEEDS[8 * g + i]), block)
        blocks.append(block)
    speed = jnp.concatenate(blocks, 0)
    for k in range(NDIR):
        cx, cy = speed * abs(float(COS[k])), speed * abs(float(SIN[k]))
        near_x, far_x = cx * (2.0 - cx), (0.5 * cx) * (cx - 1.0)
        near_y, far_y = cy * (2.0 - cy), (0.5 * cy) * (cy - 1.0)
        tab_ref[0, k] = 1.0 - ((near_x + far_x) + (near_y + far_y))
        tab_ref[1, k] = near_x
        tab_ref[2, k] = far_x
        tab_ref[3, k] = near_y
        tab_ref[4, k] = far_y


def y_spectra(even_y, ye_ref, yo_ref, yh_ref):
    shape = (HALF, 8, LANES)
    a = ye_ref[0 : HALF * 8, :].astype(F32)
    b = jnp.where(inside("gy"), yo_ref[0 : HALF * 8, :].astype(F32), 0.0)
    group = lane_of(shape) // 8
    for to, pair in ((0, (a, b)), (1, (b, a))):
        edge = jnp.where(even_y, *pair).reshape(shape)
        parts = [jnp.where(group == g, edge, 0.0)[:, None] for g in range(4)]
        yh_ref[to] = jnp.concatenate(parts, 1).reshape(HALF * NF, LANES).astype(BF16)


def y_ocean(even_y, ye_ref, yo_ref):
    def columns(ref):
        both = ref[HALF * 8 : YROWS, :].astype(F32)
        return both[0:8] + both[8:16]

    a, b = columns(ye_ref), jnp.where(inside("gy"), columns(yo_ref), 0.0)
    return jnp.where(even_y, b, a), jnp.where(even_y, a, b)


def x_ocean(even_x, xe_ref, xo_ref):
    def rows(ref):
        return ref[SPECTRA : SPECTRA + OCEAN, :].astype(F32) + ref[SPECTRA + OCEAN : XROWS, :].astype(F32)

    a, b = rows(xe_ref), jnp.where(inside("gx"), rows(xo_ref), 0.0)
    return jnp.where(even_x, b, a), jnp.where(even_x, a, b)


def extend_ocean(o_ref, left, right, ext_ref, levels=NZ):
    for c in range(3):
        for z in range(levels):
            at = c * NZ + z
            ext_ref[c, 8 * z : 8 * z + 1, :] = left[at : at + 1]
            ext_ref[c, 8 * z + 1 : 8 * z + 5, :] = o_ref[c, z]
            ext_ref[c, 8 * z + 5 : 8 * z + 6, :] = right[at : at + 1]
            ext_ref[c, 8 * z + 6 : 8 * z + 8, :] = jnp.zeros((2, LANES), F32)


def neighbours(c, q, below, above, levels):
    lanes = lane_of(q.shape)
    low = jnp.concatenate([roll(below, -(c * NZ + z), 1) for z in range(levels)], 0)
    high = jnp.concatenate([roll(above, LANES - 1 - (c * NZ + z), 1) for z in range(levels)], 0)
    return (
        roll(q, 1, 0),
        roll(q, -1, 0),
        jnp.where(lanes == 0, low, roll(q, 1, 1)),
        jnp.where(lanes == LANES - 1, high, roll(q, -1, 1)),
    )


def refraction_rates(ext_ref, below, above, rate_ref):
    grads = []
    for c in range(2):
        xm, xp, ym, yp = neighbours(c, ext_ref[c, 0:8, :], below, above, 1)
        grads.append(((xp - xm) * 0.5, (yp - ym) * 0.5))
    (ux, uy), (vx, vy) = grads
    stretch = ux - vy
    for k in range(NDIR):
        c, s = float(COS[k]), float(SIN[k])
        rate_ref[k] = (TURN * c * s) * stretch + (TURN * s * s) * vx - (TURN * c * c) * uy


def advance_ocean(ext_ref, below, above, stress, wet8, out_ref):
    zonal, north, heat = (ext_ref[c] for c in range(3))
    wet = jnp.concatenate([wet8] * NZ, 0)

    def stencil(c, q):
        xm, xp, ym, yp = neighbours(c, q, below, above, NZ)
        return (xp - xm) * 0.5, (yp - ym) * 0.5, xp + xm + yp + ym - 4.0 * q

    _, _, zonal_lap = stencil(0, zonal)
    _, _, north_lap = stencil(1, north)
    heat_x, heat_y, heat_lap = stencil(2, heat)

    def running(v):
        total = v[0:8]
        sums = [total]
        for z in range(1, NZ):
            total = total + v[8 * z : 8 * z + 8]
            sums.append(total)
        return jnp.concatenate(sums, 0)

    rest = jnp.zeros((8 * (NZ - 1), LANES), F32)
    push_u = jnp.concatenate([stress[0:8], rest], 0)
    push_v = jnp.concatenate([stress[8:16], rest], 0)
    new = (
        wet * (zonal + CORIOLIS * north - PRESS * running(heat_x) + VISC * zonal_lap + push_u),
        wet * (north - CORIOLIS * zonal - PRESS * running(heat_y) + VISC * north_lap + push_v),
        heat + wet * (DIFFUSE * heat_lap - ADVECT * (zonal * heat_x + north * heat_y)),
    )
    for c in range(3):
        for z in range(NZ):
            out_ref[c, z] = new[c][8 * z + 1 : 8 * z + 5]
    return new


def stress_of(n_ref, weights_ref):
    total = jnp.zeros((16, LANES), F32)
    for x in range(ROWS):
        cells = n_ref[x].reshape(BINS, LANES).astype(BF16)
        total = total + jnp.dot(weights_ref[x], cells, preferred_element_type=F32)
    return total


def refraction(n_ref, rate_ref, x, k):
    below = jnp.where(k == 0, NDIR - 1, k - 1)
    above = jnp.where(k == NDIR - 1, 0, k + 1)
    rate = jnp.broadcast_to(rate_ref[k, pl.ds(x + 1, 1), :], (NF, LANES))
    upwind = jnp.where(rate > 0.0, n_ref[x, below], n_ref[x, above])
    return jnp.abs(rate) * (upwind - n_ref[x, k])


def cell_of(acc_ref, x, k):
    if len(acc_ref.shape) == 4:
        return x, k
    return x, pl.ds(k, NF, stride=NDIR), slice(None)


def inner_waves(n_ref, yh_ref, rate_ref, wet, tab_ref, shift_ref, ys_ref, acc_ref, keep):
    size = QUARTER * NF
    for quarter in range(4):
        step = 1 if quarter >= 2 else -1
        side = 1 if quarter in (1, 2) else 0
        first = quarter * QUARTER
        edges = yh_ref[side, 0:size, :] if quarter < 2 else yh_ref[side, size : 2 * size, :]
        blank = jnp.zeros((LANES - 32, 2 * LANES), BF16)
        for x in range(ROWS):
            cells = n_ref[x, first : first + QUARTER].reshape(size, LANES).astype(BF16)
            edge_rows = shift_ref[side, LANES + 32 * x : LANES + 32 * x + 32, :]
            moves = jnp.concatenate([shift_ref[side, 0:LANES, :], edge_rows, blank], 0)
            ys_ref[x] = jnp.dot(jnp.concatenate([cells, edges], 1), moves, preferred_element_type=F32)

        def body(j, carry, first=first, step=step):
            k = first + j
            weights = [tab_ref[t, k] for t in range(5)]
            at = pl.ds(pl.multiple_of(j * NF, NF), NF)
            cells = [n_ref[x, k] for x in range(ROWS)]
            for x in range(ROWS):
                total = cells[x] * weights[0]
                for weight, other in zip(weights[1:3], (x + step, x + 2 * step)):
                    if 0 <= other < ROWS:
                        total = total + cells[other] * weight
                near_y, far_y = ys_ref[x, at, 0:LANES], ys_ref[x, at, LANES : 2 * LANES]
                total = total + (near_y * weights[3] + far_y * weights[4])
                if x in (1, 2):
                    total = total + refraction(n_ref, rate_ref, x, k)
                    if 0 <= x + 2 * step < ROWS:
                        total = keep(total * wet[x])
                acc_ref[cell_of(acc_ref, x, k)] = total
            return carry

        lax.fori_loop(0, QUARTER, body, 0, unroll=QUARTER)


def wet_row(mask_ref, x):
    return jnp.broadcast_to(mask_ref[pl.ds(x, 1), :].astype(F32), (NF, LANES))


def finish_far_half(n_ref, acc_ref, rate_ref, mask_ref, side, keep):
    x = 3 * side
    wet = wet_row(mask_ref, x)
    first = HALF * (1 - side)

    def body(kk, carry):
        k = first + kk
        cell = cell_of(acc_ref, x, k)
        acc_ref[cell] = keep(wet * (acc_ref[cell] + refraction(n_ref, rate_ref, x, k)))
        return carry

    lax.fori_loop(0, HALF, body, 0, unroll=6)


def finish_near_half(n_ref, acc_ref, rate_ref, mask_ref, tab_ref, halo_ref, known, side, keep):
    x, inner = 3 * side, 1 + side
    wet, wet_inner = wet_row(mask_ref, x), wet_row(mask_ref, inner)
    first = HALF * side

    def body(kk, carry):
        k = first + kk
        near = halo_ref[pl.ds(pl.multiple_of(((1 - side) * HALF + kk) * NF, NF), NF), :].astype(F32)
        far = halo_ref[pl.ds(pl.multiple_of((side * HALF + kk) * NF, NF), NF), :].astype(F32)
        near, far = jnp.where(known, near, 0.0), jnp.where(known, far, 0.0)
        cell, inner_cell = cell_of(acc_ref, x, k), cell_of(acc_ref, inner, k)
        total = acc_ref[cell] + (near * tab_ref[1, k] + far * tab_ref[2, k])
        acc_ref[cell] = keep(wet * (total + refraction(n_ref, rate_ref, x, k)))
        acc_ref[inner_cell] = keep(wet_inner * (acc_ref[inner_cell] + near * tab_ref[2, k]))
        return carry

    lax.fori_loop(0, HALF, body, 0, unroll=6)


def rounded(v):
    return v.astype(BF16).astype(F32)


def exact(v):
    return v


def wet_rows(mask_ref):
    wet = mask_ref[...].astype(F32)
    pad = jnp.zeros((1, LANES), F32)
    wet8 = jnp.concatenate([pad, wet, pad, pad, pad], 0)
    return [jnp.broadcast_to(wet[x : x + 1], (NF, LANES)) for x in range(ROWS)], wet8


def inner_kernel(n_ref, o_ref, mask_ref, tab_ref, shift_ref, ye_in, yo_in,
                 acc_ref, yh_ref, ext_ref, rate_ref, ys_ref):
    even_y = is_even("gy")
    wet, _ = wet_rows(mask_ref)
    y_spectra(even_y, ye_in, yo_in, yh_ref)
    below, above = y_ocean(even_y, ye_in, yo_in)
    unknown = jnp.zeros((OCEAN, LANES), F32)
    extend_ocean(o_ref, unknown, unknown, ext_ref, 1)
    refraction_rates(ext_ref, below, above, rate_ref)
    inner_waves(n_ref, yh_ref, rate_ref, wet, tab_ref, shift_ref, ys_ref, acc_ref, rounded)


def send_kernel(n_ref, acc_in, o_ref, mask_ref, stress_ref, xe_in, xo_in, ye_in, yo_in,
                acc_ref, ocean_ref, rate_ref, xo_ref, xrow_ref, ycol_ref, ext_ref):
    even_x, even_y = is_even("gx"), is_even("gy")
    below, above = y_ocean(even_y, ye_in, yo_in)
    left, right = x_ocean(even_x, xe_in, xo_in)
    extend_ocean(o_ref, left, right, ext_ref)
    refraction_rates(ext_ref, below, above, rate_ref)
    finish_far_half(n_ref, acc_ref, rate_ref, mask_ref, 1 - even_x.astype(jnp.int32), rounded)
    _, wet8 = wet_rows(mask_ref)
    new = advance_ocean(ext_ref, below, above, stress_ref[...], wet8, ocean_ref)
    rows = tuple(
        jnp.concatenate([new[c][8 * z + r : 8 * z + r + 1] for c in range(3) for z in range(NZ)], 0)
        for r in (1, ROWS)
    )
    send_x(acc_ref, rows, xo_ref, even_x)
    xo_ref[XROWS:, :] = jnp.zeros((16, LANES), BF16)
    xrow_ref[...] = jnp.where(even_x, rows[1], rows[0])
    ycol_ref[0], ycol_ref[1] = pack_ocean_columns(new, lane_of((8, LANES)))


def rest_kernel(n_ref, acc_in, mask_ref, tab_ref, rate_ref, edge_ref, xrow_ref, ycol_ref, xe_in, xo_in,
                acc_ref, xe_ref, ye_ref, yo_ref, e_ref):
    even_x, even_y = is_even("gx"), is_even("gy")
    side = even_x.astype(jnp.int32)
    finish_near_half(n_ref, acc_ref, rate_ref, mask_ref, tab_ref, xo_in, inside("gx"), 1 - side, rounded)
    finish_near_half(n_ref, acc_ref, rate_ref, mask_ref, tab_ref, xe_in, True, side, rounded)
    finish_far_half(n_ref, acc_ref, rate_ref, mask_ref, side, rounded)
    row = xrow_ref[...]
    send_x(acc_ref, (row, row), xe_ref, jnp.logical_not(even_x))
    for quarter in range(4):
        pack_y_edges(acc_ref, quarter, edge_ref, e_ref)
    send_y(e_ref, ycol_ref[0], ycol_ref[1], even_y, (ye_ref, yo_ref))


def inner_last_kernel(n_ref, o_ref, mask_ref, tab_ref, w_ref, shift_ref, xe_in, ye_in, yo_in,
                      acc_ref, stress_ref, done_ref,
                      yh_ref, ext_ref, rate_ref, ys_ref):
    even_x, even_y = is_even("gx"), is_even("gy")
    wet, _ = wet_rows(mask_ref)
    y_spectra(even_y, ye_in, yo_in, yh_ref)
    below, above = y_ocean(even_y, ye_in, yo_in)
    left, right = x_ocean(even_x, xe_in, xe_in)
    extend_ocean(o_ref, left, right, ext_ref, 1)
    refraction_rates(ext_ref, below, above, rate_ref)
    stress_ref[...] = stress_of(n_ref, w_ref)
    inner_waves(n_ref, yh_ref, rate_ref, wet, tab_ref, shift_ref, ys_ref, acc_ref, exact)
    side = even_x.astype(jnp.int32)
    finish_near_half(n_ref, acc_ref, rate_ref, mask_ref, tab_ref, xe_in, True, side, exact)
    finish_far_half(n_ref, acc_ref, rate_ref, mask_ref, side, exact)
    for r in range(2):
        done_ref[r] = jnp.transpose(acc_ref[2 * side + r]).astype(BF16)


def last_kernel(n_ref, acc_in, done_ref, o_ref, mask_ref, tab_ref, stress_ref, xe_in, xo_in, ye_in, yo_in,
                acc_ref, ocean_ref, out_hbm, ext_ref, rate_ref, block_ref, sems):
    even_x, even_y = is_even("gx"), is_even("gy")
    side = 1 - even_x.astype(jnp.int32)
    done = pltpu.make_async_copy(done_ref, out_hbm.at[pl.ds(2 * (1 - side), 2)], sems.at[0])
    done.start()
    below, above = y_ocean(even_y, ye_in, yo_in)
    left, right = x_ocean(even_x, xe_in, xo_in)
    extend_ocean(o_ref, left, right, ext_ref, 1)
    refraction_rates(ext_ref, below, above, rate_ref)
    finish_near_half(n_ref, acc_ref, rate_ref, mask_ref, tab_ref, xo_in, inside("gx"), side, exact)
    finish_far_half(n_ref, acc_ref, rate_ref, mask_ref, side, exact)
    copies = [done]
    for r in range(2):
        block_ref[r] = jnp.transpose(acc_ref[2 * side + r]).astype(BF16)
        copies.append(pltpu.make_async_copy(block_ref.at[r], out_hbm.at[2 * side + r], sems.at[1 + r]))
        copies[-1].start()
    _, wet8 = wet_rows(mask_ref)
    extend_ocean(o_ref, left, right, ext_ref)
    advance_ocean(ext_ref, below, above, stress_ref[...], wet8, ocean_ref)
    for copy in copies:
        copy.wait()


def swap(array, axis, odd):
    nx, ny = lax.axis_size("gx"), lax.axis_size("gy")
    pairs = []
    for i in range(nx):
        for j in range(ny):
            to = (i ^ 1, j) if axis == "gx" else (i, j ^ 1)
            if odd and axis == "gx":
                to = (((i + 1) ^ 1) - 1, j) if 0 < i < nx - 1 else (i, j ^ 1)
            if odd and axis == "gy":
                to = (i, ((j + 1) ^ 1) - 1) if 0 < j < ny - 1 else (i ^ 1, j)
            pairs.append((i * ny + j, to[0] * ny + to[1]))
    return lax.ppermute(array, ("gx", "gy"), pairs)


def call(kernel, outs, ins, scratch, params=None, any_in=(), any_out=(), aliases=None, moved=0):
    places = [HBM if i in any_in else VM for i in range(len(ins))]
    return pl.pallas_call(
        kernel,
        out_shape=[jax.ShapeDtypeStruct(shape, dtype) for shape, dtype in outs],
        in_specs=places,
        out_specs=[HBM if i in any_out else VM for i in range(len(outs))],
        scratch_shapes=scratch,
        compiler_params=params or PARAMS,
        input_output_aliases=aliases or {},
        cost_estimate=pl.CostEstimate(flops=0, bytes_accessed=moved * 1024 * 1024, transcendentals=0),
        name=kernel.__name__.removesuffix("_kernel"),
    )(*ins)


BINNED = ((ROWS, BINS, LANES), F32)
GRID = ((ROWS, NDIR, NF, LANES), F32)
XEDGE = ((XROWS, LANES), BF16)
XLONG = ((XROWS + 16, LANES), BF16)
YEDGE = ((YROWS, LANES), BF16)
DRIVE = ((16, LANES), F32)
RATES = ((NDIR, 8, LANES), F32)
YH = pltpu.VMEM((2, HALF * NF, LANES), BF16)
EXT = pltpu.VMEM((3, 8 * NZ, LANES), F32)
RATE = pltpu.VMEM(*RATES)
SHIFTED = pltpu.VMEM((ROWS, QUARTER * NF, 2 * LANES), F32)
EDGES = pltpu.VMEM((2, HALF, 8, LANES), F32)
TURNED = pltpu.VMEM((2, BINS, LANES), F32)
BLOCK = pltpu.VMEM((2, LANES, BINS), BF16)


def local(spectrum, ocean_state, sea_mask):
    ocean_shape = (ocean_state.shape, F32)
    weights = jnp.asarray(stress_table(), dtype=BF16)
    shift_table = jnp.asarray(shift_tables(), dtype=BF16)
    (xo,) = call(
        first_kernel,
        (XEDGE,),
        (spectrum, ocean_state, sea_mask),
        [
            pltpu.VMEM((2, *spectrum.shape[1:]), BF16),
            pltpu.VMEM(ocean_state.shape, F32),
            pltpu.VMEM(sea_mask.shape, jnp.int32),
            TURNED,
            pltpu.SemaphoreType.DMA((4,)),
        ],
        FIRST,
        any_in=(0, 1, 2),
        moved=32,
    )
    xo = swap(xo, "gx", 1)
    n, xe, ye, yo, edge_table = call(
        start_kernel,
        (GRID, XEDGE, YEDGE, YEDGE, ((2, ROWS * LANES, LANES), BF16)),
        (spectrum, ocean_state, sea_mask),
        [pltpu.VMEM((ROWS, BINS, LANES), F32), EDGES],
    )
    xe = swap(xe, "gx", 0)
    ye = swap(ye, "gy", 0)
    yo = swap(yo, "gy", 1)
    stress, tab = call(prepare_kernel, (DRIVE, ((5, NDIR, NF, LANES), F32)), (n, weights), [])
    (acc,) = call(
        inner_kernel,
        (GRID,),
        (n, ocean_state, sea_mask, tab, shift_table, ye, yo),
        [YH, EXT, RATE, SHIFTED],
    )
    acc, ocean, rate, xo2, xrow, ycol = call(
        send_kernel,
        (GRID, ocean_shape, RATES, XLONG, ((OCEAN, LANES), F32), ((2, 8, LANES), F32)),
        (n, acc, ocean_state, sea_mask, stress, xe, xo, ye, yo),
        [EXT],
        aliases={1: 0},
    )
    xo2 = swap(xo2, "gx", 1)
    n, xe, ye, yo = call(
        rest_kernel,
        (GRID, XEDGE, YEDGE, YEDGE),
        (n, acc, sea_mask, tab, rate, edge_table, xrow, ycol, xe, xo),
        [EDGES],
        aliases={1: 0},
    )
    xe = swap(xe, "gx", 0)
    ye = swap(ye, "gy", 0)
    yo = swap(yo, "gy", 1)
    acc, stress, done = call(
        inner_last_kernel,
        (BINNED, DRIVE, ((2, *spectrum.shape[1:]), BF16)),
        (n, ocean, sea_mask, tab, weights, shift_table, xe, ye, yo),
        [YH, EXT, RATE, SHIFTED],
    )
    _, ocean, out = call(
        last_kernel,
        (BINNED, ocean_shape, (spectrum.shape, BF16)),
        (n, acc, done, ocean, sea_mask, tab, stress, xe, xo2, ye, yo),
        [EXT, RATE, BLOCK, pltpu.SemaphoreType.DMA((3,))],
        any_out=(2,),
        aliases={1: 0},
    )
    return out, ocean


def solution(mesh):
    placed = (P("gx", "gy", None), P(None, None, "gx", "gy"), P("gx", "gy"))
    return jax.shard_map(
        local,
        mesh=mesh,
        in_specs=placed,
        out_specs=(P("gx", "gy", None), P(None, None, "gx", "gy")),
        check_vma=False,
    )
```

```python
import math

import jax
import jax.numpy as jnp
import numpy as np
from jax import lax
from jax.experimental import pallas as pl
from jax.experimental.pallas import tpu as pltpu
from jax.sharding import PartitionSpec as P

NF = 32
NDIR = 36
NZ = 16
HALF = NDIR // 2
QUARTER = NDIR // 4
ROWS = 4
LANES = 128
BINS = NF * NDIR

COURANT = 0.4
RATIO = 0.93
TURN = 0.1
STRESS = 0.1
CORIOLIS = 0.2
PRESS = 0.1
VISC = 0.15
ADVECT = 0.5
DIFFUSE = 0.15

F32 = jnp.float32
BF16 = jnp.bfloat16
VM = pl.BlockSpec(memory_space=pltpu.VMEM)
HBM = pl.BlockSpec(memory_space=pl.ANY)
FIRST = pltpu.CompilerParams(vmem_limit_bytes=56 * 1024 * 1024)
PARAMS = pltpu.CompilerParams(vmem_limit_bytes=16 * 1024 * 1024)

SPECTRA = 2 * HALF * NF
OCEAN = 3 * NZ
XROWS = SPECTRA + 2 * OCEAN
YROWS = HALF * 8 + 16

ANGLES = -0.5 * math.pi + (np.arange(NDIR, dtype=np.float32) + np.float32(0.5)) * np.float32(
    2.0 * math.pi / NDIR
)
COS = np.cos(ANGLES).astype(np.float32)
SIN = np.sin(ANGLES).astype(np.float32)
SPEEDS = (COURANT * RATIO ** np.arange(NF, dtype=np.float64)).astype(np.float32)


def stress_table():
    table = np.zeros((ROWS, 16, NDIR, NF), np.float32)
    for c, part in enumerate((COS, SIN)):
        weights = np.float32(STRESS) * SPEEDS[None, :] * part[:, None]
        for x in range(ROWS):
            table[x, c * 8 + 1 + x] = weights
    return table.reshape(ROWS, 16, BINS)


def is_even(axis):
    return lax.rem(lax.axis_index(axis), 2) == 0


def inside(axis):
    i = lax.axis_index(axis)
    return jnp.logical_and(i > 0, i < lax.axis_size(axis) - 1)


def split(v):
    high = v.astype(BF16).astype(F32)
    return high, v - high


def roll(v, shift, axis):
    return pltpu.roll(v, shift % v.shape[axis], axis)


def lane_of(shape):
    return lax.broadcasted_iota(jnp.int32, shape, len(shape) - 1)


def make_edge_tables(table_ref):
    source = lax.broadcasted_iota(jnp.int32, (LANES, LANES), 0)
    lane = lane_of((LANES, LANES)) % 8
    for side, start in enumerate((0, LANES - 2)):
        for x in range(ROWS):
            found = (lane == source + (2 * x - start)) & (lane >= 2 * x) & (lane < 2 * x + 2)
            table_ref[side, LANES * x : LANES * (x + 1), :] = jnp.where(found, 1.0, 0.0).astype(BF16)


def shift_tables():
    table = np.zeros((2, 2 * LANES, 2 * LANES), np.float32)
    for side, sign in enumerate((1, -1)):
        for far in range(2):
            for lane in range(LANES):
                source = lane + sign * (1 + far)
                if 0 <= source < LANES:
                    table[side, source, far * LANES + lane] = 1.0
                else:
                    j = source - LANES if sign > 0 else source + 2
                    for x in range(ROWS):
                        for g in range(4):
                            table[side, LANES + 32 * x + 8 * g + 2 * x + j, far * LANES + lane] = 1.0
    return table


def pack_y_edges(n_ref, quarter, tables_ref, out_ref):
    south = quarter in (1, 2)
    first = quarter * QUARTER
    rows = [
        n_ref[x, first : first + QUARTER].reshape(QUARTER * NF, LANES).astype(BF16) for x in range(ROWS)
    ]
    found = jnp.dot(
        jnp.concatenate(rows, 1), tables_ref[1 if south else 0], preferred_element_type=F32
    ).reshape(QUARTER, 4, 8, LANES)
    group = lane_of((QUARTER, 8, LANES)) // 8
    packed = found[:, 0]
    for g in range(1, 4):
        packed = jnp.where(group == g, found[:, g], packed)
    at = 0 if quarter < 2 else QUARTER
    out_ref[1 if south else 0, at : at + QUARTER] = packed


def pack_ocean_columns(blocks, lanes):
    first = jnp.zeros((8, LANES), F32)
    last = jnp.zeros((8, LANES), F32)
    for c in range(3):
        for z in range(NZ):
            block = blocks[c][8 * z : 8 * z + 8]
            at = c * NZ + z
            first = jnp.where(lanes == at, roll(block, at, 1), first)
            last = jnp.where(lanes == at, roll(block, at - (LANES - 1), 1), last)
    return first, last


def ocean_blocks(o_ref):
    pad = jnp.zeros((1, LANES), F32)
    return [
        jnp.concatenate(
            [part for z in range(NZ) for part in (pad, o_ref[c, z], pad, pad, pad)], 0
        )
        for c in range(3)
    ]


def send_x(n_ref, ocean_rows, mine_ref, low_side):
    row = jnp.where(low_side, 0, 2)
    first = jnp.where(low_side, HALF, 0)
    edge = n_ref[pl.ds(row, 2), pl.ds(first, HALF)]
    mine_ref[0:SPECTRA, :] = edge.reshape(SPECTRA, LANES).astype(BF16)
    send_ocean_row(ocean_rows, mine_ref, low_side)


def send_ocean_row(ocean_rows, mine_ref, low_side):
    low, high = ocean_rows
    whole, rest = split(jnp.where(low_side, low, high))
    mine_ref[SPECTRA : SPECTRA + OCEAN, :] = whole.astype(BF16)
    mine_ref[SPECTRA + OCEAN : XROWS, :] = rest.astype(BF16)


def send_y(edges_ref, first, last, even, outs):
    for slot, out_ref in enumerate(outs):
        takes_last = even if slot == 0 else jnp.logical_not(even)
        which = takes_last.astype(jnp.int32)
        out_ref[0 : HALF * 8, :] = edges_ref[which].reshape(HALF * 8, LANES).astype(BF16)
        whole, rest = split(jnp.where(takes_last, last, first))
        out_ref[HALF * 8 : YROWS, :] = jnp.concatenate([whole, rest], 0).astype(BF16)


def first_kernel(s_hbm, o_hbm, mask_hbm, xo_ref, s_ref, o_ref, mask_ref, t_ref, sems):
    low_side = is_even("gx")
    row = jnp.where(low_side, 0, 2)
    first = jnp.where(low_side, HALF, 0)
    copies = [pltpu.make_async_copy(s_hbm.at[row + r], s_ref.at[r], sems.at[r]) for r in range(2)]
    copies.append(pltpu.make_async_copy(mask_hbm, mask_ref, sems.at[2]))
    copies.append(pltpu.make_async_copy(o_hbm, o_ref, sems.at[3]))
    for copy in copies:
        copy.start()
    copies[2].wait()
    for r in range(2):
        copies[r].wait()
        t_ref[r] = jnp.transpose(s_ref[r].astype(F32))
        wet = mask_ref[pl.ds(row + r, 1), :].astype(F32)

        def body(kk, carry, r=r, wet=wet):
            at = pl.ds(pl.multiple_of((r * HALF + kk) * NF, NF), NF)
            xo_ref[at, :] = (t_ref[r, pl.ds(first + kk, NF, stride=NDIR), :] * wet).astype(BF16)
            return carry

        lax.fori_loop(0, HALF, body, 0, unroll=18)
    copies[3].wait()
    rows = tuple(o_ref[:, :, r, :].reshape(OCEAN, LANES) for r in (0, ROWS - 1))
    send_ocean_row(rows, xo_ref, low_side)


def prepare_kernel(n_ref, w_ref, stress_ref, tab_ref):
    make_tables(tab_ref)
    stress_ref[...] = stress_of(n_ref, w_ref)


def start_kernel(s_ref, o_ref, mask_ref,
                 n_ref, xe_ref, ye_ref, yo_ref, edge_ref, t_ref, e_ref):
    wet = mask_ref[...].astype(F32)
    for x in range(ROWS):
        t_ref[x] = jnp.transpose(s_ref[x].astype(F32))

    def body(k, carry):
        for x in range(ROWS):
            n_ref[x, k] = t_ref[x, pl.ds(k, NF, stride=NDIR), :] * wet[x : x + 1]
        return carry

    lax.fori_loop(0, NDIR, body, 0, unroll=6)
    even_x, even_y = is_even("gx"), is_even("gy")
    rows = tuple(o_ref[:, :, r, :].reshape(OCEAN, LANES) for r in (0, ROWS - 1))
    send_x(n_ref, rows, xe_ref, jnp.logical_not(even_x))
    make_edge_tables(edge_ref)
    for quarter in range(4):
        pack_y_edges(n_ref, quarter, edge_ref, e_ref)
    first, last = pack_ocean_columns(ocean_blocks(o_ref), lane_of((8, LANES)))
    send_y(e_ref, first, last, even_y, (ye_ref, yo_ref))


def make_tables(tab_ref):
    row = lax.broadcasted_iota(jnp.int32, (8, LANES), 0)
    blocks = []
    for g in range(4):
        block = jnp.full((8, LANES), float(SPEEDS[8 * g]), F32)
        for i in range(1, 8):
            block = jnp.where(row == i, float(SPEEDS[8 * g + i]), block)
        blocks.append(block)
    speed = jnp.concatenate(blocks, 0)
    for k in range(NDIR):
        cx, cy = speed * abs(float(COS[k])), speed * abs(float(SIN[k]))
        near_x, far_x = cx * (2.0 - cx), (0.5 * cx) * (cx - 1.0)
        near_y, far_y = cy * (2.0 - cy), (0.5 * cy) * (cy - 1.0)
        tab_ref[0, k] = 1.0 - ((near_x + far_x) + (near_y + far_y))
        tab_ref[1, k] = near_x
        tab_ref[2, k] = far_x
        tab_ref[3, k] = near_y
        tab_ref[4, k] = far_y


def y_spectra(even_y, ye_ref, yo_ref, yh_ref):
    shape = (HALF, 8, LANES)
    a = ye_ref[0 : HALF * 8, :].astype(F32)
    b = jnp.where(inside("gy"), yo_ref[0 : HALF * 8, :].astype(F32), 0.0)
    group = lane_of(shape) // 8
    for to, pair in ((0, (a, b)), (1, (b, a))):
        edge = jnp.where(even_y, *pair).reshape(shape)
        parts = [jnp.where(group == g, edge, 0.0)[:, None] for g in range(4)]
        yh_ref[to] = jnp.concatenate(parts, 1).reshape(HALF * NF, LANES).astype(BF16)


def y_ocean(even_y, ye_ref, yo_ref):
    def columns(ref):
        both = ref[HALF * 8 : YROWS, :].astype(F32)
        return both[0:8] + both[8:16]

    a, b = columns(ye_ref), jnp.where(inside("gy"), columns(yo_ref), 0.0)
    return jnp.where(even_y, b, a), jnp.where(even_y, a, b)


def x_ocean(even_x, xe_ref, xo_ref):
    def rows(ref):
        return ref[SPECTRA : SPECTRA + OCEAN, :].astype(F32) + ref[SPECTRA + OCEAN : XROWS, :].astype(F32)

    a, b = rows(xe_ref), jnp.where(inside("gx"), rows(xo_ref), 0.0)
    return jnp.where(even_x, b, a), jnp.where(even_x, a, b)


def extend_ocean(o_ref, left, right, ext_ref, levels=NZ):
    for c in range(3):
        for z in range(levels):
            at = c * NZ + z
            ext_ref[c, 8 * z : 8 * z + 1, :] = left[at : at + 1]
            ext_ref[c, 8 * z + 1 : 8 * z + 5, :] = o_ref[c, z]
            ext_ref[c, 8 * z + 5 : 8 * z + 6, :] = right[at : at + 1]
            ext_ref[c, 8 * z + 6 : 8 * z + 8, :] = jnp.zeros((2, LANES), F32)


def neighbours(c, q, below, above, levels):
    lanes = lane_of(q.shape)
    low = jnp.concatenate([roll(below, -(c * NZ + z), 1) for z in range(levels)], 0)
    high = jnp.concatenate([roll(above, LANES - 1 - (c * NZ + z), 1) for z in range(levels)], 0)
    return (
        roll(q, 1, 0),
        roll(q, -1, 0),
        jnp.where(lanes == 0, low, roll(q, 1, 1)),
        jnp.where(lanes == LANES - 1, high, roll(q, -1, 1)),
    )


def refraction_rates(ext_ref, below, above, rate_ref):
    grads = []
    for c in range(2):
        xm, xp, ym, yp = neighbours(c, ext_ref[c, 0:8, :], below, above, 1)
        grads.append(((xp - xm) * 0.5, (yp - ym) * 0.5))
    (ux, uy), (vx, vy) = grads
    stretch = ux - vy
    for k in range(NDIR):
        c, s = float(COS[k]), float(SIN[k])
        rate_ref[k] = (TURN * c * s) * stretch + (TURN * s * s) * vx - (TURN * c * c) * uy


def advance_ocean(ext_ref, below, above, stress, wet8, out_ref):
    zonal, north, heat = (ext_ref[c] for c in range(3))
    wet = jnp.concatenate([wet8] * NZ, 0)

    def stencil(c, q):
        xm, xp, ym, yp = neighbours(c, q, below, above, NZ)
        return (xp - xm) * 0.5, (yp - ym) * 0.5, xp + xm + yp + ym - 4.0 * q

    _, _, zonal_lap = stencil(0, zonal)
    _, _, north_lap = stencil(1, north)
    heat_x, heat_y, heat_lap = stencil(2, heat)

    def running(v):
        total = v[0:8]
        sums = [total]
        for z in range(1, NZ):
            total = total + v[8 * z : 8 * z + 8]
            sums.append(total)
        return jnp.concatenate(sums, 0)

    rest = jnp.zeros((8 * (NZ - 1), LANES), F32)
    push_u = jnp.concatenate([stress[0:8], rest], 0)
    push_v = jnp.concatenate([stress[8:16], rest], 0)
    new = (
        wet * (zonal + CORIOLIS * north - PRESS * running(heat_x) + VISC * zonal_lap + push_u),
        wet * (north - CORIOLIS * zonal - PRESS * running(heat_y) + VISC * north_lap + push_v),
        heat + wet * (DIFFUSE * heat_lap - ADVECT * (zonal * heat_x + north * heat_y)),
    )
    for c in range(3):
        for z in range(NZ):
            out_ref[c, z] = new[c][8 * z + 1 : 8 * z + 5]
    return new


def stress_of(n_ref, weights_ref):
    total = jnp.zeros((16, LANES), F32)
    for x in range(ROWS):
        cells = n_ref[x].reshape(BINS, LANES).astype(BF16)
        total = total + jnp.dot(weights_ref[x], cells, preferred_element_type=F32)
    return total


def refraction(n_ref, rate_ref, x, k):
    below = jnp.where(k == 0, NDIR - 1, k - 1)
    above = jnp.where(k == NDIR - 1, 0, k + 1)
    rate = jnp.broadcast_to(rate_ref[k, pl.ds(x + 1, 1), :], (NF, LANES))
    upwind = jnp.where(rate > 0.0, n_ref[x, below], n_ref[x, above])
    return jnp.abs(rate) * (upwind - n_ref[x, k])


def cell_of(acc_ref, x, k):
    if len(acc_ref.shape) == 4:
        return x, k
    return x, pl.ds(k, NF, stride=NDIR), slice(None)


def inner_waves(n_ref, yh_ref, rate_ref, wet, tab_ref, shift_ref, ys_ref, acc_ref, keep):
    size = QUARTER * NF
    for quarter in range(4):
        step = 1 if quarter >= 2 else -1
        side = 1 if quarter in (1, 2) else 0
        first = quarter * QUARTER
        edges = yh_ref[side, 0:size, :] if quarter < 2 else yh_ref[side, size : 2 * size, :]
        blank = jnp.zeros((LANES - 32, 2 * LANES), BF16)
        for x in range(ROWS):
            cells = n_ref[x, first : first + QUARTER].reshape(size, LANES).astype(BF16)
            edge_rows = shift_ref[side, LANES + 32 * x : LANES + 32 * x + 32, :]
            moves = jnp.concatenate([shift_ref[side, 0:LANES, :], edge_rows, blank], 0)
            ys_ref[x] = jnp.dot(jnp.concatenate([cells, edges], 1), moves, preferred_element_type=F32)

        def body(j, carry, first=first, step=step):
            k = first + j
            weights = [tab_ref[t, k] for t in range(5)]
            at = pl.ds(pl.multiple_of(j * NF, NF), NF)
            cells = [n_ref[x, k] for x in range(ROWS)]
            for x in range(ROWS):
                total = cells[x] * weights[0]
                for weight, other in zip(weights[1:3], (x + step, x + 2 * step)):
                    if 0 <= other < ROWS:
                        total = total + cells[other] * weight
                near_y, far_y = ys_ref[x, at, 0:LANES], ys_ref[x, at, LANES : 2 * LANES]
                total = total + (near_y * weights[3] + far_y * weights[4])
                if x in (1, 2):
                    total = total + refraction(n_ref, rate_ref, x, k)
                    if 0 <= x + 2 * step < ROWS:
                        total = keep(total * wet[x])
                acc_ref[cell_of(acc_ref, x, k)] = total
            return carry

        lax.fori_loop(0, QUARTER, body, 0, unroll=QUARTER)


def wet_row(mask_ref, x):
    return jnp.broadcast_to(mask_ref[pl.ds(x, 1), :].astype(F32), (NF, LANES))


def finish_far_half(n_ref, acc_ref, rate_ref, mask_ref, side, keep):
    x = 3 * side
    wet = wet_row(mask_ref, x)
    first = HALF * (1 - side)

    def body(kk, carry):
        k = first + kk
        cell = cell_of(acc_ref, x, k)
        acc_ref[cell] = keep(wet * (acc_ref[cell] + refraction(n_ref, rate_ref, x, k)))
        return carry

    lax.fori_loop(0, HALF, body, 0, unroll=18)


def finish_near_half(n_ref, acc_ref, rate_ref, mask_ref, tab_ref, halo_ref, known, side, keep):
    x, inner = 3 * side, 1 + side
    wet, wet_inner = wet_row(mask_ref, x), wet_row(mask_ref, inner)
    first = HALF * side

    def body(kk, carry):
        k = first + kk
        near = halo_ref[pl.ds(pl.multiple_of(((1 - side) * HALF + kk) * NF, NF), NF), :].astype(F32)
        far = halo_ref[pl.ds(pl.multiple_of((side * HALF + kk) * NF, NF), NF), :].astype(F32)
        near, far = jnp.where(known, near, 0.0), jnp.where(known, far, 0.0)
        cell, inner_cell = cell_of(acc_ref, x, k), cell_of(acc_ref, inner, k)
        total = acc_ref[cell] + (near * tab_ref[1, k] + far * tab_ref[2, k])
        acc_ref[cell] = keep(wet * (total + refraction(n_ref, rate_ref, x, k)))
        acc_ref[inner_cell] = keep(wet_inner * (acc_ref[inner_cell] + near * tab_ref[2, k]))
        return carry

    lax.fori_loop(0, HALF, body, 0, unroll=18)


def rounded(v):
    return v.astype(BF16).astype(F32)


def exact(v):
    return v


def wet_rows(mask_ref):
    wet = mask_ref[...].astype(F32)
    pad = jnp.zeros((1, LANES), F32)
    wet8 = jnp.concatenate([pad, wet, pad, pad, pad], 0)
    return [jnp.broadcast_to(wet[x : x + 1], (NF, LANES)) for x in range(ROWS)], wet8


def inner_kernel(n_ref, o_ref, mask_ref, tab_ref, shift_ref, ye_in, yo_in,
                 acc_ref, yh_ref, ext_ref, rate_ref, ys_ref):
    even_y = is_even("gy")
    wet, _ = wet_rows(mask_ref)
    y_spectra(even_y, ye_in, yo_in, yh_ref)
    below, above = y_ocean(even_y, ye_in, yo_in)
    unknown = jnp.zeros((OCEAN, LANES), F32)
    extend_ocean(o_ref, unknown, unknown, ext_ref, 1)
    refraction_rates(ext_ref, below, above, rate_ref)
    inner_waves(n_ref, yh_ref, rate_ref, wet, tab_ref, shift_ref, ys_ref, acc_ref, rounded)


def send_kernel(n_ref, acc_in, o_ref, mask_ref, stress_ref, xe_in, xo_in, ye_in, yo_in,
                acc_ref, ocean_ref, rate_ref, xo_ref, xrow_ref, ext_ref):
    even_x, even_y = is_even("gx"), is_even("gy")
    below, above = y_ocean(even_y, ye_in, yo_in)
    left, right = x_ocean(even_x, xe_in, xo_in)
    extend_ocean(o_ref, left, right, ext_ref)
    refraction_rates(ext_ref, below, above, rate_ref)
    finish_far_half(n_ref, acc_ref, rate_ref, mask_ref, 1 - even_x.astype(jnp.int32), rounded)
    _, wet8 = wet_rows(mask_ref)
    new = advance_ocean(ext_ref, below, above, stress_ref[...], wet8, ocean_ref)
    rows = tuple(
        jnp.concatenate([new[c][8 * z + r : 8 * z + r + 1] for c in range(3) for z in range(NZ)], 0)
        for r in (1, ROWS)
    )
    send_x(acc_ref, rows, xo_ref, even_x)
    xo_ref[XROWS:, :] = jnp.zeros((16, LANES), BF16)
    xrow_ref[...] = jnp.where(even_x, rows[1], rows[0])


def rest_kernel(n_ref, acc_in, mask_ref, tab_ref, rate_ref, edge_ref, xrow_ref, o_ref, xe_in, xo_in,
                acc_ref, xe_ref, ye_ref, yo_ref, e_ref):
    even_x, even_y = is_even("gx"), is_even("gy")
    side = even_x.astype(jnp.int32)
    finish_near_half(n_ref, acc_ref, rate_ref, mask_ref, tab_ref, xo_in, inside("gx"), 1 - side, rounded)
    finish_near_half(n_ref, acc_ref, rate_ref, mask_ref, tab_ref, xe_in, True, side, rounded)
    finish_far_half(n_ref, acc_ref, rate_ref, mask_ref, side, rounded)
    row = xrow_ref[...]
    send_x(acc_ref, (row, row), xe_ref, jnp.logical_not(even_x))
    for quarter in range(4):
        pack_y_edges(acc_ref, quarter, edge_ref, e_ref)
    first, last = pack_ocean_columns(ocean_blocks(o_ref), lane_of((8, LANES)))
    send_y(e_ref, first, last, even_y, (ye_ref, yo_ref))


def inner_last_kernel(n_ref, o_ref, mask_ref, tab_ref, w_ref, shift_ref, xe_in, ye_in, yo_in,
                      acc_ref, stress_ref, done_ref,
                      yh_ref, ext_ref, rate_ref, ys_ref):
    even_x, even_y = is_even("gx"), is_even("gy")
    wet, _ = wet_rows(mask_ref)
    y_spectra(even_y, ye_in, yo_in, yh_ref)
    below, above = y_ocean(even_y, ye_in, yo_in)
    left, right = x_ocean(even_x, xe_in, xe_in)
    extend_ocean(o_ref, left, right, ext_ref, 1)
    refraction_rates(ext_ref, below, above, rate_ref)
    stress_ref[...] = stress_of(n_ref, w_ref)
    inner_waves(n_ref, yh_ref, rate_ref, wet, tab_ref, shift_ref, ys_ref, acc_ref, exact)
    side = even_x.astype(jnp.int32)
    finish_near_half(n_ref, acc_ref, rate_ref, mask_ref, tab_ref, xe_in, True, side, exact)
    finish_far_half(n_ref, acc_ref, rate_ref, mask_ref, side, exact)
    for r in range(2):
        done_ref[r] = jnp.transpose(acc_ref[2 * side + r]).astype(BF16)


def last_kernel(n_ref, acc_in, done_ref, o_ref, mask_ref, tab_ref, stress_ref, xe_in, xo_in, ye_in, yo_in,
                acc_ref, ocean_ref, out_hbm, ext_ref, rate_ref, block_ref, sems):
    even_x, even_y = is_even("gx"), is_even("gy")
    side = 1 - even_x.astype(jnp.int32)
    done = pltpu.make_async_copy(done_ref, out_hbm.at[pl.ds(2 * (1 - side), 2)], sems.at[0])
    done.start()
    below, above = y_ocean(even_y, ye_in, yo_in)
    left, right = x_ocean(even_x, xe_in, xo_in)
    extend_ocean(o_ref, left, right, ext_ref, 1)
    refraction_rates(ext_ref, below, above, rate_ref)
    finish_near_half(n_ref, acc_ref, rate_ref, mask_ref, tab_ref, xo_in, inside("gx"), side, exact)
    finish_far_half(n_ref, acc_ref, rate_ref, mask_ref, side, exact)
    copies = [done]
    for r in range(2):
        block_ref[r] = jnp.transpose(acc_ref[2 * side + r]).astype(BF16)
        copies.append(pltpu.make_async_copy(block_ref.at[r], out_hbm.at[2 * side + r], sems.at[1 + r]))
        copies[-1].start()
    _, wet8 = wet_rows(mask_ref)
    extend_ocean(o_ref, left, right, ext_ref)
    advance_ocean(ext_ref, below, above, stress_ref[...], wet8, ocean_ref)
    for copy in copies:
        copy.wait()


def swap(array, axis, odd, wrap=False):
    nx, ny = lax.axis_size("gx"), lax.axis_size("gy")
    pairs = []
    for i in range(nx):
        for j in range(ny):
            to = (i ^ 1, j) if axis == "gx" else (i, j ^ 1)
            if odd and axis == "gx":
                to = (((i + 1) ^ 1) - 1, j) if 0 < i < nx - 1 else ((nx - 1 - i, j) if wrap else (i, j ^ 1))
            if odd and axis == "gy":
                to = (i, ((j + 1) ^ 1) - 1) if 0 < j < ny - 1 else (i ^ 1, j)
            pairs.append((i * ny + j, to[0] * ny + to[1]))
    return lax.ppermute(array, ("gx", "gy"), pairs)


def call(kernel, outs, ins, scratch, params=None, any_in=(), any_out=(), aliases=None, moved=0):
    places = [HBM if i in any_in else VM for i in range(len(ins))]
    return pl.pallas_call(
        kernel,
        out_shape=[jax.ShapeDtypeStruct(shape, dtype) for shape, dtype in outs],
        in_specs=places,
        out_specs=[HBM if i in any_out else VM for i in range(len(outs))],
        scratch_shapes=scratch,
        compiler_params=params or PARAMS,
        input_output_aliases=aliases or {},
        cost_estimate=pl.CostEstimate(flops=0, bytes_accessed=moved * 1024 * 1024, transcendentals=0),
        name=kernel.__name__.removesuffix("_kernel"),
    )(*ins)


BINNED = ((ROWS, BINS, LANES), F32)
GRID = ((ROWS, NDIR, NF, LANES), F32)
XEDGE = ((XROWS, LANES), BF16)
XLONG = ((XROWS + 16, LANES), BF16)
YEDGE = ((YROWS, LANES), BF16)
DRIVE = ((16, LANES), F32)
RATES = ((NDIR, 8, LANES), F32)
YH = pltpu.VMEM((2, HALF * NF, LANES), BF16)
EXT = pltpu.VMEM((3, 8 * NZ, LANES), F32)
RATE = pltpu.VMEM(*RATES)
SHIFTED = pltpu.VMEM((ROWS, QUARTER * NF, 2 * LANES), F32)
EDGES = pltpu.VMEM((2, HALF, 8, LANES), F32)
TURNED = pltpu.VMEM((2, BINS, LANES), F32)
BLOCK = pltpu.VMEM((2, LANES, BINS), BF16)


def local(spectrum, ocean_state, sea_mask):
    ocean_shape = (ocean_state.shape, F32)
    weights = jnp.asarray(stress_table(), dtype=BF16)
    shift_table = jnp.asarray(shift_tables(), dtype=BF16)
    (xo,) = call(
        first_kernel,
        (XEDGE,),
        (spectrum, ocean_state, sea_mask),
        [
            pltpu.VMEM((2, *spectrum.shape[1:]), BF16),
            pltpu.VMEM(ocean_state.shape, F32),
            pltpu.VMEM(sea_mask.shape, jnp.int32),
            TURNED,
            pltpu.SemaphoreType.DMA((4,)),
        ],
        FIRST,
        any_in=(0, 1, 2),
        moved=32,
    )
    xo = swap(xo, "gx", 1)
    n, xe, ye, yo, edge_table = call(
        start_kernel,
        (GRID, XEDGE, YEDGE, YEDGE, ((2, ROWS * LANES, LANES), BF16)),
        (spectrum, ocean_state, sea_mask),
        [pltpu.VMEM((ROWS, BINS, LANES), F32), EDGES],
    )
    xe = swap(xe, "gx", 0)
    ye = swap(ye, "gy", 0)
    yo = swap(yo, "gy", 1)
    stress, tab = call(prepare_kernel, (DRIVE, ((5, NDIR, NF, LANES), F32)), (n, weights), [])
    (acc,) = call(
        inner_kernel,
        (GRID,),
        (n, ocean_state, sea_mask, tab, shift_table, ye, yo),
        [YH, EXT, RATE, SHIFTED],
    )
    acc, ocean, rate, xo2, xrow = call(
        send_kernel,
        (GRID, ocean_shape, RATES, XLONG, ((OCEAN, LANES), F32)),
        (n, acc, ocean_state, sea_mask, stress, xe, xo, ye, yo),
        [EXT],
        aliases={1: 0},
    )
    xo2 = swap(xo2, "gx", 1, True)
    n, xe, ye, yo = call(
        rest_kernel,
        (GRID, XEDGE, YEDGE, YEDGE),
        (n, acc, sea_mask, tab, rate, edge_table, xrow, ocean, xe, xo),
        [EDGES],
        aliases={1: 0},
    )
    xe = swap(xe, "gx", 0)
    ye = swap(ye, "gy", 0)
    yo = swap(yo, "gy", 1)
    acc, stress, done = call(
        inner_last_kernel,
        (BINNED, DRIVE, ((2, *spectrum.shape[1:]), BF16)),
        (n, ocean, sea_mask, tab, weights, shift_table, xe, ye, yo),
        [YH, EXT, RATE, SHIFTED],
    )
    _, ocean, out = call(
        last_kernel,
        (BINNED, ocean_shape, (spectrum.shape, BF16)),
        (n, acc, done, ocean, sea_mask, tab, stress, xe, xo2, ye, yo),
        [EXT, RATE, BLOCK, pltpu.SemaphoreType.DMA((3,))],
        any_out=(2,),
        aliases={1: 0},
    )
    return out, ocean


def solution(mesh):
    placed = (P("gx", "gy", None), P(None, None, "gx", "gy"), P("gx", "gy"))
    return jax.shard_map(
        local,
        mesh=mesh,
        in_specs=placed,
        out_specs=(P("gx", "gy", None), P(None, None, "gx", "gy")),
        check_vma=False,
    )
```

```python
import math

import jax
import jax.numpy as jnp
import numpy as np
from jax import lax
from jax.experimental import pallas as pl
from jax.experimental.pallas import tpu as pltpu
from jax.sharding import PartitionSpec as P

NF = 32
NDIR = 36
NZ = 16
HALF = NDIR // 2
QUARTER = NDIR // 4
ROWS = 4
LANES = 128
BINS = NF * NDIR

COURANT = 0.4
RATIO = 0.93
TURN = 0.1
STRESS = 0.1
CORIOLIS = 0.2
PRESS = 0.1
VISC = 0.15
ADVECT = 0.5
DIFFUSE = 0.15

F32 = jnp.float32
BF16 = jnp.bfloat16
VM = pl.BlockSpec(memory_space=pltpu.VMEM)
HBM = pl.BlockSpec(memory_space=pl.ANY)
FIRST = pltpu.CompilerParams(vmem_limit_bytes=53 * 1024 * 1024)
PARAMS = pltpu.CompilerParams(vmem_limit_bytes=16 * 1024 * 1024)

SPECTRA = 2 * HALF * NF
OCEAN = 3 * NZ
XROWS = SPECTRA + 2 * OCEAN
YROWS = HALF * 8 + 16

ANGLES = -0.5 * math.pi + (np.arange(NDIR, dtype=np.float32) + np.float32(0.5)) * np.float32(
    2.0 * math.pi / NDIR
)
COS = np.cos(ANGLES).astype(np.float32)
SIN = np.sin(ANGLES).astype(np.float32)
SPEEDS = (COURANT * RATIO ** np.arange(NF, dtype=np.float64)).astype(np.float32)


def stress_table():
    table = np.zeros((ROWS, 16, NDIR, NF), np.float32)
    for c, part in enumerate((COS, SIN)):
        weights = np.float32(STRESS) * SPEEDS[None, :] * part[:, None]
        for x in range(ROWS):
            table[x, c * 8 + 1 + x] = weights
    return table.reshape(ROWS, 16, BINS)


def is_even(axis):
    return lax.rem(lax.axis_index(axis), 2) == 0


def inside(axis):
    i = lax.axis_index(axis)
    return jnp.logical_and(i > 0, i < lax.axis_size(axis) - 1)


def split(v):
    high = v.astype(BF16).astype(F32)
    return high, v - high


def roll(v, shift, axis):
    return pltpu.roll(v, shift % v.shape[axis], axis)


def lane_of(shape):
    return lax.broadcasted_iota(jnp.int32, shape, len(shape) - 1)


def make_edge_tables(table_ref):
    source = lax.broadcasted_iota(jnp.int32, (LANES, LANES), 0)
    lane = lane_of((LANES, LANES)) % 8
    for side, start in enumerate((0, LANES - 2)):
        for x in range(ROWS):
            found = (lane == source + (2 * x - start)) & (lane >= 2 * x) & (lane < 2 * x + 2)
            table_ref[side, LANES * x : LANES * (x + 1), :] = jnp.where(found, 1.0, 0.0).astype(BF16)


def shift_tables():
    table = np.zeros((2, 2 * LANES, 2 * LANES), np.float32)
    for side, sign in enumerate((1, -1)):
        for far in range(2):
            for lane in range(LANES):
                source = lane + sign * (1 + far)
                if 0 <= source < LANES:
                    table[side, source, far * LANES + lane] = 1.0
                else:
                    j = source - LANES if sign > 0 else source + 2
                    for x in range(ROWS):
                        for g in range(4):
                            table[side, LANES + 32 * x + 8 * g + 2 * x + j, far * LANES + lane] = 1.0
    return table


def pack_y_edges(n_ref, quarter, tables_ref, out_ref):
    south = quarter in (1, 2)
    first = quarter * QUARTER
    rows = [
        n_ref[x, first : first + QUARTER].reshape(QUARTER * NF, LANES).astype(BF16) for x in range(ROWS)
    ]
    found = jnp.dot(
        jnp.concatenate(rows, 1), tables_ref[1 if south else 0], preferred_element_type=F32
    ).reshape(QUARTER, 4, 8, LANES)
    group = lane_of((QUARTER, 8, LANES)) // 8
    packed = found[:, 0]
    for g in range(1, 4):
        packed = jnp.where(group == g, found[:, g], packed)
    at = 0 if quarter < 2 else QUARTER
    out_ref[1 if south else 0, at : at + QUARTER] = packed


def pack_ocean_columns(blocks, lanes):
    first = jnp.zeros((8, LANES), F32)
    last = jnp.zeros((8, LANES), F32)
    for c in range(3):
        for z in range(NZ):
            block = blocks[c][8 * z : 8 * z + 8]
            at = c * NZ + z
            first = jnp.where(lanes == at, roll(block, at, 1), first)
            last = jnp.where(lanes == at, roll(block, at - (LANES - 1), 1), last)
    return first, last


def ocean_blocks(o_ref):
    pad = jnp.zeros((1, LANES), F32)
    return [
        jnp.concatenate(
            [part for z in range(NZ) for part in (pad, o_ref[c, z], pad, pad, pad)], 0
        )
        for c in range(3)
    ]


def send_x(n_ref, ocean_rows, mine_ref, low_side):
    row = jnp.where(low_side, 0, 2)
    first = jnp.where(low_side, HALF, 0)
    edge = n_ref[pl.ds(row, 2), pl.ds(first, HALF)]
    mine_ref[0:SPECTRA, :] = edge.reshape(SPECTRA, LANES).astype(BF16)
    send_ocean_row(ocean_rows, mine_ref, low_side)


def send_ocean_row(ocean_rows, mine_ref, low_side):
    low, high = ocean_rows
    whole, rest = split(jnp.where(low_side, low, high))
    mine_ref[SPECTRA : SPECTRA + OCEAN, :] = whole.astype(BF16)
    mine_ref[SPECTRA + OCEAN : XROWS, :] = rest.astype(BF16)


def send_y(edges_ref, first, last, even, outs):
    for slot, out_ref in enumerate(outs):
        takes_last = even if slot == 0 else jnp.logical_not(even)
        which = takes_last.astype(jnp.int32)
        out_ref[0 : HALF * 8, :] = edges_ref[which].reshape(HALF * 8, LANES).astype(BF16)
        whole, rest = split(jnp.where(takes_last, last, first))
        out_ref[HALF * 8 : YROWS, :] = jnp.concatenate([whole, rest], 0).astype(BF16)


def first_kernel(s_hbm, o_hbm, mask_hbm, xo_ref, s_ref, o_ref, mask_ref, t_ref, sems):
    low_side = is_even("gx")
    row = jnp.where(low_side, 0, 2)
    first = jnp.where(low_side, HALF, 0)
    copies = [pltpu.make_async_copy(s_hbm.at[row + r], s_ref.at[r], sems.at[r]) for r in range(2)]
    copies.append(pltpu.make_async_copy(mask_hbm, mask_ref, sems.at[2]))
    copies.append(pltpu.make_async_copy(o_hbm, o_ref, sems.at[3]))
    for copy in copies:
        copy.start()
    copies[2].wait()
    for r in range(2):
        copies[r].wait()
        t_ref[r] = jnp.transpose(s_ref[r].astype(F32))
        wet = mask_ref[pl.ds(row + r, 1), :].astype(F32)

        def body(kk, carry, r=r, wet=wet):
            at = pl.ds(pl.multiple_of((r * HALF + kk) * NF, NF), NF)
            xo_ref[at, :] = (t_ref[r, pl.ds(first + kk, NF, stride=NDIR), :] * wet).astype(BF16)
            return carry

        lax.fori_loop(0, HALF, body, 0, unroll=18)
    copies[3].wait()
    rows = tuple(o_ref[:, :, r, :].reshape(OCEAN, LANES) for r in (0, ROWS - 1))
    send_ocean_row(rows, xo_ref, low_side)


def prepare_kernel(n_ref, w_ref, stress_ref, tab_ref):
    make_tables(tab_ref)
    stress_ref[...] = stress_of(n_ref, w_ref)


def start_kernel(s_ref, o_ref, mask_ref,
                 n_ref, xe_ref, ye_ref, yo_ref, edge_ref, t_ref, e_ref):
    wet = mask_ref[...].astype(F32)
    for x in range(ROWS):
        t_ref[x] = jnp.transpose(s_ref[x].astype(F32))

    def body(k, carry):
        for x in range(ROWS):
            n_ref[x, k] = t_ref[x, pl.ds(k, NF, stride=NDIR), :] * wet[x : x + 1]
        return carry

    lax.fori_loop(0, NDIR, body, 0, unroll=6)
    even_x, even_y = is_even("gx"), is_even("gy")
    rows = tuple(o_ref[:, :, r, :].reshape(OCEAN, LANES) for r in (0, ROWS - 1))
    send_x(n_ref, rows, xe_ref, jnp.logical_not(even_x))
    make_edge_tables(edge_ref)
    for quarter in range(4):
        pack_y_edges(n_ref, quarter, edge_ref, e_ref)
    first, last = pack_ocean_columns(ocean_blocks(o_ref), lane_of((8, LANES)))
    send_y(e_ref, first, last, even_y, (ye_ref, yo_ref))


def make_tables(tab_ref):
    row = lax.broadcasted_iota(jnp.int32, (8, LANES), 0)
    blocks = []
    for g in range(4):
        block = jnp.full((8, LANES), float(SPEEDS[8 * g]), F32)
        for i in range(1, 8):
            block = jnp.where(row == i, float(SPEEDS[8 * g + i]), block)
        blocks.append(block)
    speed = jnp.concatenate(blocks, 0)
    for k in range(NDIR):
        cx, cy = speed * abs(float(COS[k])), speed * abs(float(SIN[k]))
        near_x, far_x = cx * (2.0 - cx), (0.5 * cx) * (cx - 1.0)
        near_y, far_y = cy * (2.0 - cy), (0.5 * cy) * (cy - 1.0)
        tab_ref[0, k] = 1.0 - ((near_x + far_x) + (near_y + far_y))
        tab_ref[1, k] = near_x
        tab_ref[2, k] = far_x
        tab_ref[3, k] = near_y
        tab_ref[4, k] = far_y


def y_spectra(even_y, ye_ref, yo_ref, yh_ref):
    shape = (HALF, 8, LANES)
    a = ye_ref[0 : HALF * 8, :].astype(F32)
    b = jnp.where(inside("gy"), yo_ref[0 : HALF * 8, :].astype(F32), 0.0)
    group = lane_of(shape) // 8
    for to, pair in ((0, (a, b)), (1, (b, a))):
        edge = jnp.where(even_y, *pair).reshape(shape)
        parts = [jnp.where(group == g, edge, 0.0)[:, None] for g in range(4)]
        yh_ref[to] = jnp.concatenate(parts, 1).reshape(HALF * NF, LANES).astype(BF16)


def y_ocean(even_y, ye_ref, yo_ref):
    def columns(ref):
        both = ref[HALF * 8 : YROWS, :].astype(F32)
        return both[0:8] + both[8:16]

    a, b = columns(ye_ref), jnp.where(inside("gy"), columns(yo_ref), 0.0)
    return jnp.where(even_y, b, a), jnp.where(even_y, a, b)


def x_ocean(even_x, xe_ref, xo_ref):
    def rows(ref):
        return ref[SPECTRA : SPECTRA + OCEAN, :].astype(F32) + ref[SPECTRA + OCEAN : XROWS, :].astype(F32)

    a, b = rows(xe_ref), jnp.where(inside("gx"), rows(xo_ref), 0.0)
    return jnp.where(even_x, b, a), jnp.where(even_x, a, b)


def extend_ocean(o_ref, left, right, ext_ref, levels=NZ):
    for c in range(3):
        for z in range(levels):
            at = c * NZ + z
            ext_ref[c, 8 * z : 8 * z + 1, :] = left[at : at + 1]
            ext_ref[c, 8 * z + 1 : 8 * z + 5, :] = o_ref[c, z]
            ext_ref[c, 8 * z + 5 : 8 * z + 6, :] = right[at : at + 1]
            ext_ref[c, 8 * z + 6 : 8 * z + 8, :] = jnp.zeros((2, LANES), F32)


def neighbours(c, q, below, above, levels):
    lanes = lane_of(q.shape)
    low = jnp.concatenate([roll(below, -(c * NZ + z), 1) for z in range(levels)], 0)
    high = jnp.concatenate([roll(above, LANES - 1 - (c * NZ + z), 1) for z in range(levels)], 0)
    return (
        roll(q, 1, 0),
        roll(q, -1, 0),
        jnp.where(lanes == 0, low, roll(q, 1, 1)),
        jnp.where(lanes == LANES - 1, high, roll(q, -1, 1)),
    )


def refraction_rates(ext_ref, below, above, rate_ref):
    grads = []
    for c in range(2):
        xm, xp, ym, yp = neighbours(c, ext_ref[c, 0:8, :], below, above, 1)
        grads.append(((xp - xm) * 0.5, (yp - ym) * 0.5))
    (ux, uy), (vx, vy) = grads
    stretch = ux - vy
    for k in range(NDIR):
        c, s = float(COS[k]), float(SIN[k])
        rate_ref[k] = (TURN * c * s) * stretch + (TURN * s * s) * vx - (TURN * c * c) * uy


def advance_ocean(ext_ref, below, above, stress, wet8, out_ref):
    zonal, north, heat = (ext_ref[c] for c in range(3))
    wet = jnp.concatenate([wet8] * NZ, 0)

    def stencil(c, q):
        xm, xp, ym, yp = neighbours(c, q, below, above, NZ)
        return (xp - xm) * 0.5, (yp - ym) * 0.5, xp + xm + yp + ym - 4.0 * q

    _, _, zonal_lap = stencil(0, zonal)
    _, _, north_lap = stencil(1, north)
    heat_x, heat_y, heat_lap = stencil(2, heat)

    def running(v):
        total = v[0:8]
        sums = [total]
        for z in range(1, NZ):
            total = total + v[8 * z : 8 * z + 8]
            sums.append(total)
        return jnp.concatenate(sums, 0)

    rest = jnp.zeros((8 * (NZ - 1), LANES), F32)
    push_u = jnp.concatenate([stress[0:8], rest], 0)
    push_v = jnp.concatenate([stress[8:16], rest], 0)
    new = (
        wet * (zonal + CORIOLIS * north - PRESS * running(heat_x) + VISC * zonal_lap + push_u),
        wet * (north - CORIOLIS * zonal - PRESS * running(heat_y) + VISC * north_lap + push_v),
        heat + wet * (DIFFUSE * heat_lap - ADVECT * (zonal * heat_x + north * heat_y)),
    )
    for c in range(3):
        for z in range(NZ):
            out_ref[c, z] = new[c][8 * z + 1 : 8 * z + 5]
    return new


def stress_of(n_ref, weights_ref):
    total = jnp.zeros((16, LANES), F32)
    for x in range(ROWS):
        cells = n_ref[x].reshape(BINS, LANES).astype(BF16)
        total = total + jnp.dot(weights_ref[x], cells, preferred_element_type=F32)
    return total


def refraction(n_ref, rate_ref, x, k):
    below = jnp.where(k == 0, NDIR - 1, k - 1)
    above = jnp.where(k == NDIR - 1, 0, k + 1)
    rate = jnp.broadcast_to(rate_ref[k, pl.ds(x + 1, 1), :], (NF, LANES))
    upwind = jnp.where(rate > 0.0, n_ref[x, below], n_ref[x, above])
    return jnp.abs(rate) * (upwind - n_ref[x, k])


def cell_of(acc_ref, x, k):
    if len(acc_ref.shape) == 4:
        return x, k
    return x, pl.ds(k, NF, stride=NDIR), slice(None)


def inner_waves(n_ref, yh_ref, rate_ref, wet, tab_ref, shift_ref, ys_ref, acc_ref, keep):
    size = QUARTER * NF
    for quarter in range(4):
        step = 1 if quarter >= 2 else -1
        side = 1 if quarter in (1, 2) else 0
        first = quarter * QUARTER
        edges = yh_ref[side, 0:size, :] if quarter < 2 else yh_ref[side, size : 2 * size, :]
        blank = jnp.zeros((LANES - 32, 2 * LANES), BF16)
        for x in range(ROWS):
            cells = n_ref[x, first : first + QUARTER].reshape(size, LANES).astype(BF16)
            edge_rows = shift_ref[side, LANES + 32 * x : LANES + 32 * x + 32, :]
            moves = jnp.concatenate([shift_ref[side, 0:LANES, :], edge_rows, blank], 0)
            ys_ref[x] = jnp.dot(jnp.concatenate([cells, edges], 1), moves, preferred_element_type=F32)

        def body(j, carry, first=first, step=step):
            k = first + j
            weights = [tab_ref[t, k] for t in range(5)]
            at = pl.ds(pl.multiple_of(j * NF, NF), NF)
            cells = [n_ref[x, k] for x in range(ROWS)]
            for x in range(ROWS):
                total = cells[x] * weights[0]
                for weight, other in zip(weights[1:3], (x + step, x + 2 * step)):
                    if 0 <= other < ROWS:
                        total = total + cells[other] * weight
                near_y, far_y = ys_ref[x, at, 0:LANES], ys_ref[x, at, LANES : 2 * LANES]
                total = total + (near_y * weights[3] + far_y * weights[4])
                if x in (1, 2):
                    total = total + refraction(n_ref, rate_ref, x, k)
                    if 0 <= x + 2 * step < ROWS:
                        total = keep(total * wet[x])
                acc_ref[cell_of(acc_ref, x, k)] = total
            return carry

        lax.fori_loop(0, QUARTER, body, 0, unroll=QUARTER)


def wet_row(mask_ref, x):
    return jnp.broadcast_to(mask_ref[pl.ds(x, 1), :].astype(F32), (NF, LANES))


def finish_far_half(n_ref, acc_ref, rate_ref, mask_ref, side, keep):
    x = 3 * side
    wet = wet_row(mask_ref, x)
    first = HALF * (1 - side)

    def body(kk, carry):
        k = first + kk
        cell = cell_of(acc_ref, x, k)
        acc_ref[cell] = keep(wet * (acc_ref[cell] + refraction(n_ref, rate_ref, x, k)))
        return carry

    lax.fori_loop(0, HALF, body, 0, unroll=18)


def finish_near_half(n_ref, acc_ref, rate_ref, mask_ref, tab_ref, halo_ref, known, side, keep):
    x, inner = 3 * side, 1 + side
    wet, wet_inner = wet_row(mask_ref, x), wet_row(mask_ref, inner)
    first = HALF * side

    def body(kk, carry):
        k = first + kk
        near = halo_ref[pl.ds(pl.multiple_of(((1 - side) * HALF + kk) * NF, NF), NF), :].astype(F32)
        far = halo_ref[pl.ds(pl.multiple_of((side * HALF + kk) * NF, NF), NF), :].astype(F32)
        near, far = jnp.where(known, near, 0.0), jnp.where(known, far, 0.0)
        cell, inner_cell = cell_of(acc_ref, x, k), cell_of(acc_ref, inner, k)
        total = acc_ref[cell] + (near * tab_ref[1, k] + far * tab_ref[2, k])
        acc_ref[cell] = keep(wet * (total + refraction(n_ref, rate_ref, x, k)))
        acc_ref[inner_cell] = keep(wet_inner * (acc_ref[inner_cell] + near * tab_ref[2, k]))
        return carry

    lax.fori_loop(0, HALF, body, 0, unroll=6)


def rounded(v):
    return v.astype(BF16).astype(F32)


def exact(v):
    return v


def wet_rows(mask_ref):
    wet = mask_ref[...].astype(F32)
    pad = jnp.zeros((1, LANES), F32)
    wet8 = jnp.concatenate([pad, wet, pad, pad, pad], 0)
    return [jnp.broadcast_to(wet[x : x + 1], (NF, LANES)) for x in range(ROWS)], wet8


def inner_kernel(n_ref, o_ref, mask_ref, tab_ref, shift_ref, ye_in, yo_in,
                 acc_ref, yh_ref, ext_ref, rate_ref, ys_ref):
    even_y = is_even("gy")
    wet, _ = wet_rows(mask_ref)
    y_spectra(even_y, ye_in, yo_in, yh_ref)
    below, above = y_ocean(even_y, ye_in, yo_in)
    unknown = jnp.zeros((OCEAN, LANES), F32)
    extend_ocean(o_ref, unknown, unknown, ext_ref, 1)
    refraction_rates(ext_ref, below, above, rate_ref)
    inner_waves(n_ref, yh_ref, rate_ref, wet, tab_ref, shift_ref, ys_ref, acc_ref, rounded)


def send_kernel(n_ref, acc_in, o_ref, mask_ref, stress_ref, xe_in, xo_in, ye_in, yo_in,
                acc_ref, ocean_ref, rate_ref, xo_ref, xrow_ref, ext_ref):
    even_x, even_y = is_even("gx"), is_even("gy")
    below, above = y_ocean(even_y, ye_in, yo_in)
    left, right = x_ocean(even_x, xe_in, xo_in)
    extend_ocean(o_ref, left, right, ext_ref)
    refraction_rates(ext_ref, below, above, rate_ref)
    finish_far_half(n_ref, acc_ref, rate_ref, mask_ref, 1 - even_x.astype(jnp.int32), rounded)
    _, wet8 = wet_rows(mask_ref)
    new = advance_ocean(ext_ref, below, above, stress_ref[...], wet8, ocean_ref)
    rows = tuple(
        jnp.concatenate([new[c][8 * z + r : 8 * z + r + 1] for c in range(3) for z in range(NZ)], 0)
        for r in (1, ROWS)
    )
    send_x(acc_ref, rows, xo_ref, even_x)
    xo_ref[XROWS:, :] = jnp.zeros((16, LANES), BF16)
    xrow_ref[...] = jnp.where(even_x, rows[1], rows[0])


def rest_kernel(n_ref, acc_in, mask_ref, tab_ref, rate_ref, edge_ref, xrow_ref, o_ref, xe_in, xo_in,
                acc_ref, xe_ref, ye_ref, yo_ref, e_ref):
    even_x, even_y = is_even("gx"), is_even("gy")
    side = even_x.astype(jnp.int32)
    finish_near_half(n_ref, acc_ref, rate_ref, mask_ref, tab_ref, xo_in, inside("gx"), 1 - side, rounded)
    finish_near_half(n_ref, acc_ref, rate_ref, mask_ref, tab_ref, xe_in, True, side, rounded)
    finish_far_half(n_ref, acc_ref, rate_ref, mask_ref, side, rounded)
    row = xrow_ref[...]
    send_x(acc_ref, (row, row), xe_ref, jnp.logical_not(even_x))
    for quarter in range(4):
        pack_y_edges(acc_ref, quarter, edge_ref, e_ref)
    first, last = pack_ocean_columns(ocean_blocks(o_ref), lane_of((8, LANES)))
    send_y(e_ref, first, last, even_y, (ye_ref, yo_ref))


def inner_last_kernel(n_ref, o_ref, mask_ref, tab_ref, w_ref, shift_ref, xe_in, ye_in, yo_in,
                      acc_ref, stress_ref, done_ref,
                      yh_ref, ext_ref, rate_ref, ys_ref):
    even_x, even_y = is_even("gx"), is_even("gy")
    wet, _ = wet_rows(mask_ref)
    y_spectra(even_y, ye_in, yo_in, yh_ref)
    below, above = y_ocean(even_y, ye_in, yo_in)
    left, right = x_ocean(even_x, xe_in, xe_in)
    extend_ocean(o_ref, left, right, ext_ref, 1)
    refraction_rates(ext_ref, below, above, rate_ref)
    stress_ref[...] = stress_of(n_ref, w_ref)
    inner_waves(n_ref, yh_ref, rate_ref, wet, tab_ref, shift_ref, ys_ref, acc_ref, exact)
    side = even_x.astype(jnp.int32)
    finish_near_half(n_ref, acc_ref, rate_ref, mask_ref, tab_ref, xe_in, True, side, exact)
    finish_far_half(n_ref, acc_ref, rate_ref, mask_ref, side, exact)
    for r in range(2):
        done_ref[r] = jnp.transpose(acc_ref[2 * side + r]).astype(BF16)


def last_kernel(n_ref, acc_in, done_ref, o_ref, mask_ref, tab_ref, stress_ref, xe_in, xo_in, ye_in, yo_in,
                acc_ref, ocean_ref, out_hbm, ext_ref, rate_ref, block_ref, sems):
    even_x, even_y = is_even("gx"), is_even("gy")
    side = 1 - even_x.astype(jnp.int32)
    done = pltpu.make_async_copy(done_ref, out_hbm.at[pl.ds(2 * (1 - side), 2)], sems.at[0])
    done.start()
    below, above = y_ocean(even_y, ye_in, yo_in)
    left, right = x_ocean(even_x, xe_in, xo_in)
    extend_ocean(o_ref, left, right, ext_ref, 1)
    refraction_rates(ext_ref, below, above, rate_ref)
    finish_near_half(n_ref, acc_ref, rate_ref, mask_ref, tab_ref, xo_in, inside("gx"), side, exact)
    finish_far_half(n_ref, acc_ref, rate_ref, mask_ref, side, exact)
    copies = [done]
    for r in range(2):
        block_ref[r] = jnp.transpose(acc_ref[2 * side + r]).astype(BF16)
        copies.append(pltpu.make_async_copy(block_ref.at[r], out_hbm.at[2 * side + r], sems.at[1 + r]))
        copies[-1].start()
    _, wet8 = wet_rows(mask_ref)
    extend_ocean(o_ref, left, right, ext_ref)
    advance_ocean(ext_ref, below, above, stress_ref[...], wet8, ocean_ref)
    for copy in copies:
        copy.wait()


def swap(array, axis, odd, wrap=False):
    nx, ny = lax.axis_size("gx"), lax.axis_size("gy")
    pairs = []
    for i in range(nx):
        for j in range(ny):
            to = (i ^ 1, j) if axis == "gx" else (i, j ^ 1)
            if odd and axis == "gx":
                to = (((i + 1) ^ 1) - 1, j) if 0 < i < nx - 1 else ((nx - 1 - i, j) if wrap else (i, j ^ 1))
            if odd and axis == "gy":
                to = (i, ((j + 1) ^ 1) - 1) if 0 < j < ny - 1 else (i ^ 1, j)
            pairs.append((i * ny + j, to[0] * ny + to[1]))
    return lax.ppermute(array, ("gx", "gy"), pairs)


def call(kernel, outs, ins, scratch, params=None, any_in=(), any_out=(), aliases=None, moved=0):
    places = [HBM if i in any_in else VM for i in range(len(ins))]
    return pl.pallas_call(
        kernel,
        out_shape=[jax.ShapeDtypeStruct(shape, dtype) for shape, dtype in outs],
        in_specs=places,
        out_specs=[HBM if i in any_out else VM for i in range(len(outs))],
        scratch_shapes=scratch,
        compiler_params=params or PARAMS,
        input_output_aliases=aliases or {},
        cost_estimate=pl.CostEstimate(flops=0, bytes_accessed=moved * 1024 * 1024, transcendentals=0),
        name=kernel.__name__.removesuffix("_kernel"),
    )(*ins)


BINNED = ((ROWS, BINS, LANES), F32)
GRID = ((ROWS, NDIR, NF, LANES), F32)
XEDGE = ((XROWS, LANES), BF16)
XLONG = ((XROWS + 16, LANES), BF16)
YEDGE = ((YROWS, LANES), BF16)
DRIVE = ((16, LANES), F32)
RATES = ((NDIR, 8, LANES), F32)
YH = pltpu.VMEM((2, HALF * NF, LANES), BF16)
EXT = pltpu.VMEM((3, 8 * NZ, LANES), F32)
RATE = pltpu.VMEM(*RATES)
SHIFTED = pltpu.VMEM((ROWS, QUARTER * NF, 2 * LANES), F32)
EDGES = pltpu.VMEM((2, HALF, 8, LANES), F32)
TURNED = pltpu.VMEM((2, BINS, LANES), F32)
BLOCK = pltpu.VMEM((2, LANES, BINS), BF16)


def local(spectrum, ocean_state, sea_mask):
    ocean_shape = (ocean_state.shape, F32)
    weights = jnp.asarray(stress_table(), dtype=BF16)
    shift_table = jnp.asarray(shift_tables(), dtype=BF16)
    (xo,) = call(
        first_kernel,
        (XEDGE,),
        (spectrum, ocean_state, sea_mask),
        [
            pltpu.VMEM((2, *spectrum.shape[1:]), BF16),
            pltpu.VMEM(ocean_state.shape, F32),
            pltpu.VMEM(sea_mask.shape, jnp.int32),
            TURNED,
            pltpu.SemaphoreType.DMA((4,)),
        ],
        FIRST,
        any_in=(0, 1, 2),
        moved=32,
    )
    xo = swap(xo, "gx", 1)
    n, xe, ye, yo, edge_table = call(
        start_kernel,
        (GRID, XEDGE, YEDGE, YEDGE, ((2, ROWS * LANES, LANES), BF16)),
        (spectrum, ocean_state, sea_mask),
        [pltpu.VMEM((ROWS, BINS, LANES), F32), EDGES],
    )
    xe = swap(xe, "gx", 0)
    ye = swap(ye, "gy", 0)
    yo = swap(yo, "gy", 1)
    stress, tab = call(prepare_kernel, (DRIVE, ((5, NDIR, NF, LANES), F32)), (n, weights), [])
    (acc,) = call(
        inner_kernel,
        (GRID,),
        (n, ocean_state, sea_mask, tab, shift_table, ye, yo),
        [YH, EXT, RATE, SHIFTED],
    )
    acc, ocean, rate, xo2, xrow = call(
        send_kernel,
        (GRID, ocean_shape, RATES, XLONG, ((OCEAN, LANES), F32)),
        (n, acc, ocean_state, sea_mask, stress, xe, xo, ye, yo),
        [EXT],
        aliases={1: 0},
    )
    xo2 = swap(xo2, "gx", 1, True)
    n, xe, ye, yo = call(
        rest_kernel,
        (GRID, XEDGE, YEDGE, YEDGE),
        (n, acc, sea_mask, tab, rate, edge_table, xrow, ocean, xe, xo),
        [EDGES],
        aliases={1: 0},
    )
    xe = swap(xe, "gx", 0)
    ye = swap(ye, "gy", 0)
    yo = swap(yo, "gy", 1)
    acc, stress, done = call(
        inner_last_kernel,
        (BINNED, DRIVE, ((2, *spectrum.shape[1:]), BF16)),
        (n, ocean, sea_mask, tab, weights, shift_table, xe, ye, yo),
        [YH, EXT, RATE, SHIFTED],
    )
    _, ocean, out = call(
        last_kernel,
        (BINNED, ocean_shape, (spectrum.shape, BF16)),
        (n, acc, done, ocean, sea_mask, tab, stress, xe, xo2, ye, yo),
        [EXT, RATE, BLOCK, pltpu.SemaphoreType.DMA((3,))],
        any_out=(2,),
        aliases={1: 0},
    )
    return out, ocean


def solution(mesh):
    placed = (P("gx", "gy", None), P(None, None, "gx", "gy"), P("gx", "gy"))
    return jax.shard_map(
        local,
        mesh=mesh,
        in_specs=placed,
        out_specs=(P("gx", "gy", None), P(None, None, "gx", "gy")),
        check_vma=False,
    )
```
